32 devices in a mesh: gx: 4 (over z), gy: 8 (over y, x, core).
Axes of the slice: x: 2, y: 2, z: 4, core: 2. Of those that a mesh axis runs over, the one named last changes fastest.
Arguments:
- tokens: bfloat16 [256, 14, 20, 384], P(('gx', 'gy')), may hold values from -6 to 6
- bucket: int32 [256], P(('gx', 'gy')), may hold values from 0 to 1
- counts: int32 [32], P(('gx', 'gy')), may hold values from 4 to 8, as said below
- mod_weights: bfloat16 [591360], P(('gx', 'gy')), may hold values from -0.3125 to 0.3125
- mlp_weights: bfloat16 [1179648], P(('gx', 'gy')), may hold values from -0.3125 to 0.3125
- small_params: bfloat16 [37664], P(('gx', 'gy')), as said below
- cotangent: bfloat16 [256, 14, 20, 384], P(('gx', 'gy')), may hold values from -6 to 6
Outputs:
- out_tokens: bfloat16 [256, 14, 20, 384], P(('gx', 'gy'))
- grad_tokens: float32 [256, 14, 20, 384], P(('gx', 'gy'))
- grad_mod: float32 [591360], P(('gx', 'gy'))
- grad_mlp: float32 [1179648], P(('gx', 'gy'))
- grad_small: float32 [37664], P(('gx', 'gy'))
The draws below stay inside these ranges and needn't reach their ends.
Inputs may be any that keep to these rules, and one draw needn't show every extreme that they name: `counts`: each device's live slots; some device holds exactly 8. `small_params`: Gains, biases, depthwise kernels and layer scales in the stated layout.
All inputs are finite; a program needn't handle non-finite values.
Results may differ from the reference program's by a relative error of at most 0.0084.
Values may be sent and summed in bfloat16 or wider, within the bound.
No kernel may reach another device: no remote copies, remote signals or barrier semaphores. Data moves between devices by JAX's collectives and lax.ppermute only.
A program may use at most 448 MiB of HBM per device.

```python
import jax
import jax.numpy as jnp
from jax import lax

C = 384
HID = 1536
GH = 14
GW = 20
SLOTS = 8
RANKS = 32
IMAGES = 256
MODLEN = 591360
MLPLEN = 1179648
SMALL = 37664


def draw_counts(key, part):
    key = jax.random.fold_in(key, 5)
    lowest = max(1, SLOTS // 2)
    drawn = jax.random.randint(key, (RANKS,), lowest, SLOTS + 1)
    fullest = jax.random.randint(jax.random.fold_in(key, 1), (), 0, RANKS)
    return jnp.where(jnp.arange(RANKS) == fullest, SLOTS, drawn).astype(jnp.int32)


def draw_small_params(key, part):
    key = jax.random.fold_in(key, 11)
    noise = jax.random.normal(key, (SMALL,), jnp.float32)
    spread = jax.random.uniform(jax.random.fold_in(key, 1), (SMALL,), jnp.float32, 0.0, 1.0)
    place = jnp.arange(SMALL)

    def inside(lower, upper):
        return (place >= lower) & (place < upper)
    values = 0.1 * noise
    values = jnp.where(inside(0, C) | inside(90 * C + 4, 91 * C + 4), 1.0 + 0.15 * noise, values)
    values = jnp.where(inside(4 * C, 4 * C + 4), 0.5 * noise, values)
    values = jnp.where(inside(4 * C + 4, 13 * C + 4), noise / 3.0, values)
    values = jnp.where(inside(13 * C + 4, 38 * C + 4), noise / 5.0, values)
    values = jnp.where(inside(38 * C + 4, 87 * C + 4), noise / 7.0, values)
    values = jnp.where(inside(89 * C + 4, 90 * C + 4), 0.5 + spread, values)
    values = jnp.where(inside(93 * C + 4 + HID, 94 * C + 4 + HID), 0.3 + 0.7 * spread, values)
    return values.astype(jnp.bfloat16)


def plant(array, rng, smallest, largest):
    extent = array.shape
    spot = [jax.random.randint(jax.random.fold_in(rng, axis), (), 0, extent[axis]) for axis in range(len(extent))]
    array = array.at[tuple(spot)].set(smallest)
    longest = extent.index(max(extent))
    spot[longest] = (spot[longest] + 1) % extent[longest]
    return array.at[tuple(spot)].set(largest)


def block_scale(own_key, shape, split, smallest, largest):
    def one(axis_at, parts):
        heights = jax.random.uniform(jax.random.fold_in(jax.random.fold_in(own_key, 6), axis_at), (parts,), jnp.float32, smallest / len(split), largest / len(split))
        return jnp.repeat(jnp.exp(heights), shape[axis_at] // parts).reshape((-1,) + (1,) * (len(shape) - axis_at - 1))

    factor_of = one(*split[0])
    for cut in split[1:]:
        factor_of = factor_of * one(*cut)
    return factor_of


def normal_values(key, shape, deviation, reach, cuts=(), kind=jnp.bfloat16):
    entries = deviation * jax.random.normal(key, shape, jnp.float32)
    if cuts:
        entries = entries * block_scale(key, shape, cuts, -0.22, 0.18)
    return jnp.clip(entries, -reach, reach).astype(kind)


def setup_inputs(seed: int = 0) -> dict:
    seeds = jax.random.split(jax.random.key(seed), 8)
    tokens = normal_values(seeds[0], (IMAGES, GH, GW, C), 1.0, 6.0, ((0, 32),))
    bucket = plant(jax.random.randint(seeds[1], (IMAGES,), 0, 2), jax.random.fold_in(seeds[1], 1), 0, 1).astype(jnp.int32)
    counts = draw_counts(jax.random.fold_in(seeds[7], 71), 0)
    mod_weights = normal_values(seeds[3], (MODLEN,), C ** -0.5, 0.3125, ((0, 32),))
    mlp_weights = normal_values(seeds[4], (MLPLEN,), C ** -0.5, 0.3125, ((0, 32),))
    small_params = draw_small_params(jax.random.fold_in(seeds[7], 71), 0)
    cotangent = normal_values(seeds[6], (IMAGES, GH, GW, C), 1.0, 6.0, ((0, 32),))
    return {"tokens": tokens, "bucket": bucket, "counts": counts, "mod_weights": mod_weights, "mlp_weights": mlp_weights, "small_params": small_params, "cotangent": cotangent}


@jax.custom_vjp
def low(v):
    return lax.optimization_barrier(v.astype(jnp.bfloat16)).astype(jnp.float32)

@jax.custom_vjp
def low_back(v):
    return v

def low_keep(v):
    return (low(v), None)

def low_pass(kept, grad):
    return (grad,)

def back_keep(v):
    return (v, None)

def back_low(kept, grad):
    return (low(grad),)
low.defvjp(low_keep, low_pass)
low_back.defvjp(back_keep, back_low)
epsilon = 1e-05

def product(left, right):
    return jnp.dot(left, right, precision=lax.Precision.HIGHEST, preferred_element_type=jnp.float32)

def gelu_exact(values):
    return jax.nn.gelu(values, approximate=False)

def layer_norm(field_in, gain_vec, shift_vec):
    average = lax.optimization_barrier(jnp.mean(field_in, axis=-1, keepdims=True))
    centred = field_in - average
    variance = lax.optimization_barrier(jnp.mean(centred * centred, axis=-1, keepdims=True))
    return centred * lax.rsqrt(variance + epsilon) * gain_vec + shift_vec

def depthwise(field_in, kernel):
    kernel_width = kernel.shape[1]
    half_width = kernel_width // 2
    padded = jnp.pad(field_in, ((0, 0), (half_width, half_width), (half_width, half_width), (0, 0)))
    rows_in = field_in.shape[1]
    cols_in = field_in.shape[2]
    ctx_total = jnp.zeros_like(field_in)
    for row_shift in range(kernel_width):
        for col_shift in range(kernel_width):
            window = padded[:, row_shift:row_shift + rows_in, col_shift:col_shift + cols_in, :]
            ctx_total = ctx_total + window * kernel[:, row_shift, col_shift][:, None, None, :]
    return ctx_total

def oriented(kernel, bucket):
    turned = jnp.swapaxes(kernel, 0, 1)
    turned_mask = (bucket == 1)[:, None, None, None]
    return jnp.where(turned_mask, turned[None], kernel[None])

def focal(context, gates, bucket, kernels):
    level_ctx = context
    ctx_total = jnp.zeros_like(context)
    for level_index in range(3):
        level_ctx = gelu_exact(depthwise(level_ctx, oriented(kernels[level_index], bucket)))
        ctx_total = ctx_total + level_ctx * gates[..., level_index:level_index + 1]
    summary = gelu_exact(lax.optimization_barrier(jnp.mean(level_ctx, axis=(1, 2), keepdims=True)))
    return ctx_total + summary * gates[..., 3:4]

def unpack_small(small_vec):
    lengths = [C, C, 2 * C + 4, 9 * C, 25 * C, 49 * C, C, C, C, C, C, HID, C, C]
    pieces = []
    offset = 0
    for length in lengths:
        pieces.append(small_vec[offset:offset + length])
        offset = offset + length
    kernels = (pieces[3].reshape(3, 3, C), pieces[4].reshape(5, 5, C), pieces[5].reshape(7, 7, C))
    return (pieces[0], pieces[1], pieces[2], kernels, pieces[6], pieces[7], pieces[8], pieces[9], pieces[10], pieces[11], pieces[12], pieces[13])

def split_mod(flat_vec):
    boundary = C * (2 * C + 4)
    return (flat_vec[:boundary].reshape(C, 2 * C + 4), flat_vec[boundary:boundary + C * C].reshape(C, C), flat_vec[boundary + C * C:].reshape(C, C))

def split_mlp(flat_vec):
    return (flat_vec[:C * HID].reshape(C, HID), flat_vec[C * HID:].reshape(HID, C))

def block(field_in, bucket, live_mask, mod_vec, mlp_vec, small_vec):
    gain_one, shift_one, merged_bias, kernels, mod_bias, proj_bias, scale_one, gain_two, shift_two, up_bias, down_bias, scale_two = unpack_small(small_vec)
    w_merged, w_modul, w_proj = split_mod(mod_vec)
    w_up, w_down = split_mlp(mlp_vec)
    grid_shape = field_in.shape
    flat_in = field_in.reshape(-1, C)
    normed = low(layer_norm(flat_in, gain_one, shift_one))
    merged_out = low_back(product(normed, w_merged) + merged_bias)
    query_part = merged_out[:, :C]
    context = merged_out[:, C:2 * C].reshape(grid_shape)
    gates = merged_out[:, 2 * C:].reshape(grid_shape[:3] + (4,))
    mixed_ctx = low(focal(context, gates, bucket, kernels).reshape(-1, C))
    modulator = low_back(product(mixed_ctx, w_modul) + mod_bias)
    modulated = low(query_part * modulator)
    branch = low_back(product(modulated, w_proj) + proj_bias)
    middle = flat_in + scale_one * branch
    second = low(layer_norm(middle, gain_two, shift_two))
    expanded = low_back(product(second, w_up) + up_bias)
    activated = low(gelu_exact(expanded))
    shrunk = low_back(product(activated, w_down) + down_bias)
    result = (middle + scale_two * shrunk).reshape(grid_shape)
    return result * live_mask[:, None, None, None]

def reference(tokens, bucket, counts, mod_weights, mlp_weights, small_params, cotangent):
    mod32 = mod_weights.astype(jnp.float32)
    mlp32 = mlp_weights.astype(jnp.float32)
    small32 = small_params.astype(jnp.float32)
    slot_index = jnp.arange(IMAGES, dtype=jnp.int32)
    owner = (slot_index // SLOTS).astype(jnp.int32)
    live_mask = (slot_index % SLOTS < counts[owner]).astype(jnp.float32)
    grid_tail = tokens.shape[1:]
    grouped = (tokens.reshape((RANKS, SLOTS) + grid_tail), bucket.reshape(RANKS, SLOTS), live_mask.reshape(RANKS, SLOTS), cotangent.reshape((RANKS, SLOTS) + grid_tail))

    def scan_step(totals, inputs):
        tok_group, bucket_group, mask_group, cot_group = inputs

        def forward(mod_vec, mlp_vec, small_vec, field_in):
            return block(field_in, bucket_group, mask_group, mod_vec, mlp_vec, small_vec)
        result, pullback = jax.vjp(forward, mod32, mlp32, small32, tok_group.astype(jnp.float32))
        grad_modw, grad_mlpw, grad_smallw, grad_field = pullback(cot_group.astype(jnp.float32))
        updated = (totals[0] + grad_modw, totals[1] + grad_mlpw, totals[2] + grad_smallw)
        return (updated, (result.astype(jnp.bfloat16), grad_field))
    initial = (jnp.zeros_like(mod32), jnp.zeros_like(mlp32), jnp.zeros_like(small32))
    totals, (outputs, field_grads) = lax.scan(scan_step, initial, grouped)
    return (outputs.reshape(tokens.shape), field_grads.reshape(tokens.shape), totals[0], totals[1], totals[2])
```

```python
import functools

import jax
import jax.numpy as jnp
import numpy as np
from jax import lax
from jax.experimental import pallas as pl
from jax.experimental.pallas import tpu as pltpu
from jax.sharding import PartitionSpec as P

C = 384
HID = 1536
GH = 14
GW = 20
HALF = 144
IMG = 2 * HALF
PAIR = 2 * IMG
C2 = 2 * C
NY = 17
NX = 23
NV = 12
NU = 8
Q = NU * NV
AR = 2 * (Q + 16)
BR = 2 * Q
SR = 4 * Q + 32
LEVELS = (3, 5, 7)
TAPS = 64
GATES = 128
MERGED = C2 + GATES
BROWS = 768
HCHUNK = 512
AXES = ("gx", "gy")
f32 = jnp.float32
bf16 = jnp.bfloat16
EPS = 1e-05
ROOT_HALF = 0.7071067811865476
INV_ROOT_2PI = 0.3989422804014327


def _hi(a):
    return a.astype(bf16)


def _lo(a):
    return (a - a.astype(bf16).astype(np.float64)).astype(bf16)


@functools.lru_cache(maxsize=None)
def constants():
    row = np.arange(HALF)
    real = (row < 7 * GW).astype(np.float64)
    yy = np.minimum(row // GW, 6) - (GH - 1) / 2
    xx = row % GW - (GW - 1) / 2
    uv = [(u, v) for u in range(1, NU + 1) for v in range(NV)]
    u0 = [(0, v) for v in range(NV)]
    wu = 2 * np.pi / NY
    wv = 2 * np.pi / NX

    def trig(pairs, pad):
        u = np.array([p[0] for p in pairs] + [0] * pad, np.float64)[:, None]
        v = np.array([p[1] for p in pairs] + [0] * pad, np.float64)[:, None]
        use = np.array([1.0] * len(pairs) + [0.0] * pad)[:, None] * real[None]
        cy, sy = np.cos(wu * u * yy) * use, np.sin(wu * u * yy) * use
        cx, sx = np.cos(wv * v * xx), np.sin(wv * v * xx)
        weight = np.where(u > 0, 2.0, 1.0) * np.where(v > 0, 2.0, 1.0) / (NY * NX)
        return cy * cx, -cy * sx, sy * cx, -sy * sx, weight

    e_re, e_im, o_re, o_im, w1 = trig(uv, 0)
    z_re, z_im, _, _, w0 = trig(u0, 16 - NV)
    fe = np.concatenate([e_re, z_re, e_im, z_im], 0)
    fo = np.concatenate([o_re, o_im], 0)
    half = np.concatenate([0.5 * w1, w0, 0.5 * w1, w0], 0)
    ge = (fe * half).T
    go = (fo * np.concatenate([0.5 * w1, 0.5 * w1], 0)).T

    es, adj = [], []
    for k in LEVELS:
        h = k // 2
        ty, tx = np.meshgrid(np.arange(k) - h, np.arange(k) - h, indexing="ij")
        u = np.array([p[0] for p in uv], np.float64)[:, None]
        v = np.array([p[1] for p in uv], np.float64)[:, None]
        v0 = np.array(list(range(NV)) + [0] * (16 - NV), np.float64)[:, None]
        use0 = np.array([1.0] * NV + [0.0] * (16 - NV))[:, None]
        for bucket in (0, 1):
            sy, sx = (ty, tx) if bucket == 0 else (tx, ty)
            py = sy.reshape(1, -1) * wu
            px = sx.reshape(1, -1) * wv
            plus = u * py + v * px
            minus = -u * py + v * px
            zero = v0 * px
            e = np.concatenate(
                [np.cos(plus), np.sin(plus), np.cos(minus), np.sin(minus), np.cos(zero) * use0, np.sin(zero) * use0], 0
            )
            wp = np.where(v > 0, 2.0, 1.0) / (NY * NX)
            wz = np.where(v0 > 0, 2.0, 1.0) * use0 / (NY * NX)
            a = np.concatenate(
                [
                    np.cos(plus) * wp,
                    -np.sin(plus) * wp,
                    np.cos(minus) * wp,
                    -np.sin(minus) * wp,
                    np.cos(zero) * wz,
                    -np.sin(zero) * wz,
                ],
                0,
            ).T
            full = np.zeros((SR, TAPS))
            full[:, : k * k] = e
            es.append(np.concatenate([_hi(full), _lo(full)], 1))
            back = np.zeros((TAPS, SR))
            back[: k * k] = a
            adj.append(np.concatenate([_hi(back), _hi(back), _lo(back)], 1))
    return dict(
        fe=np.concatenate([_hi(fe), _lo(fe), _hi(fe)], 1),
        fo=np.concatenate([_hi(fo), _lo(fo), _hi(fo)], 1),
        ge=np.concatenate([_hi(ge), _lo(ge), _hi(ge)], 1),
        go=np.concatenate([_hi(go), _lo(go), _hi(go)], 1),
        es=np.stack(es),
        adj=np.stack(adj),
    )


def dot(a, b):
    return jnp.dot(a, b, preferred_element_type=f32)


def dot_nt(a, b):
    return lax.dot_general(a, b, (((1,), (1,)), ((), ())), preferred_element_type=f32)


def dot_tn(a, b):
    return lax.dot_general(a, b, (((0,), (0,)), ((), ())), preferred_element_type=f32)


def gelu_pair(x):
    cdf = 0.5 * lax.erf(x * ROOT_HALF) + 0.5
    return x * cdf, cdf + x * (jnp.exp(x * x * -0.5) * INV_ROOT_2PI)


def split(x):
    hi = x.astype(bf16)
    return hi, (x - hi.astype(f32)).astype(bf16)


def rows16(i, n=16):
    return pl.ds(pl.multiple_of(i * n, n), n)


def at(base, i, n=16):
    return pl.ds(pl.multiple_of(base + i * n, n), n)


def loop(n, body, init=None, unroll=1):
    if init is None:

        def plain(i, c):
            body(i)
            return c

        lax.fori_loop(0, n, plain, 0, unroll=unroll)
        return None
    return lax.fori_loop(0, n, body, init, unroll=unroll)


def norm_stats(x):
    mean = jnp.mean(x, axis=-1, keepdims=True)
    centred = x - mean
    var = jnp.mean(centred * centred, axis=-1, keepdims=True)
    r = lax.rsqrt(var + EPS)
    return centred * r, r


def sum8(x):
    n = x.shape[0] // 8
    total = x[0:8]
    for k in range(1, n):
        total = total + x[8 * k : 8 * k + 8]
    return total


def grid_rows(im, y):
    return im * IMG + (y * GW if y < 7 else HALF + (GH - 1 - y) * GW)


def lanes(im):
    return slice(im * C, im * C + C)


(V_G1, V_B1, V_BQ, V_BC, V_HB, V_PB, V_S1, V_G2, V_B2, V_BM2, V_S2, V_BG) = range(12)
VROWS = 16


def kernel_a(
    bucket, counts, x_ref, cot_ref, wf, wh, wp, vec, kcat, es, fe, fo, ge, go,
    xrow_o, up_o, normed_o, q_o, gates_o, mod_o, mixed_o, modulated_o, branch_o, z_o, g_o, spec_o, mean_o, h_o,
    xr, ctx, ecat, ocat, s_a, s_b, s_e, s_o, yca, ycb, mix,
):
    step = pl.program_id(0)

    @pl.when(step == 0)
    def _():
        xr[...] = jnp.zeros_like(xr)
        for lb in range(6):
            h_o[lb] = dot(es[lb], kcat[lb // 2])

    for im in range(2):
        live = (step * 2 + im < counts[0]).astype(f32)
        for y in range(GH):
            at_row = grid_rows(im, y)
            xr[at_row : at_row + GW, :] = cot_ref[im, y].astype(f32) * live

    def move_up(i):
        s = rows16(i, 32)
        up_o[s, :] = xr[s, :].astype(bf16)

    loop(PAIR // 32, move_up)
    for im in range(2):
        for y in range(GH):
            at_row = grid_rows(im, y)
            xr[at_row : at_row + GW, :] = x_ref[im, y].astype(f32)

    g1, b1 = vec[V_G1 : V_G1 + 1, :], vec[V_B1 : V_B1 + 1, :]

    def norm(i):
        s = rows16(i, 32)
        x = xr[s, :]
        xrow_o[s, :] = x.astype(bf16)
        n, _ = norm_stats(x)
        normed_o[s, :] = (n * g1 + b1).astype(bf16)

    loop(PAIR // 32, norm)
    q_o[...] = dot(normed_o[...], wf[:, :C]) + vec[V_BQ : V_BQ + 1, :]
    ctx[...] = dot(normed_o[...], wf[:, C:C2]) + vec[V_BC : V_BC + 1, :]
    gates_o[...] = dot(normed_o[...], wf[:, C2:]) + vec[V_BG : V_BG + 1, :GATES]

    def put_pair(im, i, top, bot):
        e_hi, e_lo = split(top + bot)
        o_hi, o_lo = split(top - bot)
        for base, ev, ov in ((0, e_hi, o_hi), (HALF, e_hi, o_hi), (2 * HALF, e_lo, o_lo)):
            ecat[at(base, i), lanes(im)] = ev
            ocat[at(base, i), lanes(im)] = ov

    for im in range(2):

        def first(i, im=im):
            put_pair(im, i, ctx[at(im * IMG, i), :], ctx[at(im * IMG + HALF, i), :])

        loop(HALF // 16, first)

    for level in range(3):
        s_a[...] = dot(fe[...], ecat[...])
        s_b[...] = dot(fo[...], ocat[...])
        base = level * SR
        for im in range(2):
            b = bucket[step * 2 + im]
            lb = level * 2 + b
            for lt in range(3):
                ls = slice(im * C + lt * 128, im * C + lt * 128 + 128)
                hs = slice(lt * 128, lt * 128 + 128)

                def filt(i, ls=ls, hs=hs, lb=lb, base=base):
                    a_re, a_im = s_a[at(0, i), ls], s_a[at(Q + 16, i), ls]
                    b_re, b_im = s_b[at(0, i), ls], s_b[at(Q, i), ls]
                    xp_re, xp_im = a_re + b_im, a_im - b_re
                    xm_re, xm_im = a_re - b_im, a_im + b_re
                    spec_o[at(base, i), ls] = xp_re
                    spec_o[at(base + Q, i), ls] = xp_im
                    spec_o[at(base + 2 * Q, i), ls] = xm_re
                    spec_o[at(base + 3 * Q, i), ls] = xm_im
                    p_re, p_im = h_o[lb, at(0, i), hs], h_o[lb, at(Q, i), hs]
                    q_re, q_im = h_o[lb, at(2 * Q, i), hs], h_o[lb, at(3 * Q, i), hs]
                    yp_re, yp_im = p_re * xp_re - p_im * xp_im, p_re * xp_im + p_im * xp_re
                    ym_re, ym_im = q_re * xm_re - q_im * xm_im, q_re * xm_im + q_im * xm_re
                    for dst, off, width, val in (
                        (yca, 0, AR, yp_re + ym_re),
                        (yca, Q + 16, AR, yp_im + ym_im),
                        (ycb, 0, BR, ym_im - yp_im),
                        (ycb, Q, BR, yp_re - ym_re),
                    ):
                        hi, lo = split(val)
                        dst[at(off, i), ls] = hi
                        dst[at(off + width, i), ls] = hi
                        dst[at(off + 2 * width, i), ls] = lo

                loop(Q // 16, filt)
            ls = lanes(im)
            x_re, x_im = s_a[Q : Q + 16, ls], s_a[2 * Q + 16 : 2 * Q + 32, ls]
            spec_o[base + 4 * Q : base + 4 * Q + 16, ls] = x_re
            spec_o[base + 4 * Q + 16 : base + 4 * Q + 32, ls] = x_im
            p_re, p_im = h_o[lb, 4 * Q : 4 * Q + 16, :], h_o[lb, 4 * Q + 16 : 4 * Q + 32, :]
            for off, val in ((Q, p_re * x_re - p_im * x_im), (2 * Q + 16, p_re * x_im + p_im * x_re)):
                hi, lo = split(val)
                yca[off : off + 16, ls] = hi
                yca[off + AR : off + AR + 16, ls] = hi
                yca[off + 2 * AR : off + 2 * AR + 16, ls] = lo
        s_e[...] = dot(ge[...], yca[...])
        s_o[...] = dot(go[...], ycb[...])
        for im in range(2):

            def act(i, total, im=im, level=level):
                ls = lanes(im)
                even, odd = s_e[at(0, i), ls], s_o[at(0, i), ls]
                both = []
                for h, a in ((0, even + odd), (HALF, even - odd)):
                    z, g = gelu_pair(a)
                    z_o[at(level * IMG + h, i), ls] = z.astype(bf16)
                    g_o[at(level * IMG + h, i), ls] = g
                    s = at(im * IMG + h, i)
                    part = z * gates_o[s, level : level + 1]
                    mix[s, :] = part if level == 0 else mix[s, :] + part
                    both.append(z)
                if level < 2:
                    put_pair(im, i, both[0], both[1])
                    return total
                return total + sum8(both[0]) + sum8(both[1])

            total = loop(HALF // 16, act, jnp.zeros((8, C), f32))
            if level == 2:
                mean = jnp.sum(total, axis=0, keepdims=True) * (1.0 / (GH * GW))
                mean_o[:, lanes(im)] = jnp.broadcast_to(mean, (8, C))

    for im in range(2):
        glob, _ = gelu_pair(mean_o[0:1, lanes(im)])

        def finish(i, im=im, glob=glob):
            s = at(im * IMG, i, 32)
            mixed_o[s, :] = (mix[s, :] + gates_o[s, 3:4] * glob).astype(bf16)

        loop(IMG // 32, finish)
    mod_o[...] = dot(mixed_o[...], wh[...]) + vec[V_HB : V_HB + 1, :]

    def modulate(i):
        s = rows16(i, 32)
        modulated_o[s, :] = (q_o[s, :] * mod_o[s, :]).astype(bf16)

    loop(PAIR // 32, modulate)
    branch_o[...] = dot(modulated_o[...], wp[...]) + vec[V_PB : V_PB + 1, :]


(S_S1, S_G2, S_B2, S_BM2, S_S2) = range(5)


def kernel_b(
    x_ref, branch, up, w1, w2, vec, bm1,
    dmid_o, out_o, gw1, gw2, sums, bsum,
    mid, second, dshr, shr, dsec, act, dexp, hid, vacc, bacc,
):
    step = pl.program_id(0)

    @pl.when(step == 0)
    def _():
        gw1[...] = jnp.zeros_like(gw1)
        gw2[...] = jnp.zeros_like(gw2)
        vacc[...] = jnp.zeros_like(vacc)
        bacc[...] = jnp.zeros_like(bacc)

    g2, b2 = vec[V_G2 : V_G2 + 1, :], vec[V_B2 : V_B2 + 1, :]
    s1, s2 = vec[V_S1 : V_S1 + 1, :], vec[V_S2 : V_S2 + 1, :]

    def norm(i):
        s = rows16(i, 32)
        middle = x_ref[s, :].astype(f32) + s1 * branch[s, :]
        mid[s, :] = middle
        n, _ = norm_stats(middle)
        second[s, :] = (n * g2 + b2).astype(bf16)
        dshr[s, :] = (up[s, :].astype(f32) * s2).astype(bf16)

    loop(BROWS // 32, norm)
    for h in range(HID // HCHUNK):
        hs = slice(h * HCHUNK, (h + 1) * HCHUNK)
        hid[...] = dot(second[...], w1[:, hs]) + bm1[0:1, hs]
        dact = dot_nt(dshr[...], w2[hs, :])
        dsec_h = dact
        shr_h = hid
        del dsec_h, shr_h
        act_g = dact

        def gelu(i, hs=hs):
            s = rows16(i, 16)
            z, g = gelu_pair(hid[s, :])
            act[s, :] = z.astype(bf16)
            hid[s, :] = g

        loop(BROWS // 16, gelu)
        d = act_g * hid[...]
        dexp[...] = d.astype(bf16)
        bacc[:, hs] += jnp.sum(d.reshape(BROWS // 8, 8, HCHUNK), axis=0)
        part = dot(act[...], w2[hs, :])
        back = dot_nt(dexp[...], w1[:, hs])
        if h == 0:
            shr[...] = part
            dsec[...] = back
        else:
            shr[...] += part
            dsec[...] += back
        gw1[:, hs] += dot_tn(second[...], dexp[...])
        gw2[hs, :] += dot_tn(act[...], dshr[...])

    bm2 = vec[V_BM2 : V_BM2 + 1, :]

    def finish(i, c):
        t_s1, t_g2, t_b2, t_bm2, t_s2 = c
        s = rows16(i, 32)
        middle = mid[s, :]
        u = up[s, :].astype(f32)
        shrunk = shr[s, :] + bm2
        out_o[s, :] = middle + s2 * shrunk
        n, r = norm_stats(middle)
        d = dsec[s, :]
        e = d * g2
        dn = d * n
        dv = r * (e - jnp.mean(e, axis=-1, keepdims=True) - n * jnp.mean(e * n, axis=-1, keepdims=True))
        dm = u + dv
        dmid_o[s, :] = dm
        return (
            t_s1 + sum8(dm * branch[s, :]),
            t_g2 + sum8(dn),
            t_b2 + sum8(d),
            t_bm2 + sum8(dshr[s, :].astype(f32)),
            t_s2 + sum8(u * shrunk),
        )

    zero = jnp.zeros((8, C), f32)
    totals = loop(BROWS // 32, finish, (zero,) * 5)
    for k, t in enumerate(totals):
        vacc[k] += t

    @pl.when(step == pl.num_programs(0) - 1)
    def _():
        sums[...] = jnp.zeros_like(sums)
        for k in range(5):
            sums[k : k + 1, :] = jnp.sum(vacc[k], axis=0, keepdims=True)
        bsum[...] = jnp.broadcast_to(jnp.sum(bacc[...], axis=0, keepdims=True), bsum.shape)


(T_PB, T_HB, T_G1, T_B1) = range(4)


def kernel_c(
    bucket, counts, dmid, out_rows, x_ref, normed, q_ref, gates, mod, mixed, modulated, z_ref, g_ref, spec, mean_ref, h_ref,
    wf, wh, wp, vec, adj, fe, fo, ge, go,
    gtok_o, out_o, gwf, gwh, gwp, sums, fsum, dk,
    stage, dmix, dmer, d1, d2, ecat, ocat, s_a, s_b, s_e, s_o, yca, ycb, acc, cat, vacc, facc,
):
    step = pl.program_id(0)
    last = pl.num_programs(0) - 1

    @pl.when(step == 0)
    def _():
        for ref in (gwf, gwh, gwp, vacc, facc, acc):
            ref[...] = jnp.zeros_like(ref)

    s1, g1 = vec[V_S1 : V_S1 + 1, :], vec[V_G1 : V_G1 + 1, :]
    zero = jnp.zeros((8, C), f32)

    def scale(i, t):
        s = rows16(i, 32)
        d = s1 * dmid[s, :]
        d1[s, :] = d.astype(bf16)
        return t + sum8(d)

    vacc[T_PB] += loop(PAIR // 32, scale, zero)
    gwp[...] += dot_tn(modulated[...], d1[...])
    dmix[...] = dot_nt(d1[...], wp[...])

    def demod(i, c):
        t_q, t_hb = c
        s = rows16(i, 32)
        dm = dmix[s, :]
        dq = dm * mod[s, :]
        dd = dm * q_ref[s, :]
        dmer[s, :C] = dq.astype(bf16)
        d2[s, :] = dd.astype(bf16)
        return t_q + sum8(dq), t_hb + sum8(dd)

    t_q, t_hb = loop(PAIR // 32, demod, (zero, zero))
    facc[:, :C] += t_q
    vacc[T_HB] += t_hb
    gwh[...] += dot_tn(mixed[...], d2[...])
    dmix[...] = dot_nt(d2[...], wh[...])

    lane = lax.broadcasted_iota(jnp.int32, (16, GATES), 1)
    dmeans = []
    for im in range(2):
        ls = lanes(im)
        glob, dglob = gelu_pair(mean_ref[0:1, ls])

        def gate_grad(i, c, im=im, ls=ls, glob=glob):
            t_glob, t_g = c
            for h in (0, HALF):
                s = at(im * IMG + h, i)
                dm = dmix[s, :]
                dg = jnp.zeros((16, GATES), f32)
                for k in range(4):
                    other = z_ref[at(k * IMG + h, i), ls].astype(f32) if k < 3 else glob
                    col = jnp.sum(dm * other, axis=-1, keepdims=True)
                    dg = jnp.where(lane == k, col, dg)
                dmer[s, C2:] = dg.astype(bf16)
                t_g = t_g + sum8(dg)
                t_glob = t_glob + sum8(dm * gates[s, 3:4])
            return t_glob, t_g

        t_glob, t_g = loop(HALF // 16, gate_grad, (zero, jnp.zeros((8, GATES), f32)))
        facc[:, C2:] += t_g
        dmeans.append(jnp.sum(t_glob, axis=0, keepdims=True) * dglob * (1.0 / (GH * GW)))

    for level in (2, 1, 0):
        for im in range(2):
            ls = lanes(im)

            def before(i, im=im, ls=ls, level=level, dmean=dmeans[im]):
                parts = []
                if level < 2:
                    even, odd = s_e[at(0, i), ls], s_o[at(0, i), ls]
                    through = (even + odd, even - odd)
                else:
                    through = (dmean, dmean)
                for k, h in enumerate((0, HALF)):
                    s = at(im * IMG + h, i)
                    dz = gates[s, level : level + 1] * dmix[s, :] + through[k]
                    parts.append(dz * g_ref[at(level * IMG + h, i), ls])
                ecat[at(0, i), ls] = (parts[0] + parts[1]).astype(bf16)
                ocat[at(0, i), ls] = (parts[0] - parts[1]).astype(bf16)

            loop(HALF // 16, before)
        s_a[...] = dot(fe[...], ecat[...])
        s_b[...] = dot(fo[...], ocat[...])
        base = level * SR
        for im in range(2):
            b = bucket[step * 2 + im]
            lb = level * 2 + b
            for lt in range(3):
                ls = slice(im * C + lt * 128, im * C + lt * 128 + 128)
                hs = slice(lt * 128, lt * 128 + 128)

                def filt(i, ls=ls, hs=hs, lb=lb, base=base):
                    a_re, a_im = s_a[at(0, i), ls], s_a[at(Q + 16, i), ls]
                    b_re, b_im = s_b[at(0, i), ls], s_b[at(Q, i), ls]
                    dp_re, dp_im = a_re + b_im, a_im - b_re
                    dm_re, dm_im = a_re - b_im, a_im + b_re
                    xp_re, xp_im = spec[at(base, i), ls], spec[at(base + Q, i), ls]
                    xm_re, xm_im = spec[at(base + 2 * Q, i), ls], spec[at(base + 3 * Q, i), ls]
                    acc[lb, at(0, i), hs] += xp_re * dp_re + xp_im * dp_im
                    acc[lb, at(Q, i), hs] += xp_im * dp_re - xp_re * dp_im
                    acc[lb, at(2 * Q, i), hs] += xm_re * dm_re + xm_im * dm_im
                    acc[lb, at(3 * Q, i), hs] += xm_im * dm_re - xm_re * dm_im
                    p_re, p_im = h_ref[lb, at(0, i), hs], h_ref[lb, at(Q, i), hs]
                    q_re, q_im = h_ref[lb, at(2 * Q, i), hs], h_ref[lb, at(3 * Q, i), hs]
                    yp_re, yp_im = p_re * dp_re + p_im * dp_im, p_re * dp_im - p_im * dp_re
                    ym_re, ym_im = q_re * dm_re + q_im * dm_im, q_re * dm_im - q_im * dm_re
                    yca[at(0, i), ls] = (yp_re + ym_re).astype(bf16)
                    yca[at(Q + 16, i), ls] = (yp_im + ym_im).astype(bf16)
                    ycb[at(0, i), ls] = (ym_im - yp_im).astype(bf16)
                    ycb[at(Q, i), ls] = (yp_re - ym_re).astype(bf16)

                loop(Q // 16, filt)
            ls = lanes(im)
            d_re, d_im = s_a[Q : Q + 16, ls], s_a[2 * Q + 16 : 2 * Q + 32, ls]
            x_re = spec[base + 4 * Q : base + 4 * Q + 16, ls]
            x_im = spec[base + 4 * Q + 16 : base + 4 * Q + 32, ls]
            acc[lb, 4 * Q : 4 * Q + 16, :] += x_re * d_re + x_im * d_im
            acc[lb, 4 * Q + 16 : 4 * Q + 32, :] += x_im * d_re - x_re * d_im
            p_re, p_im = h_ref[lb, 4 * Q : 4 * Q + 16, :], h_ref[lb, 4 * Q + 16 : 4 * Q + 32, :]
            yca[Q : Q + 16, ls] = (p_re * d_re + p_im * d_im).astype(bf16)
            yca[2 * Q + 16 : 2 * Q + 32, ls] = (p_re * d_im - p_im * d_re).astype(bf16)
        s_e[...] = dot(ge[...], yca[...])
        s_o[...] = dot(go[...], ycb[...])

    for im in range(2):
        ls = lanes(im)

        def context(i, t, im=im, ls=ls):
            even, odd = s_e[at(0, i), ls], s_o[at(0, i), ls]
            top, bot = even + odd, even - odd
            dmer[at(im * IMG, i), C:C2] = top.astype(bf16)
            dmer[at(im * IMG + HALF, i), C:C2] = bot.astype(bf16)
            return t + sum8(top) + sum8(bot)

        facc[:, C:C2] += loop(HALF // 16, context, zero)

    gwf[...] += dot_tn(normed[...], dmer[...])
    dmix[...] = dot_nt(dmer[...], wf[...])

    def norm_back(i, c):
        t_g, t_b = c
        s = rows16(i, 32)
        n, r = norm_stats(x_ref[s, :].astype(f32))
        d = dmix[s, :]
        e = d * g1
        dv = r * (e - jnp.mean(e, axis=-1, keepdims=True) - n * jnp.mean(e * n, axis=-1, keepdims=True))
        stage[s, :] = dmid[s, :] + dv
        return t_g + sum8(d * n), t_b + sum8(d)

    t_g, t_b = loop(PAIR // 32, norm_back, (zero, zero))
    vacc[T_G1] += t_g
    vacc[T_B1] += t_b
    for im in range(2):
        live = (step * 2 + im < counts[0]).astype(f32)
        for y in range(GH):
            at_row = grid_rows(im, y)
            gtok_o[im, y] = stage[at_row : at_row + GW, :]
            out_o[im, y] = (out_rows[at_row : at_row + GW, :] * live).astype(bf16)

    @pl.when(step == last)
    def _():
        sums[...] = jnp.zeros_like(sums)
        for k in range(4):
            sums[k : k + 1, :] = jnp.sum(vacc[k], axis=0, keepdims=True)
        fsum[...] = jnp.broadcast_to(jnp.sum(facc[...], axis=0, keepdims=True), fsum.shape)
        for level in range(3):
            total = None
            for b in range(2):
                lb = level * 2 + b

                def parts(i, lb=lb):
                    hi, lo = split(acc[lb, at(0, i), :])
                    cat[at(0, i), :] = hi
                    cat[at(SR, i), :] = lo
                    cat[at(2 * SR, i), :] = hi

                loop(SR // 16, parts)
                term = dot(adj[lb], cat[...])
                total = term if total is None else total + term
            dk[level] = total


def full(shape):
    return pl.BlockSpec(shape, lambda i, n=len(shape): (0,) * n)


def rows(n, width):
    return pl.BlockSpec((n, width), lambda i: (i, 0))


def smem():
    return pl.BlockSpec(memory_space=pltpu.SMEM)


def image_block():
    return pl.BlockSpec((2, GH, GW, C), lambda i: (i, 0, 0, 0))


def sds(shape, dtype):
    return jax.ShapeDtypeStruct(shape, dtype)


def params(mib):
    return pltpu.CompilerParams(vmem_limit_bytes=mib * 2**20, dimension_semantics=("arbitrary",))


def compute(tokens, bucket, counts, wf, wh, wp, w1, w2, vec, bm1, kcat, cotangent):
    con = constants()
    slots = tokens.shape[0]
    pairs = slots // 2
    n = pairs * PAIR
    fwd = [jnp.asarray(con[k]) for k in ("fe", "fo", "ge", "go")]
    a_out = [
        (sds((n, C), bf16), rows(PAIR, C)),
        (sds((n, C), bf16), rows(PAIR, C)),
        (sds((n, C), bf16), rows(PAIR, C)),
        (sds((n, C), f32), rows(PAIR, C)),
        (sds((n, GATES), f32), rows(PAIR, GATES)),
        (sds((n, C), f32), rows(PAIR, C)),
        (sds((n, C), bf16), rows(PAIR, C)),
        (sds((n, C), bf16), rows(PAIR, C)),
        (sds((n, C), f32), rows(PAIR, C)),
        (sds((pairs * 3 * IMG, C2), bf16), rows(3 * IMG, C2)),
        (sds((pairs * 3 * IMG, C2), f32), rows(3 * IMG, C2)),
        (sds((pairs * 3 * SR, C2), f32), rows(3 * SR, C2)),
        (sds((pairs * 8, C2), f32), rows(8, C2)),
        (sds((6, SR, C), f32), full((6, SR, C))),
    ]
    xrow, up, normed, q, gates, mod, mixed, modulated, branch, z, g, spec, mean, h = pl.pallas_call(
        kernel_a,
        grid=(pairs,),
        out_shape=[o[0] for o in a_out],
        out_specs=[o[1] for o in a_out],
        in_specs=[smem(), smem(), image_block(), image_block()]
        + [full(w.shape) for w in (wf, wh, wp, vec, kcat, con["es"], *fwd)],
        scratch_shapes=[
            pltpu.VMEM((PAIR, C), f32),
            pltpu.VMEM((PAIR, C), f32),
            pltpu.VMEM((3 * HALF, C2), bf16),
            pltpu.VMEM((3 * HALF, C2), bf16),
            pltpu.VMEM((AR, C2), f32),
            pltpu.VMEM((BR, C2), f32),
            pltpu.VMEM((HALF, C2), f32),
            pltpu.VMEM((HALF, C2), f32),
            pltpu.VMEM((3 * AR, C2), bf16),
            pltpu.VMEM((3 * BR, C2), bf16),
            pltpu.VMEM((PAIR, C), f32),
        ],
        compiler_params=params(60),
        name="focal_forward",
    )(bucket, counts, tokens, cotangent, wf, wh, wp, vec, kcat, jnp.asarray(con["es"]), *fwd)

    b_out = [
        (sds((n, C), f32), rows(BROWS, C)),
        (sds((n, C), f32), rows(BROWS, C)),
        (sds((C, HID), f32), full((C, HID))),
        (sds((HID, C), f32), full((HID, C))),
        (sds((8, C), f32), full((8, C))),
        (sds((8, HID), f32), full((8, HID))),
    ]
    dmid, out_rows, gw1, gw2, sums_b, bsum = pl.pallas_call(
        kernel_b,
        grid=(n // BROWS,),
        out_shape=[o[0] for o in b_out],
        out_specs=[o[1] for o in b_out],
        in_specs=[rows(BROWS, C)] * 3 + [full(w.shape) for w in (w1, w2, vec, bm1)],
        scratch_shapes=[
            pltpu.VMEM((BROWS, C), f32),
            pltpu.VMEM((BROWS, C), bf16),
            pltpu.VMEM((BROWS, C), bf16),
            pltpu.VMEM((BROWS, C), f32),
            pltpu.VMEM((BROWS, C), f32),
            pltpu.VMEM((BROWS, HCHUNK), bf16),
            pltpu.VMEM((BROWS, HCHUNK), bf16),
            pltpu.VMEM((BROWS, HCHUNK), f32),
            pltpu.VMEM((5, 8, C), f32),
            pltpu.VMEM((8, HID), f32),
        ],
        compiler_params=params(60),
        name="mlp",
    )(xrow, branch, up, w1, w2, vec, bm1)

    bwd = [jnp.asarray(con["fe"][:, :HALF]), jnp.asarray(con["fo"][:, :HALF])]
    bwd += [jnp.asarray(con["ge"][:, :AR]), jnp.asarray(con["go"][:, :BR])]
    c_out = [
        (sds(tokens.shape, f32), image_block()),
        (sds(tokens.shape, bf16), image_block()),
        (sds((C, MERGED), f32), full((C, MERGED))),
        (sds((C, C), f32), full((C, C))),
        (sds((C, C), f32), full((C, C))),
        (sds((8, C), f32), full((8, C))),
        (sds((8, MERGED), f32), full((8, MERGED))),
        (sds((3, TAPS, C), f32), full((3, TAPS, C))),
    ]
    gtok, out, gwf, gwh, gwp, sums_c, fsum, dk = pl.pallas_call(
        kernel_c,
        grid=(pairs,),
        out_shape=[o[0] for o in c_out],
        out_specs=[o[1] for o in c_out],
        in_specs=[smem(), smem()]
        + [rows(PAIR, C)] * 5
        + [rows(PAIR, GATES)]
        + [rows(PAIR, C)] * 3
        + [rows(3 * IMG, C2)] * 2
        + [rows(3 * SR, C2), rows(8, C2), full(h.shape)]
        + [full(w.shape) for w in (wf, wh, wp, vec, con["adj"], *bwd)],
        scratch_shapes=[
            pltpu.VMEM((PAIR, C), f32),
            pltpu.VMEM((PAIR, C), f32),
            pltpu.VMEM((PAIR, MERGED), bf16),
            pltpu.VMEM((PAIR, C), bf16),
            pltpu.VMEM((PAIR, C), bf16),
            pltpu.VMEM((HALF, C2), bf16),
            pltpu.VMEM((HALF, C2), bf16),
            pltpu.VMEM((AR, C2), f32),
            pltpu.VMEM((BR, C2), f32),
            pltpu.VMEM((HALF, C2), f32),
            pltpu.VMEM((HALF, C2), f32),
            pltpu.VMEM((AR, C2), bf16),
            pltpu.VMEM((BR, C2), bf16),
            pltpu.VMEM((6, SR, C), f32),
            pltpu.VMEM((3 * SR, C), bf16),
            pltpu.VMEM((4, 8, C), f32),
            pltpu.VMEM((8, MERGED), f32),
        ],
        compiler_params=params(62),
        name="focal_backward",
    )(
        bucket, counts, dmid, out_rows, xrow, normed, q, gates, mod, mixed, modulated, z, g, spec, mean, h,
        wf, wh, wp, vec, jnp.asarray(con["adj"]), *bwd,
    )
    return out, gtok, gwf, gwh, gwp, gw1, gw2, sums_b, bsum, sums_c, fsum, dk


def unpack_weights(mod_full, mlp_full, small):
    cut = C * (C2 + 4)
    wf = jnp.pad(mod_full[:cut].reshape(C, C2 + 4), ((0, 0), (0, GATES - 4)))
    wh = mod_full[cut : cut + C * C].reshape(C, C)
    wp = mod_full[cut + C * C :].reshape(C, C)
    w1 = mlp_full[: C * HID].reshape(C, HID)
    w2 = mlp_full[C * HID :].reshape(HID, C)
    k0 = 4 * C + 4
    taps = small[k0 : k0 + 83 * C].reshape(83, C)
    kc = []
    start = 0
    for k in LEVELS:
        piece = jnp.pad(taps[start : start + k * k], ((0, TAPS - k * k), (0, 0)))
        kc.append(jnp.concatenate([piece, piece], 0))
        start += k * k
    kcat = jnp.stack(kc)
    s32 = small.astype(f32)
    tail = k0 + 83 * C

    def seg(offset):
        return s32[offset : offset + C]

    order = [seg(0), seg(C), seg(2 * C), seg(3 * C), seg(tail), seg(tail + C), seg(tail + 2 * C), seg(tail + 3 * C), seg(tail + 4 * C)]
    order += [seg(tail + 5 * C + HID), seg(tail + 6 * C + HID), jnp.pad(s32[4 * C : 4 * C + 4], (0, C - 4))]
    vec = jnp.pad(jnp.stack(order), ((0, VROWS - len(order)), (0, 0)))
    bm1 = jnp.broadcast_to(s32[None, tail + 5 * C : tail + 5 * C + HID], (8, HID))
    return wf, wh, wp, w1, w2, vec, bm1, kcat


def pack_small(sums_b, bsum, sums_c, fsum, dk, size):
    flat = [
        sums_c[T_G1], sums_c[T_B1], fsum[0, : C2 + 4], dk[0, :9].reshape(-1), dk[1, :25].reshape(-1), dk[2, :49].reshape(-1),
        sums_c[T_HB], sums_c[T_PB], sums_b[S_S1], sums_b[S_G2], sums_b[S_B2], bsum[0], sums_b[S_BM2], sums_b[S_S2],
    ]
    used = 94 * C + 4 + HID
    return jnp.concatenate(flat + [jnp.zeros((size - used,), f32)])


def local(tokens, bucket, counts, mod_weights, mlp_weights, small_params, cotangent):
    mod_full = lax.all_gather(mod_weights, AXES, axis=0, tiled=True)
    small = lax.all_gather(small_params, AXES, axis=0, tiled=True)
    mlp_full = lax.all_gather(mlp_weights, AXES, axis=0, tiled=True)
    wf, wh, wp, w1, w2, vec, bm1, kcat = unpack_weights(mod_full, mlp_full, small)
    out, gtok, gwf, gwh, gwp, gw1, gw2, sums_b, bsum, sums_c, fsum, dk = compute(
        tokens, bucket, counts, wf, wh, wp, w1, w2, vec, bm1, kcat, cotangent
    )
    mlp_flat = jnp.concatenate([gw1.reshape(-1), gw2.reshape(-1)])
    grad_mlp = lax.psum_scatter(mlp_flat, AXES, scatter_dimension=0, tiled=True)
    mod_flat = jnp.concatenate([gwf[:, : C2 + 4].reshape(-1), gwh.reshape(-1), gwp.reshape(-1)])
    small_flat = pack_small(sums_b, bsum, sums_c, fsum, dk, small.shape[0])
    grad_mod = lax.psum_scatter(mod_flat, AXES, scatter_dimension=0, tiled=True)
    grad_small = lax.psum_scatter(small_flat, AXES, scatter_dimension=0, tiled=True)
    return out, gtok, grad_mod, grad_mlp, grad_small


def solution(mesh):
    images = P(AXES, None, None, None)
    flat = P(AXES)
    return jax.shard_map(
        local,
        mesh=mesh,
        in_specs=(images, flat, flat, flat, flat, flat, images),
        out_specs=(images, images, flat, flat, flat),
        check_vma=False,
    )
```

```python
import functools

import jax
import jax.numpy as jnp
import numpy as np
from jax import lax
from jax.experimental import pallas as pl
from jax.experimental.pallas import tpu as pltpu
from jax.sharding import PartitionSpec as P

C = 384
HID = 1536
GH = 14
GW = 20
HALF = 144
IMG = 2 * HALF
PAIR = 2 * IMG
C2 = 2 * C
NY = 17
NX = 23
NV = 12
NU = 8
Q = NU * NV
AR = 2 * (Q + 16)
BR = 2 * Q
SR = 4 * Q + 32
LEVELS = (3, 5, 7)
TAPS = 64
GATES = 128
MERGED = C2 + GATES
BROWS = 768
HCHUNK = 512
AXES = ("gx", "gy")
f32 = jnp.float32
bf16 = jnp.bfloat16
EPS = 1e-05
ROOT_HALF = 0.7071067811865476
INV_ROOT_2PI = 0.3989422804014327


def _hi(a):
    return a.astype(bf16)


def _lo(a):
    return (a - a.astype(bf16).astype(np.float64)).astype(bf16)


@functools.lru_cache(maxsize=None)
def constants():
    row = np.arange(HALF)
    real = (row < 7 * GW).astype(np.float64)
    yy = np.minimum(row // GW, 6) - (GH - 1) / 2
    xx = row % GW - (GW - 1) / 2
    uv = [(u, v) for u in range(1, NU + 1) for v in range(NV)]
    u0 = [(0, v) for v in range(NV)]
    wu = 2 * np.pi / NY
    wv = 2 * np.pi / NX

    def trig(pairs, pad):
        u = np.array([p[0] for p in pairs] + [0] * pad, np.float64)[:, None]
        v = np.array([p[1] for p in pairs] + [0] * pad, np.float64)[:, None]
        use = np.array([1.0] * len(pairs) + [0.0] * pad)[:, None] * real[None]
        cy, sy = np.cos(wu * u * yy) * use, np.sin(wu * u * yy) * use
        cx, sx = np.cos(wv * v * xx), np.sin(wv * v * xx)
        weight = np.where(u > 0, 2.0, 1.0) * np.where(v > 0, 2.0, 1.0) / (NY * NX)
        return cy * cx, -cy * sx, sy * cx, -sy * sx, weight

    e_re, e_im, o_re, o_im, w1 = trig(uv, 0)
    z_re, z_im, _, _, w0 = trig(u0, 16 - NV)
    fe = np.concatenate([e_re, z_re, e_im, z_im], 0)
    fo = np.concatenate([o_re, o_im], 0)
    half = np.concatenate([0.5 * w1, w0, 0.5 * w1, w0], 0)
    ge = (fe * half).T
    go = (fo * np.concatenate([0.5 * w1, 0.5 * w1], 0)).T

    es, adj = [], []
    for k in LEVELS:
        h = k // 2
        ty, tx = np.meshgrid(np.arange(k) - h, np.arange(k) - h, indexing="ij")
        u = np.array([p[0] for p in uv], np.float64)[:, None]
        v = np.array([p[1] for p in uv], np.float64)[:, None]
        v0 = np.array(list(range(NV)) + [0] * (16 - NV), np.float64)[:, None]
        use0 = np.array([1.0] * NV + [0.0] * (16 - NV))[:, None]
        for bucket in (0, 1):
            sy, sx = (ty, tx) if bucket == 0 else (tx, ty)
            py = sy.reshape(1, -1) * wu
            px = sx.reshape(1, -1) * wv
            plus = u * py + v * px
            minus = -u * py + v * px
            zero = v0 * px
            e = np.concatenate(
                [np.cos(plus), np.sin(plus), np.cos(minus), np.sin(minus), np.cos(zero) * use0, np.sin(zero) * use0], 0
            )
            wp = np.where(v > 0, 2.0, 1.0) / (NY * NX)
            wz = np.where(v0 > 0, 2.0, 1.0) * use0 / (NY * NX)
            a = np.concatenate(
                [
                    np.cos(plus) * wp,
                    -np.sin(plus) * wp,
                    np.cos(minus) * wp,
                    -np.sin(minus) * wp,
                    np.cos(zero) * wz,
                    -np.sin(zero) * wz,
                ],
                0,
            ).T
            full = np.zeros((SR, TAPS))
            full[:, : k * k] = e
            es.append(np.concatenate([_hi(full), _lo(full)], 1))
            back = np.zeros((TAPS, SR))
            back[: k * k] = a
            adj.append(np.concatenate([_hi(back), _hi(back), _lo(back)], 1))
    return dict(
        fe=np.concatenate([_hi(fe), _lo(fe), _hi(fe)], 1),
        fo=np.concatenate([_hi(fo), _lo(fo), _hi(fo)], 1),
        ge=np.concatenate([_hi(ge), _lo(ge), _hi(ge)], 1),
        go=np.concatenate([_hi(go), _lo(go), _hi(go)], 1),
        es=np.stack(es),
        adj=np.stack(adj),
    )


def dot(a, b):
    return jnp.dot(a, b, preferred_element_type=f32)


def dot_nt(a, b):
    return lax.dot_general(a, b, (((1,), (1,)), ((), ())), preferred_element_type=f32)


def dot_tn(a, b):
    return lax.dot_general(a, b, (((0,), (0,)), ((), ())), preferred_element_type=f32)


def gelu_pair(x):
    cdf = 0.5 * lax.erf(x * ROOT_HALF) + 0.5
    return x * cdf, cdf + x * (jnp.exp(x * x * -0.5) * INV_ROOT_2PI)


def split(x):
    hi = x.astype(bf16)
    return hi, (x - hi.astype(f32)).astype(bf16)


def at(base, i, n=16):
    return slice(base + i * n, base + i * n + n)


def norm_stats(x):
    mean = jnp.mean(x, axis=-1, keepdims=True)
    centred = x - mean
    var = jnp.mean(centred * centred, axis=-1, keepdims=True)
    r = lax.rsqrt(var + EPS)
    return centred * r, r


def sum8(x):
    total = x[0:8]
    for k in range(1, x.shape[0] // 8):
        total = total + x[8 * k : 8 * k + 8]
    return total


def grid_rows(im, y):
    return im * IMG + (y * GW if y < 7 else HALF + (GH - 1 - y) * GW)


def lanes(im):
    return slice(im * C, im * C + C)


(V_G1, V_B1, V_BQ, V_BC, V_HB, V_PB, V_S1, V_G2, V_B2, V_BM2, V_S2, V_BG) = range(12)
VROWS = 16
(S_HB, S_PB, S_S1, S_G2, S_B2, S_BM2, S_S2, S_BQ) = range(8)


def kernel_prep(counts, x_ref, cot_ref, xrow_o, up_o, n_o, nb_o, r_o, xs, cs, xr, cr):
    slots = x_ref.shape[2]
    line = GW * slots
    for im in range(slots):
        for h in (GH // 2 * GW, HALF + GH // 2 * GW):
            xr[im * IMG + h : im * IMG + h + 4, :] = jnp.zeros((4, C), f32)
            cr[im * IMG + h : im * IMG + h + 4, :] = jnp.zeros((4, C), f32)
    for y in range(GH):
        for lt in range(C // 128):
            ls = slice(128 * lt, 128 * lt + 128)
            xs[lt, line * y : line * (y + 1), :] = x_ref[y, :, :, ls].astype(f32).reshape(line, 128)
            cs[lt, line * y : line * (y + 1), :] = cot_ref[y, :, :, ls].astype(f32).reshape(line, 128)
    for im in range(slots):
        live = (im < counts[0]).astype(f32)
        for y in range(GH):
            a = grid_rows(im, y)
            for lt in range(C // 128):
                ls = slice(128 * lt, 128 * lt + 128)
                one = pl.ds(line * y + im, GW, stride=slots)
                xr[a : a + GW, ls] = xs[lt, one, :]
                cr[a : a + GW, ls] = cs[lt, one, :] * live
        for i in range(IMG // 32):
            s = at(im * IMG, i, 32)
            x = xr[s, :]
            xrow_o[s, :] = x.astype(bf16)
            up_o[s, :] = cr[s, :].astype(bf16)
            n, r = norm_stats(x)
            n_o[s, :] = n
            nb_o[s, :] = n.astype(bf16)
            r_o[s, :] = jnp.broadcast_to(r, (32, 128))


def kernel_forward(
    bucket, n_ref, wf, vec, kcat, es, fe, fo, ge, go,
    q_o, gates_o, mixed_o, z_o, g_o, spec_o, mean_o, h_o,
    normed, ctx, ecat, ocat, s_a, s_b, s_e, s_o, yca, ycb, mix,
):
    step = pl.program_id(0)

    @pl.when(step == 0)
    def _():
        for lb in range(6):
            h_o[lb] = dot(es[lb], kcat[lb // 2])

    g1, b1 = vec[V_G1 : V_G1 + 1, :], vec[V_B1 : V_B1 + 1, :]
    for i in range(PAIR // 32):
        s = at(0, i, 32)
        normed[s, :] = (n_ref[s, :] * g1 + b1).astype(bf16)
    merged = dot(normed[...], wf[...])
    ctx[...] = merged[:, C:C2] + vec[V_BC : V_BC + 1, :]
    gates_o[...] = merged[:, C2:] + vec[V_BG : V_BG + 1, :GATES]
    q_o[...] = merged[:, :C] + vec[V_BQ : V_BQ + 1, :]

    def put_pair(im, i, top, bot):
        e_hi, e_lo = split(top + bot)
        o_hi, o_lo = split(top - bot)
        for base, ev, ov in ((0, e_hi, o_hi), (HALF, e_hi, o_hi), (2 * HALF, e_lo, o_lo)):
            ecat[at(base, i), lanes(im)] = ev
            ocat[at(base, i), lanes(im)] = ov

    for im in range(2):
        for i in range(HALF // 16):
            put_pair(im, i, ctx[at(im * IMG, i), :], ctx[at(im * IMG + HALF, i), :])

    for level in range(3):
        s_a[...] = dot(fe[...], ecat[...])
        s_b[...] = dot(fo[...], ocat[...])
        base = level * SR
        for im in range(2):
            lb = level * 2 + bucket[step * 2 + im]
            for i in range(Q // 16):
                for lt in range(3):
                    ls = slice(im * C + lt * 128, im * C + lt * 128 + 128)
                    hs = slice(lt * 128, lt * 128 + 128)
                    a_re, a_im = s_a[at(0, i), ls], s_a[at(Q + 16, i), ls]
                    b_re, b_im = s_b[at(0, i), ls], s_b[at(Q, i), ls]
                    xp_re, xp_im = a_re + b_im, a_im - b_re
                    xm_re, xm_im = a_re - b_im, a_im + b_re
                    spec_o[at(base, i), ls] = xp_re
                    spec_o[at(base + Q, i), ls] = xp_im
                    spec_o[at(base + 2 * Q, i), ls] = xm_re
                    spec_o[at(base + 3 * Q, i), ls] = xm_im
                    p_re, p_im = h_o[lb, at(0, i), hs], h_o[lb, at(Q, i), hs]
                    q_re, q_im = h_o[lb, at(2 * Q, i), hs], h_o[lb, at(3 * Q, i), hs]
                    yp_re, yp_im = p_re * xp_re - p_im * xp_im, p_re * xp_im + p_im * xp_re
                    ym_re, ym_im = q_re * xm_re - q_im * xm_im, q_re * xm_im + q_im * xm_re
                    for dst, off, width, val in (
                        (yca, 0, AR, yp_re + ym_re),
                        (yca, Q + 16, AR, yp_im + ym_im),
                        (ycb, 0, BR, ym_im - yp_im),
                        (ycb, Q, BR, yp_re - ym_re),
                    ):
                        hi, lo = split(val)
                        dst[at(off, i), ls] = hi
                        dst[at(off + width, i), ls] = hi
                        dst[at(off + 2 * width, i), ls] = lo
            ls = lanes(im)
            x_re, x_im = s_a[Q : Q + 16, ls], s_a[2 * Q + 16 : 2 * Q + 32, ls]
            spec_o[base + 4 * Q : base + 4 * Q + 16, ls] = x_re
            spec_o[base + 4 * Q + 16 : base + 4 * Q + 32, ls] = x_im
            p_re, p_im = h_o[lb, 4 * Q : 4 * Q + 16, :], h_o[lb, 4 * Q + 16 : 4 * Q + 32, :]
            for off, val in ((Q, p_re * x_re - p_im * x_im), (2 * Q + 16, p_re * x_im + p_im * x_re)):
                hi, lo = split(val)
                yca[off : off + 16, ls] = hi
                yca[off + AR : off + AR + 16, ls] = hi
                yca[off + 2 * AR : off + 2 * AR + 16, ls] = lo
        s_e[...] = dot(ge[...], yca[...])
        s_o[...] = dot(go[...], ycb[...])
        for im in range(2):
            ls = lanes(im)
            total = jnp.zeros((8, C), f32)
            for i in range(HALF // 16):
                even, odd = s_e[at(0, i), ls], s_o[at(0, i), ls]
                both = []
                for h, a in ((0, even + odd), (HALF, even - odd)):
                    z, g = gelu_pair(a)
                    z_o[at(level * IMG + h, i), ls] = z.astype(bf16)
                    g_o[at(level * IMG + h, i), ls] = g
                    s = at(im * IMG + h, i)
                    part = z * gates_o[s, level : level + 1]
                    mix[s, :] = part if level == 0 else mix[s, :] + part
                    both.append(z)
                if level < 2:
                    put_pair(im, i, both[0], both[1])
                else:
                    total = total + sum8(both[0]) + sum8(both[1])
            if level == 2:
                mean = jnp.sum(total, axis=0, keepdims=True) * (1.0 / (GH * GW))
                mean_o[:, ls] = jnp.broadcast_to(mean, (8, C))

    for im in range(2):
        glob, _ = gelu_pair(mean_o[0:1, lanes(im)])
        for i in range(IMG // 32):
            s = at(im * IMG, i, 32)
            mixed_o[s, :] = (mix[s, :] + gates_o[s, 3:4] * glob).astype(bf16)


def kernel_middle(
    x_ref, up, mixed, q_ref, wh, wp, w1, w2, vec, bm1,
    dmid_o, out_o, dq_o, dmix_o, gw1, gw2, gwh, gwp, sums, bsum,
    mod, modulated, branch, mid, second, dshr, shr, dsec, act, dexp, hid, vacc, bacc,
):
    step = pl.program_id(0)

    @pl.when(step == 0)
    def _():
        for ref in (gw1, gw2, gwh, gwp, vacc, bacc):
            ref[...] = jnp.zeros_like(ref)

    g2, b2 = vec[V_G2 : V_G2 + 1, :], vec[V_B2 : V_B2 + 1, :]
    s1, s2 = vec[V_S1 : V_S1 + 1, :], vec[V_S2 : V_S2 + 1, :]
    bm2 = vec[V_BM2 : V_BM2 + 1, :]
    zero = jnp.zeros((8, C), f32)

    mod[...] = dot(mixed[...], wh[...]) + vec[V_HB : V_HB + 1, :]
    for i in range(BROWS // 32):
        s = at(0, i, 32)
        modulated[s, :] = (q_ref[s, :] * mod[s, :]).astype(bf16)
        dshr[s, :] = (up[s, :].astype(f32) * s2).astype(bf16)
    branch[...] = dot(modulated[...], wp[...]) + vec[V_PB : V_PB + 1, :]
    for i in range(BROWS // 32):
        s = at(0, i, 32)
        middle = x_ref[s, :].astype(f32) + s1 * branch[s, :]
        mid[s, :] = middle
        n, _ = norm_stats(middle)
        second[s, :] = (n * g2 + b2).astype(bf16)

    for h in range(HID // HCHUNK):
        hs = slice(h * HCHUNK, (h + 1) * HCHUNK)
        hid[...] = dot(second[...], w1[:, hs]) + bm1[0:1, hs]
        dact = dot_nt(dshr[...], w2[hs, :])
        total = jnp.zeros((8, HCHUNK), f32)
        for i in range(BROWS // 16):
            s = at(0, i)
            z, g = gelu_pair(hid[s, :])
            act[s, :] = z.astype(bf16)
            d = dact[s, :] * g
            dexp[s, :] = d.astype(bf16)
            total = total + sum8(d)
        bacc[:, hs] += total
        part = dot(act[...], w2[hs, :])
        back = dot_nt(dexp[...], w1[:, hs])
        if h == 0:
            shr[...] = part
            dsec[...] = back
        else:
            shr[...] += part
            dsec[...] += back
        gw1[:, hs] += dot_tn(second[...], dexp[...])
        gw2[hs, :] += dot_tn(act[...], dshr[...])

    t_s1 = t_g2 = t_b2 = t_bm2 = t_s2 = t_pb = t_hb = t_bq = zero
    dbr = second
    for i in range(BROWS // 32):
        s = at(0, i, 32)
        middle = mid[s, :]
        u = up[s, :].astype(f32)
        shrunk = shr[s, :] + bm2
        out_o[s, :] = middle + s2 * shrunk
        n, r = norm_stats(middle)
        d = dsec[s, :]
        e = d * g2
        dn = d * n
        dv = r * (e - jnp.mean(e, axis=-1, keepdims=True) - n * jnp.mean(e * n, axis=-1, keepdims=True))
        dm = u + dv
        dmid_o[s, :] = dm
        db = s1 * dm
        dbr[s, :] = db.astype(bf16)
        t_s1 = t_s1 + sum8(dm * branch[s, :])
        t_g2 = t_g2 + sum8(dn)
        t_b2 = t_b2 + sum8(d)
        t_bm2 = t_bm2 + sum8(dshr[s, :].astype(f32))
        t_s2 = t_s2 + sum8(u * shrunk)
        t_pb = t_pb + sum8(db)

    gwp[...] += dot_tn(modulated[...], dbr[...])
    dmod = dot_nt(dbr[...], wp[...])
    dm2 = dshr
    for i in range(BROWS // 32):
        s = at(0, i, 32)
        dm = dmod[s, :]
        dq = dm * mod[s, :]
        dd = dm * q_ref[s, :]
        dq_o[s, :] = dq.astype(bf16)
        dm2[s, :] = dd.astype(bf16)
        t_bq = t_bq + sum8(dq)
        t_hb = t_hb + sum8(dd)
    gwh[...] += dot_tn(mixed[...], dm2[...])
    dmix_o[...] = dot_nt(dm2[...], wh[...])

    for k, t in ((S_HB, t_hb), (S_PB, t_pb), (S_S1, t_s1), (S_G2, t_g2), (S_B2, t_b2), (S_BM2, t_bm2), (S_S2, t_s2), (S_BQ, t_bq)):
        vacc[k] += t

    @pl.when(step == pl.num_programs(0) - 1)
    def _():
        for k in range(8):
            sums[k : k + 1, :] = jnp.sum(vacc[k], axis=0, keepdims=True)
        bsum[...] = jnp.broadcast_to(jnp.sum(bacc[...], axis=0, keepdims=True), bsum.shape)


def kernel_backward(
    bucket, nb_ref, dq_ref, dmix, gates, z_ref, g_ref, spec, mean_ref, h_ref, wf, vec, sums, adj, fe, fo, ge, go,
    dmer, gwf, fsum, gb, dk,
    ecat, ocat, s_a, s_b, s_e, s_o, yca, ycb, acc, cat, facc,
):
    step = pl.program_id(0)
    last = pl.num_programs(0) - 1

    @pl.when(step == 0)
    def _():
        for ref in (gwf, facc, acc):
            ref[...] = jnp.zeros_like(ref)

    zero = jnp.zeros((8, C), f32)
    lane = lax.broadcasted_iota(jnp.int32, (16, GATES), 1)
    dmeans = []
    t_g = jnp.zeros((8, GATES), f32)
    for im in range(2):
        ls = lanes(im)
        glob, dglob = gelu_pair(mean_ref[0:1, ls])
        t_glob = zero
        for i in range(HALF // 16):
            for h in (0, HALF):
                s = at(im * IMG + h, i)
                dm = dmix[s, :]
                dg = jnp.zeros((16, GATES), f32)
                for k in range(4):
                    other = z_ref[at(k * IMG + h, i), ls].astype(f32) if k < 3 else glob
                    col = jnp.sum(dm * other, axis=-1, keepdims=True)
                    dg = jnp.where(lane == k, col, dg)
                dmer[s, :C] = dq_ref[s, :]
                dmer[s, C2:] = dg.astype(bf16)
                t_g = t_g + sum8(dg)
                t_glob = t_glob + sum8(dm * gates[s, 3:4])
        dmeans.append(jnp.sum(t_glob, axis=0, keepdims=True) * dglob * (1.0 / (GH * GW)))
    facc[:, C2:] += t_g

    for level in (2, 1, 0):
        for im in range(2):
            ls = lanes(im)
            for i in range(HALF // 16):
                parts = []
                if level < 2:
                    even, odd = s_e[at(0, i), ls], s_o[at(0, i), ls]
                    through = (even + odd, even - odd)
                else:
                    through = (dmeans[im], dmeans[im])
                for k, h in enumerate((0, HALF)):
                    s = at(im * IMG + h, i)
                    dz = gates[s, level : level + 1] * dmix[s, :] + through[k]
                    parts.append(dz * g_ref[at(level * IMG + h, i), ls])
                ecat[at(0, i), ls] = (parts[0] + parts[1]).astype(bf16)
                ocat[at(0, i), ls] = (parts[0] - parts[1]).astype(bf16)
        s_a[...] = dot(fe[...], ecat[...])
        s_b[...] = dot(fo[...], ocat[...])
        base = level * SR
        for im in range(2):
            lb = level * 2 + bucket[step * 2 + im]
            for i in range(Q // 16):
                for lt in range(3):
                    ls = slice(im * C + lt * 128, im * C + lt * 128 + 128)
                    hs = slice(lt * 128, lt * 128 + 128)
                    a_re, a_im = s_a[at(0, i), ls], s_a[at(Q + 16, i), ls]
                    b_re, b_im = s_b[at(0, i), ls], s_b[at(Q, i), ls]
                    dp_re, dp_im = a_re + b_im, a_im - b_re
                    dm_re, dm_im = a_re - b_im, a_im + b_re
                    xp_re, xp_im = spec[at(base, i), ls], spec[at(base + Q, i), ls]
                    xm_re, xm_im = spec[at(base + 2 * Q, i), ls], spec[at(base + 3 * Q, i), ls]
                    acc[lb, at(0, i), hs] += xp_re * dp_re + xp_im * dp_im
                    acc[lb, at(Q, i), hs] += xp_im * dp_re - xp_re * dp_im
                    acc[lb, at(2 * Q, i), hs] += xm_re * dm_re + xm_im * dm_im
                    acc[lb, at(3 * Q, i), hs] += xm_im * dm_re - xm_re * dm_im
                    p_re, p_im = h_ref[lb, at(0, i), hs], h_ref[lb, at(Q, i), hs]
                    q_re, q_im = h_ref[lb, at(2 * Q, i), hs], h_ref[lb, at(3 * Q, i), hs]
                    yp_re, yp_im = p_re * dp_re + p_im * dp_im, p_re * dp_im - p_im * dp_re
                    ym_re, ym_im = q_re * dm_re + q_im * dm_im, q_re * dm_im - q_im * dm_re
                    yca[at(0, i), ls] = (yp_re + ym_re).astype(bf16)
                    yca[at(Q + 16, i), ls] = (yp_im + ym_im).astype(bf16)
                    ycb[at(0, i), ls] = (ym_im - yp_im).astype(bf16)
                    ycb[at(Q, i), ls] = (yp_re - ym_re).astype(bf16)
            ls = lanes(im)
            d_re, d_im = s_a[Q : Q + 16, ls], s_a[2 * Q + 16 : 2 * Q + 32, ls]
            x_re = spec[base + 4 * Q : base + 4 * Q + 16, ls]
            x_im = spec[base + 4 * Q + 16 : base + 4 * Q + 32, ls]
            acc[lb, 4 * Q : 4 * Q + 16, :] += x_re * d_re + x_im * d_im
            acc[lb, 4 * Q + 16 : 4 * Q + 32, :] += x_im * d_re - x_re * d_im
            p_re, p_im = h_ref[lb, 4 * Q : 4 * Q + 16, :], h_ref[lb, 4 * Q + 16 : 4 * Q + 32, :]
            yca[Q : Q + 16, ls] = (p_re * d_re + p_im * d_im).astype(bf16)
            yca[2 * Q + 16 : 2 * Q + 32, ls] = (p_re * d_im - p_im * d_re).astype(bf16)
        s_e[...] = dot(ge[...], yca[...])
        s_o[...] = dot(go[...], ycb[...])

    t_c = zero
    for im in range(2):
        ls = lanes(im)
        for i in range(HALF // 16):
            even, odd = s_e[at(0, i), ls], s_o[at(0, i), ls]
            top, bot = even + odd, even - odd
            dmer[at(im * IMG, i), C:C2] = top.astype(bf16)
            dmer[at(im * IMG + HALF, i), C:C2] = bot.astype(bf16)
            t_c = t_c + sum8(top) + sum8(bot)
    facc[:, C:C2] += t_c
    gwf[...] += dot_tn(nb_ref[...], dmer[...])

    @pl.when(step == last)
    def _():
        facc[:, :C] = jnp.broadcast_to(sums[S_BQ : S_BQ + 1, :] * 0.125, (8, C))
        colsum = jnp.sum(facc[...], axis=0, keepdims=True)
        fsum[...] = jnp.broadcast_to(colsum, fsum.shape)
        wide = wf[...].astype(f32)
        t_hi, t_lo = split(wide * gwf[...])
        ones = jnp.ones((8, MERGED), bf16)
        gb[0:8, :] = dot_nt(ones, t_hi) + dot_nt(ones, t_lo)
        c_hi, c_lo = split(fsum[...])
        gb[8:16, :] = dot_nt(c_hi, wf[...]) + dot_nt(c_lo, wf[...])
        g1 = jnp.transpose(jnp.broadcast_to(vec[V_G1 : V_G1 + 1, :], (128, C)))
        b1 = jnp.transpose(jnp.broadcast_to(vec[V_B1 : V_B1 + 1, :], (128, C)))
        for t in range(MERGED // 128):
            ls = slice(128 * t, 128 * t + 128)
            gwf[:, ls] = gwf[:, ls] * g1 + b1 * fsum[0:1, ls]
        for level in range(3):
            total = None
            for b in range(2):
                lb = level * 2 + b
                for i in range(SR // 16):
                    hi, lo = split(acc[lb, at(0, i), :])
                    cat[at(0, i), :] = hi
                    cat[at(SR, i), :] = lo
                    cat[at(2 * SR, i), :] = hi
                term = dot(adj[lb], cat[...])
                total = term if total is None else total + term
            dk[level] = total


def kernel_tail(counts, dmer, wf, n_ref, r_ref, dmid, out_rows, vec, gtok_o, out_o, stage, gs, os):
    step = pl.program_id(0)
    slots = out_o.shape[2]
    line = GW * slots
    g1 = vec[V_G1 : V_G1 + 1, :]
    d_normed = dot_nt(dmer[...], wf[...])
    for i in range(PAIR // 32):
        s = at(0, i, 32)
        n = n_ref[s, :]
        e = d_normed[s, :] * g1
        dv = e - jnp.mean(e, axis=-1, keepdims=True) - n * jnp.mean(e * n, axis=-1, keepdims=True)
        stage[s, :] = dmid[s, :] + r_ref[s, 0:1] * dv
    for im in range(2):
        slot = step * 2 + im
        live = (slot < counts[0]).astype(f32)
        for y in range(GH):
            a = grid_rows(im, y)
            for lt in range(C // 128):
                ls = slice(128 * lt, 128 * lt + 128)
                one = pl.ds(line * y + slot, GW, stride=slots)
                gs[lt, one, :] = stage[a : a + GW, ls]
                os[lt, one, :] = out_rows[a : a + GW, ls] * live

    @pl.when(step == pl.num_programs(0) - 1)
    def _():
        for y in range(GH):
            for lt in range(C // 128):
                ls = slice(128 * lt, 128 * lt + 128)
                gtok_o[y, :, :, ls] = gs[lt, line * y : line * (y + 1), :].reshape(GW, slots, 128)
                out_o[y, :, :, ls] = os[lt, line * y : line * (y + 1), :].reshape(GW, slots, 128).astype(bf16)


def block_rows(length):
    return 8 * (length // 1024 if length % 1024 == 0 else (length + 1022) // 1024 + 1)


def place(shard, device):
    length = shard.shape[0]
    n = block_rows(length) * 128
    if n == length:
        return shard.reshape(-1, 128)
    offset = lax.rem(device * length, 1024)
    return lax.dynamic_update_slice(jnp.zeros((n,), shard.dtype), shard, (offset,)).reshape(-1, 128)


def take(block, length, device):
    flat = block.reshape(-1)
    if flat.shape[0] == length:
        return flat
    return lax.dynamic_slice(flat, (lax.rem(device * length, 1024),), (length,))


def first_row(length, device):
    return pl.multiple_of((device * length) // 1024 * 8, 8)


def device_at(pos, gy, i, j, c):
    return (pos[0] ^ j) * gy + (pos[1] ^ (2 * i + c))


def shift_left(first, second, sh):
    if sh == 0:
        return first
    lane = lax.broadcasted_iota(jnp.int32, first.shape, 1)
    return jnp.where(lane < 128 - sh, pltpu.roll(first, 128 - sh, 1), pltpu.roll(second, 128 - sh, 1))


def shift_right(first, second, sh):
    lane = lax.broadcasted_iota(jnp.int32, first.shape, 1)
    return jnp.where(lane < sh, pltpu.roll(first, sh, 1), pltpu.roll(second, sh, 1))


WIDE = C2 + 4
WF_ROWS = C * WIDE // 128
W_ROWS = C * C // 128
PERIOD = 32
STRIDE = PERIOD * WIDE // 128
K_ROW = 12
TAIL_ROW = K_ROW + 83 * C // 128
B_HB, B_PB, B_S1, B_G2, B_B2, B_BM1 = (TAIL_ROW + 3 * k for k in range(6))
B_BM2 = B_BM1 + HID // 128
B_S2 = B_BM2 + 3
END_ROW = B_S2 + 3


def kernel_unpack_mod(gx, gy, mod_len, small_len, pos, own, oth, wf_o, wh_o, wp_o, vec_o, bm1_o, kcat_o, flat, small, moved, wide):
    flat[...] = jnp.zeros_like(flat)
    small[...] = jnp.zeros_like(small)
    mr, sr = block_rows(mod_len), block_rows(small_len)
    for i in range(gy // 2):
        for j in range(gx):
            for c, src in enumerate((own, oth)):
                d = device_at(pos, gy, i, j, c)
                block = src[i, j].astype(f32)
                flat[pl.ds(first_row(mod_len, d), mr), :] += block[:mr]
                small[pl.ds(first_row(small_len, d), sr), :] += block[mr : mr + sr]
    lane = lax.broadcasted_iota(jnp.int32, (16, 128), 1)
    for p in range(PERIOD):
        for j in range(MERGED // 128):
            f = WIDE * p + 128 * j
            row, sh = f // 128, f % 128
            a = flat[pl.ds(row, 16, stride=STRIDE), :]
            b = flat[pl.ds(row + 1, 16, stride=STRIDE), :] if sh else a
            v = shift_left(a, b, sh)
            if j == MERGED // 128 - 1:
                v = jnp.where(lane < 4, v, 0.0)
            wide[j, pl.ds(p, 16, stride=PERIOD), :] = v
    for j in range(MERGED // 128):
        wf_o[:, 128 * j : 128 * j + 128] = wide[j, :C, :].astype(bf16)
    for j in range(3):
        ls = slice(128 * j, 128 * j + 128)
        wh_o[:, ls] = flat[pl.ds(WF_ROWS + j, C, stride=3), :].astype(bf16)
        wp_o[:, ls] = flat[pl.ds(WF_ROWS + W_ROWS + j, C, stride=3), :].astype(bf16)
    n = moved.shape[0]
    moved[...] = shift_left(small[0:n, :], small[1 : n + 1, :], 4)
    vec_o[...] = jnp.zeros_like(vec_o)
    for row, src, start in (
        (V_G1, small, 0), (V_B1, small, 3), (V_BQ, small, 6), (V_BC, small, 9),
        (V_HB, moved, B_HB), (V_PB, moved, B_PB), (V_S1, moved, B_S1), (V_G2, moved, B_G2), (V_B2, moved, B_B2),
        (V_BM2, moved, B_BM2), (V_S2, moved, B_S2),
    ):
        for j in range(3):
            vec_o[row : row + 1, 128 * j : 128 * j + 128] = src[start + j : start + j + 1, :]
    vec_o[V_BG : V_BG + 1, 0:128] = jnp.where(lane[0:1] < 4, small[K_ROW : K_ROW + 1, :], 0.0)
    for t in range(HID // 128):
        bm1_o[:, 128 * t : 128 * t + 128] = jnp.broadcast_to(moved[B_BM1 + t : B_BM1 + t + 1, :], (8, 128))
    start = 0
    for level, k in enumerate(LEVELS):
        for j in range(3):
            taps = moved[pl.ds(K_ROW + 3 * start + j, TAPS, stride=3), :].astype(bf16)
            kcat_o[level, 0:TAPS, 128 * j : 128 * j + 128] = taps
            kcat_o[level, TAPS:, 128 * j : 128 * j + 128] = taps
        start += k * k


def kernel_unpack_mlp(gx, gy, mlp_len, pos, *refs):
    blocks, (w1_o, w2_o, flat) = refs[: gy // 2], refs[gy // 2 :]
    mr = block_rows(mlp_len)
    aligned = mr * 128 == mlp_len
    if not aligned:
        flat[...] = jnp.zeros_like(flat)
    for i, src in enumerate(blocks):
        for j in range(gx):
            for c in range(2):
                rows_at = pl.ds(first_row(mlp_len, device_at(pos, gy, i, j, c)), mr)
                if aligned:
                    flat[rows_at, :] = src[c, j].astype(f32)
                else:
                    flat[rows_at, :] += src[c, j].astype(f32)
    for t in range(HID // 128):
        w1_o[:, 128 * t : 128 * t + 128] = flat[pl.ds(t, C, stride=HID // 128), :].astype(bf16)
    for t in range(C // 128):
        w2_o[:, 128 * t : 128 * t + 128] = flat[pl.ds(C * HID // 128 + t, HID, stride=C // 128), :].astype(bf16)


def send_slots(gx, gy, pos, flat, length, base, own, oth):
    mr = block_rows(length)
    for i in range(gy // 2):
        for j in range(gx):
            for c, dst in enumerate((own, oth)):
                d = device_at(pos, gy, i, j, c)
                dst[i, j, base : base + mr, :] = flat[pl.ds(first_row(length, d), mr), :].astype(bf16)


def kernel_pack_mlp(gx, gy, mlp_len, pos, gw1, gw2, own, oth, flat):
    used = 2 * C * HID // 128
    if flat.shape[0] > used:
        flat[used:, :] = jnp.zeros_like(flat[used:, :])
    for t in range(HID // 128):
        flat[pl.ds(t, C, stride=HID // 128), :] = gw1[:, 128 * t : 128 * t + 128]
    for t in range(C // 128):
        flat[pl.ds(C * HID // 128 + t, HID, stride=C // 128), :] = gw2[:, 128 * t : 128 * t + 128]
    send_slots(gx, gy, pos, flat, mlp_len, 0, own, oth)


def kernel_pack_mod(gx, gy, mod_len, small_len, pos, gwf, gwh, gwp, sums, bsum, fsum, gb, dk, own, oth, flat, small, moved, wide):
    lane = lax.broadcasted_iota(jnp.int32, (16, 128), 1)
    used = WF_ROWS + 2 * W_ROWS
    if flat.shape[0] > used:
        flat[used:, :] = jnp.zeros_like(flat[used:, :])
    for j in range(MERGED // 128):
        wide[j, :C, :] = gwf[:, 128 * j : 128 * j + 128]
    for f in range(STRIDE):
        p = 128 * f // WIDE
        col = 128 * f - WIDE * p
        t, sh = col // 128, col % 128

        def piece(row, tile):
            tile = min(tile, MERGED // 128 - 1)
            return wide[tile, pl.ds(row, 16, stride=PERIOD), :]

        v = shift_left(piece(p, t), piece(p, t + 1), sh)
        left = WIDE - col
        if left < 128:
            v = jnp.where(lane < left, v, pltpu.roll(piece(p + 1, 0), left, 1))
        flat[pl.ds(f, 16, stride=STRIDE), :] = v
    for j in range(3):
        ls = slice(128 * j, 128 * j + 128)
        flat[pl.ds(WF_ROWS + j, C, stride=3), :] = gwh[:, ls]
        flat[pl.ds(WF_ROWS + W_ROWS + j, C, stride=3), :] = gwp[:, ls]
    moved[...] = jnp.zeros_like(moved)
    small[...] = jnp.zeros_like(small)
    start = 0
    for level, k in enumerate(LEVELS):
        for j in range(3):
            moved[pl.ds(K_ROW + 3 * start + j, k * k, stride=3), :] = dk[level, 0 : k * k, 128 * j : 128 * j + 128]
        start += k * k
    for start, row in (
        (B_HB, S_HB), (B_PB, S_PB), (B_S1, S_S1), (B_G2, S_G2), (B_B2, S_B2), (B_BM2, S_BM2), (B_S2, S_S2),
    ):
        for j in range(3):
            moved[start + j : start + j + 1, :] = sums[row : row + 1, 128 * j : 128 * j + 128]
    for t in range(HID // 128):
        moved[B_BM1 + t : B_BM1 + t + 1, :] = bsum[0:1, 128 * t : 128 * t + 128]
    n = moved.shape[0]
    small[8:n, :] = shift_right(moved[7 : n - 1, :], moved[8:n, :], 4)
    for j in range(3):
        ls = slice(128 * j, 128 * j + 128)
        small[j : j + 1, :] = gb[0:1, ls]
        small[3 + j : 4 + j, :] = gb[8:9, ls]
        small[6 + j : 7 + j, :] = fsum[0:1, ls]
        small[9 + j : 10 + j, :] = fsum[0:1, C + 128 * j : C + 128 * j + 128]
    gate_lane = lane[0:1] < 4
    small[K_ROW : K_ROW + 1, :] = jnp.where(gate_lane, fsum[0:1, C2:], small[K_ROW : K_ROW + 1, :])
    mr, sr = block_rows(mod_len), block_rows(small_len)
    send_slots(gx, gy, pos, flat, mod_len, 0, own, oth)
    for i in range(gy // 2):
        for j in range(gx):
            for c, dst in enumerate((own, oth)):
                block = small[pl.ds(first_row(small_len, device_at(pos, gy, i, j, c)), sr), :]
                pad = own.shape[2] - mr - sr
                if pad:
                    block = jnp.concatenate([block, jnp.zeros((pad, 128), f32)], 0)
                dst[i, j, mr:, :] = block.astype(bf16)


def kernel_add(n_in, *refs):
    outs = refs[n_in:]
    many = len(outs) > 1
    for k, o in enumerate(outs):
        total = None
        for ref in refs[:n_in]:
            v = (ref[k] if many else ref[...]).astype(f32)
            total = v if total is None else total + v
        o[...] = total.astype(o.dtype)


def full(shape):
    return pl.BlockSpec(shape, lambda *i, n=len(shape): (0,) * n)


def rows(n, width):
    return pl.BlockSpec((n, width), lambda i: (i, 0))


def smem():
    return pl.BlockSpec(memory_space=pltpu.SMEM)


def sds(shape, dtype):
    return jax.ShapeDtypeStruct(shape, dtype)


def call(kernel, name, grid, ins, outs, scratch, mib, micros):
    return pl.pallas_call(
        kernel,
        grid=grid,
        in_specs=[s for _, s in ins],
        out_shape=[o for o, _ in outs],
        out_specs=[s for _, s in outs],
        scratch_shapes=[pltpu.VMEM(shape, dtype) for shape, dtype in scratch],
        compiler_params=pltpu.CompilerParams(vmem_limit_bytes=mib * 2**20),
        cost_estimate=pl.CostEstimate(flops=int(micros * 1e9), bytes_accessed=int(micros * 1e6), transcendentals=0),
        name=name,
    )(*[a for a, _ in ins])


def whole(*arrays):
    return [(a, full(a.shape)) for a in arrays]


def by_rows(n, *arrays):
    return [(a, rows(n, a.shape[1])) for a in arrays]


def prep(tokens, counts, cotangent):
    slots = tokens.shape[2]
    n = slots * IMG
    outs = [(sds((n, C), t), full((n, C))) for t in (bf16, bf16, f32, bf16)] + [(sds((n, 128), f32), full((n, 128)))]
    native = ((C // 128, GH * GW * slots, 128), f32)
    scratch = [native, native, ((n, C), f32), ((n, C), f32)]
    return call(kernel_prep, "prep", (), [(counts, smem())] + whole(tokens, cotangent), outs, scratch, 60, 6)


def forward(n1, bucket, wf, vec, kcat):
    con = constants()
    pairs = n1.shape[0] // PAIR
    n = pairs * PAIR
    outs = [
        (sds((n, C), f32), rows(PAIR, C)),
        (sds((n, GATES), f32), rows(PAIR, GATES)),
        (sds((n, C), bf16), rows(PAIR, C)),
        (sds((pairs * 3 * IMG, C2), bf16), rows(3 * IMG, C2)),
        (sds((pairs * 3 * IMG, C2), f32), rows(3 * IMG, C2)),
        (sds((pairs * 3 * SR, C2), f32), rows(3 * SR, C2)),
        (sds((pairs * 8, C2), f32), rows(8, C2)),
        (sds((6, SR, C), f32), full((6, SR, C))),
    ]
    mats = [jnp.asarray(con[k]) for k in ("es", "fe", "fo", "ge", "go")]
    ins = [(bucket, smem())] + by_rows(PAIR, n1) + whole(wf, vec, kcat, *mats)
    scratch = [
        ((PAIR, C), bf16), ((PAIR, C), f32), ((3 * HALF, C2), bf16), ((3 * HALF, C2), bf16), ((AR, C2), f32), ((BR, C2), f32),
        ((HALF, C2), f32), ((HALF, C2), f32), ((3 * AR, C2), bf16), ((3 * BR, C2), bf16), ((PAIR, C), f32),
    ]
    return call(kernel_forward, "focal_forward", (pairs,), ins, outs, scratch, 60, 32)


def middle(xrow, up, mixed, q, wh, wp, w1, w2, vec, bm1):
    n = xrow.shape[0]
    outs = [
        (sds((n, C), f32), rows(BROWS, C)),
        (sds((n, C), f32), rows(BROWS, C)),
        (sds((n, C), bf16), rows(BROWS, C)),
        (sds((n, C), f32), rows(BROWS, C)),
    ]
    outs += [(sds(s, f32), full(s)) for s in ((C, HID), (HID, C), (C, C), (C, C), (8, C), (8, HID))]
    ins = by_rows(BROWS, xrow, up, mixed, q) + whole(wh, wp, w1, w2, vec, bm1)
    blk = (BROWS, C)
    scratch = [
        (blk, f32), (blk, bf16), (blk, f32), (blk, f32), (blk, bf16), (blk, bf16), (blk, f32), (blk, f32),
        ((BROWS, HCHUNK), bf16), ((BROWS, HCHUNK), bf16), ((BROWS, HCHUNK), f32), ((8, 8, C), f32), ((8, HID), f32),
    ]
    return call(kernel_middle, "middle", (n // BROWS,), ins, outs, scratch, 62, 42)


def backward(bucket, nb, dq, dmix, gates, z, g, spec, mean, h, wf, vec, sums):
    con = constants()
    pairs = nb.shape[0] // PAIR
    mats = [jnp.asarray(con["adj"]), jnp.asarray(con["fe"][:, :HALF]), jnp.asarray(con["fo"][:, :HALF])]
    mats += [jnp.asarray(con["ge"][:, :AR]), jnp.asarray(con["go"][:, :BR])]
    outs = [(sds((nb.shape[0], MERGED), bf16), rows(PAIR, MERGED))]
    outs += [(sds(s, f32), full(s)) for s in ((C, MERGED), (8, MERGED), (16, C), (3, TAPS, C))]
    ins = [(bucket, smem())] + by_rows(PAIR, nb, dq, dmix, gates) + by_rows(3 * IMG, z, g) + by_rows(3 * SR, spec)
    ins += by_rows(8, mean) + whole(h, wf, vec, sums, *mats)
    scratch = [
        ((HALF, C2), bf16), ((HALF, C2), bf16), ((AR, C2), f32), ((BR, C2), f32), ((HALF, C2), f32), ((HALF, C2), f32),
        ((AR, C2), bf16), ((BR, C2), bf16), ((6, SR, C), f32), ((3 * SR, C), bf16), ((8, MERGED), f32),
    ]
    return call(kernel_backward, "focal_backward", (pairs,), ins, outs, scratch, 62, 32)


def tail(shape, counts, dmer, wf, n1, r1, dmid, out_rows, vec):
    slots = shape[2]
    outs = [(sds(shape, f32), full(shape)), (sds(shape, bf16), full(shape))]
    ins = [(counts, smem())] + by_rows(PAIR, dmer) + whole(wf) + by_rows(PAIR, n1, r1, dmid, out_rows) + whole(vec)
    native = ((C // 128, GH * GW * slots, 128), f32)
    return call(kernel_tail, "tail", (slots // 2,), ins, outs, [((PAIR, C), f32), native, native], 60, 10)


def span(length, ndev):
    return ((ndev - 1) * length) // 1024 * 8 + block_rows(length)


def unpack_mod(gx, gy, pos, own, oth, mod_len, small_len):
    ndev = gx * gy
    outs = [sds((C, MERGED), bf16), sds((C, C), bf16), sds((C, C), bf16), sds((VROWS, C), f32), sds((8, HID), f32), sds((3, 2 * TAPS, C), bf16)]
    top = STRIDE * 15 + STRIDE + 8
    flat_rows = max(span(mod_len, ndev), top)
    small_rows = max(span(small_len, ndev), END_ROW + 26)
    scratch = [((flat_rows, 128), f32), ((small_rows + 8, 128), f32), ((small_rows, 128), f32), ((MERGED // 128, PERIOD * 16, 128), f32)]
    kernel = functools.partial(kernel_unpack_mod, gx, gy, mod_len, small_len)
    return call(kernel, "unpack_mod", (), [(pos, smem())] + whole(own, oth), [(o, full(o.shape)) for o in outs], scratch, 48, 4)


def unpack_mlp(gx, gy, pos, blocks, mlp_len):
    outs = [sds((C, HID), bf16), sds((HID, C), bf16)]
    kernel = functools.partial(kernel_unpack_mlp, gx, gy, mlp_len)
    scratch = [((span(mlp_len, gx * gy), 128), f32)]
    return call(kernel, "unpack_mlp", (), [(pos, smem())] + whole(*blocks), [(o, full(o.shape)) for o in outs], scratch, 48, 3)


def pack_mlp(gx, gy, pos, gw1, gw2, mlp_len):
    shape = (gy // 2, gx, block_rows(mlp_len), 128)
    outs = [sds(shape, bf16)] * 2
    kernel = functools.partial(kernel_pack_mlp, gx, gy, mlp_len)
    scratch = [((span(mlp_len, gx * gy), 128), f32)]
    return call(kernel, "pack_mlp", (), [(pos, smem())] + whole(gw1, gw2), [(o, full(o.shape)) for o in outs], scratch, 48, 3)


def pack_mod(gx, gy, pos, grads, mod_len, small_len):
    ndev = gx * gy
    shape = (gy // 2, gx, -(-(block_rows(mod_len) + block_rows(small_len)) // 16) * 16, 128)
    outs = [sds(shape, bf16)] * 2
    kernel = functools.partial(kernel_pack_mod, gx, gy, mod_len, small_len)
    small_rows = -(-max(span(small_len, ndev), END_ROW + 2) // 8) * 8
    scratch = [((max(span(mod_len, ndev), STRIDE * 16 + 8), 128), f32), ((small_rows, 128), f32), ((small_rows, 128), f32)]
    scratch.append(((MERGED // 128, PERIOD * 16, 128), f32))
    return call(kernel, "pack_mod", (), [(pos, smem())] + whole(*grads), [(o, full(o.shape)) for o in outs], scratch, 48, 4)


def add(arrays, outs, name):
    return call(functools.partial(kernel_add, len(arrays)), name, (), whole(*arrays), [(o, full(o.shape)) for o in outs], [], 48, 2)


def swap(x, mask, ndev):
    return lax.ppermute(x, AXES, [(k, k ^ mask) for k in range(ndev)])


def around(x, step, count, ndev):
    return [x] + [swap(x, step * k, ndev) for k in range(1, count)]


def after(values):
    return lax.optimization_barrier(values)


def travel(parts, step, ndev):
    return [parts[0]] + [swap(p, step * k, ndev) for k, p in enumerate(parts) if k]


def sum_core(own, oth, gx, gy, name):
    got = swap(oth, 1, gx * gy)
    return add([own, got], [sds(own.shape[1:], f32 if k == 0 else bf16) for k in range(gy // 2)], name + "_sum_core")


def sum_plane(parts, gx, name):
    shape = parts[0].shape[1:]
    return add(parts, [sds(shape, f32 if k == 0 else bf16) for k in range(gx)], name + "_sum_plane")


def sum_line(parts, name):
    return add(parts, [sds(parts[0].shape, f32)], name + "_sum_line")[0]


def local(gx, gy, tokens, bucket, counts, mod_weights, mlp_weights, small_params, cotangent):
    ndev = gx * gy
    gxi, gyi = lax.axis_index("gx"), lax.axis_index("gy")
    device = gxi * gy + gyi
    pos = jnp.stack([gxi, gyi]).astype(jnp.int32)
    mod_len, small_len, mlp_len = mod_weights.shape[0], small_params.shape[0], mlp_weights.shape[0]
    mr, sr = block_rows(mod_len), block_rows(small_len)

    blocks = [place(mod_weights, device), place(small_params, device)]
    pad = -(mr + sr) % 16
    if pad:
        blocks.append(jnp.zeros((pad, 128), bf16))
    line = around(jnp.concatenate(blocks, 0), gy, gx, ndev)
    native = (1, 2, 0, 3)
    xrow, up, n1, nb, r1 = prep(jnp.transpose(tokens, native), counts, jnp.transpose(cotangent, native))
    line, mlp_mine, (xrow, up, n1, nb, r1) = after((line, place(mlp_weights, device), (xrow, up, n1, nb, r1)))
    plane = jnp.stack(around(jnp.stack(line), 2, gy // 2, ndev))
    mlp_line = jnp.stack(around(mlp_mine, gy, gx, ndev))
    plane, mlp_line = after((plane, mlp_line))
    other = swap(plane, 1, ndev)
    mlp_both = jnp.stack([mlp_line, swap(mlp_line, 1, ndev)])
    other, mlp_both = after((other, mlp_both))
    mlp_blocks = around(mlp_both, 2, gy // 2, ndev)

    wf, wh, wp, vec, bm1, kcat = unpack_mod(gx, gy, pos, plane, other, mod_len, small_len)
    q, gates, mixed, z, g, spec, mean, h = forward(n1, bucket, wf, vec, kcat)
    mlp_blocks, mixed = after((mlp_blocks, mixed))
    w1, w2 = unpack_mlp(gx, gy, pos, mlp_blocks, mlp_len)
    dmid, out_rows, dq, dmix, gw1, gw2, gwh, gwp, sums, bsum = middle(xrow, up, mixed, q, wh, wp, w1, w2, vec, bm1)
    own, oth = pack_mlp(gx, gy, pos, gw1, gw2, mlp_len)
    parts = sum_core(own, oth, gx, gy, "mlp")
    parts, dmix = after((parts, dmix))
    mlp_plane = travel(parts, 2, ndev)
    dmer, gwf, fsum, gb, dk = backward(bucket, nb, dq, dmix, gates, z, g, spec, mean, h, wf, vec, sums)
    mlp_plane, gwf = after((mlp_plane, gwf))
    parts = sum_plane(mlp_plane, gx, "mlp")
    own, oth = pack_mod(gx, gy, pos, (gwf, gwh, gwp, sums, bsum, fsum, gb, dk), mod_len, small_len)
    own, oth, parts = after((own, oth, parts))
    mod_parts = sum_core(own, oth, gx, gy, "mod")
    mlp_line = travel(parts, gy, ndev)
    mod_plane = travel(mod_parts, 2, ndev)
    gtok, out = tail((GH, GW) + tokens.shape[:1] + (C,), counts, dmer, wf, n1, r1, dmid, out_rows, vec)
    mod_plane, mlp_line, gtok, out = after((mod_plane, mlp_line, gtok, out))
    mod_line = travel(sum_plane(mod_plane, gx, "mod"), gy, ndev)
    grad_mlp = take(sum_line(mlp_line, "mlp"), mlp_len, device)
    total = sum_line(mod_line, "mod")
    back = (2, 0, 1, 3)
    grad_mod = take(total[:mr], mod_len, device)
    grad_small = take(total[mr : mr + sr], small_len, device)
    return jnp.transpose(out, back), jnp.transpose(gtok, back), grad_mod, grad_mlp, grad_small


def solution(mesh):
    images = P(AXES, None, None, None)
    flat = P(AXES)
    return jax.shard_map(
        functools.partial(local, mesh.shape["gx"], mesh.shape["gy"]),
        mesh=mesh,
        in_specs=(images, flat, flat, flat, flat, flat, images),
        out_specs=(images, images, flat, flat, flat),
        check_vma=False,
    )
```

```python
import functools

import jax
import jax.numpy as jnp
import numpy as np
from jax import lax
from jax.experimental import pallas as pl
from jax.experimental.pallas import tpu as pltpu
from jax.sharding import PartitionSpec as P

C = 384
HID = 1536
GH = 14
GW = 20
HALF = 144
IMG = 2 * HALF
PAIR = 2 * IMG
C2 = 2 * C
NY = 17
NX = 23
NV = 12
NU = 8
Q = NU * NV
AR = 2 * (Q + 16)
BR = 2 * Q
SR = 4 * Q + 32
LEVELS = (3, 5, 7)
TAPS = 64
GATES = 128
MERGED = C2 + GATES
BROWS = 768
HCHUNK = 512
AXES = ("gx", "gy")
f32 = jnp.float32
bf16 = jnp.bfloat16
EPS = 1e-05
ROOT_HALF = 0.7071067811865476
INV_ROOT_2PI = 0.3989422804014327


def _hi(a):
    return a.astype(bf16)


def _lo(a):
    return (a - a.astype(bf16).astype(np.float64)).astype(bf16)


@functools.lru_cache(maxsize=None)
def constants():
    row = np.arange(HALF)
    real = (row < 7 * GW).astype(np.float64)
    yy = np.minimum(row // GW, 6) - (GH - 1) / 2
    xx = row % GW - (GW - 1) / 2
    uv = [(u, v) for u in range(1, NU + 1) for v in range(NV)]
    u0 = [(0, v) for v in range(NV)]
    wu = 2 * np.pi / NY
    wv = 2 * np.pi / NX

    def trig(pairs, pad):
        u = np.array([p[0] for p in pairs] + [0] * pad, np.float64)[:, None]
        v = np.array([p[1] for p in pairs] + [0] * pad, np.float64)[:, None]
        use = np.array([1.0] * len(pairs) + [0.0] * pad)[:, None] * real[None]
        cy, sy = np.cos(wu * u * yy) * use, np.sin(wu * u * yy) * use
        cx, sx = np.cos(wv * v * xx), np.sin(wv * v * xx)
        weight = np.where(u > 0, 2.0, 1.0) * np.where(v > 0, 2.0, 1.0) / (NY * NX)
        return cy * cx, -cy * sx, sy * cx, -sy * sx, weight

    e_re, e_im, o_re, o_im, w1 = trig(uv, 0)
    z_re, z_im, _, _, w0 = trig(u0, 16 - NV)
    fe = np.concatenate([e_re, z_re, e_im, z_im], 0)
    fo = np.concatenate([o_re, o_im], 0)
    half = np.concatenate([0.5 * w1, w0, 0.5 * w1, w0], 0)
    ge = (fe * half).T
    go = (fo * np.concatenate([0.5 * w1, 0.5 * w1], 0)).T

    u = np.array([p[0] for p in uv], np.float64)[:, None]
    v = np.array([p[1] for p in uv], np.float64)[:, None]
    v0 = np.array(list(range(NV)) + [0] * (16 - NV), np.float64)[:, None]
    use0 = np.array([1.0] * NV + [0.0] * (16 - NV))[:, None]
    wp = np.where(v > 0, 2.0, 1.0) / (NY * NX)
    wz = np.where(v0 > 0, 2.0, 1.0) * use0 / (NY * NX)
    weights = np.concatenate([wp, -wp, wp, -wp, wz, -wz], 0)
    es = []
    for k in LEVELS:
        h = k // 2
        ty, tx = np.meshgrid(np.arange(k) - h, np.arange(k) - h, indexing="ij")
        for bucket in (0, 1):
            sy, sx = (ty, tx) if bucket == 0 else (tx, ty)
            py = sy.reshape(1, -1) * wu
            px = sx.reshape(1, -1) * wv
            plus = u * py + v * px
            minus = -u * py + v * px
            zero = v0 * px
            e = [np.cos(plus), np.sin(plus), np.cos(minus), np.sin(minus), np.cos(zero) * use0, np.sin(zero) * use0]
            whole_e = np.zeros((SR, TAPS))
            whole_e[:, : k * k] = np.concatenate(e, 0)
            es.append(np.concatenate([_hi(whole_e), _lo(whole_e)], 1))
    return dict(
        fe=np.concatenate([_hi(fe), _lo(fe), _hi(fe)], 1),
        fo=np.concatenate([_hi(fo), _lo(fo), _hi(fo)], 1),
        ge=np.concatenate([_hi(ge), _lo(ge), _hi(ge)], 1),
        go=np.concatenate([_hi(go), _lo(go), _hi(go)], 1),
        es=np.stack(es),
        weights=np.broadcast_to(weights, (SR, 128)).astype(np.float32),
    )


def dot(a, b):
    return jnp.dot(a, b, preferred_element_type=f32)


def dot_nt(a, b):
    return lax.dot_general(a, b, (((1,), (1,)), ((), ())), preferred_element_type=f32)


def dot_tn(a, b):
    return lax.dot_general(a, b, (((0,), (0,)), ((), ())), preferred_element_type=f32)


def gelu_pair(x):
    cdf = 0.5 * lax.erf(x * ROOT_HALF) + 0.5
    return x * cdf, cdf + x * (jnp.exp(x * x * -0.5) * INV_ROOT_2PI)


def split(x):
    hi = x.astype(bf16)
    return hi, (x - hi.astype(f32)).astype(bf16)


def at(base, i, n=16):
    return slice(base + i * n, base + i * n + n)


def norm_stats(x):
    mean = jnp.mean(x, axis=-1, keepdims=True)
    centred = x - mean
    var = jnp.mean(centred * centred, axis=-1, keepdims=True)
    r = lax.rsqrt(var + EPS)
    return centred * r, r


def sum8(x):
    total = x[0:8]
    for k in range(1, x.shape[0] // 8):
        total = total + x[8 * k : 8 * k + 8]
    return total


def grid_rows(im, y):
    return im * IMG + (y * GW if y < 7 else HALF + (GH - 1 - y) * GW)


def lanes(im):
    return slice(im * C, im * C + C)


(V_G1, V_B1, V_BQ, V_BC, V_HB, V_PB, V_S1, V_G2, V_B2, V_BM2, V_S2, V_BG) = range(12)
VROWS = 16
(S_HB, S_PB, S_S1, S_G2, S_B2, S_BM2, S_S2, S_BQ) = range(8)


def from_native(src, native):
    slots = src.shape[2]
    line = GW * slots
    for y in range(GH):
        for lt in range(C // 128):
            ls = slice(128 * lt, 128 * lt + 128)
            native[lt, line * y : line * (y + 1), :] = src[y, :, :, ls].astype(f32).reshape(line, 128)


def image_rows(native, image, slot, slots, gain):
    for h in (GH // 2 * GW, HALF + GH // 2 * GW):
        image[h : h + 4, :] = jnp.zeros((4, C), f32)
    for y in range(GH):
        a = grid_rows(0, y)
        for lt in range(C // 128):
            v = native[lt, pl.ds(GW * slots * y + slot, GW, stride=slots), :]
            image[a : a + GW, 128 * lt : 128 * lt + 128] = v if gain is None else v * gain


def kernel_prep(x_ref, xrow_o, nb_o, stat_o, native, image):
    slot = pl.program_id(0)

    @pl.when(slot == 0)
    def _():
        from_native(x_ref, native)

    image_rows(native, image, slot, x_ref.shape[2], None)
    lane = lax.broadcasted_iota(jnp.int32, (32, 128), 1)
    for i in range(IMG // 32):
        s = at(0, i, 32)
        x = image[s, :]
        xrow_o[s, :] = x.astype(bf16)
        mean = jnp.mean(x, axis=-1, keepdims=True)
        centred = x - mean
        r = lax.rsqrt(jnp.mean(centred * centred, axis=-1, keepdims=True) + EPS)
        nb_o[s, :] = (centred * r).astype(bf16)
        stat_o[s, :] = jnp.where(lane == 0, mean, r)


def kernel_upstream(counts, cot_ref, up_o, native, image):
    slot = pl.program_id(0)

    @pl.when(slot == 0)
    def _():
        from_native(cot_ref, native)

    image_rows(native, image, slot, cot_ref.shape[2], (slot < counts[0]).astype(f32))
    for i in range(IMG // 32):
        s = at(0, i, 32)
        up_o[s, :] = image[s, :].astype(bf16)


CHAINS = 3
CHAIN = C2 // CHAINS


def staggered(phases):
    lists = [phases(t) for t in range(CHAINS)]
    for turn in range(len(lists[0]) + CHAINS - 1):
        for t in range(CHAINS):
            if 0 <= turn - t < len(lists[t]):
                lists[t][turn - t]()


def sub_tiles(t):
    for k in range(t * CHAIN // 128, (t + 1) * CHAIN // 128):
        lt = k % (C // 128)
        yield k // (C // 128), slice(128 * k, 128 * k + 128), slice(128 * lt, 128 * lt + 128)


def spread_gates(gates, wide):
    for k in range(4):
        for i in range(PAIR // 32):
            s = at(0, i, 32)
            wide[k, s, :] = jnp.broadcast_to(gates[s, k : k + 1], (32, 128))


def kernel_forward(
    bucket, x_ref, stat, wf, vec, kcat, es, fe, fo, ge, go,
    q_o, gates_o, mixed_o, z_o, g_o, spec_o, mean_o,
    h_o, normed, ctx, ecat, ocat, s_a, s_b, s_e, s_o, yca, ycb, mix, wide,
):
    step = pl.program_id(0)

    @pl.when(step == 0)
    def _():
        for lb in range(6):
            h_o[lb] = dot(es[lb], kcat[lb // 2])

    g1, b1 = vec[V_G1 : V_G1 + 1, :], vec[V_B1 : V_B1 + 1, :]
    for i in range(PAIR // 32):
        s = at(0, i, 32)
        n = (x_ref[s, :].astype(f32) - stat[s, 0:1]) * stat[s, 1:2]
        normed[s, :] = (n * g1 + b1).astype(bf16)
    right = dot(normed[...], wf[:, C + 128 :])
    left = dot(normed[...], wf[:, : C + 128])
    ctx[:, :128] = left[:, C:] + vec[V_BC : V_BC + 1, :128]
    ctx[:, 128:] = right[:, : C - 128] + vec[V_BC : V_BC + 1, 128:]
    gates_o[...] = right[:, C - 128 :] + vec[V_BG : V_BG + 1, :GATES]
    q_o[...] = left[:, :C] + vec[V_BQ : V_BQ + 1, :]
    spread_gates(gates_o, wide)
    lbs = [[level * 2 + bucket[step * 2 + im] for im in range(2)] for level in range(3)]

    def put_pair(ls, i, top, bot):
        e_hi, e_lo = split(top + bot)
        o_hi, o_lo = split(top - bot)
        for base, ev, ov in ((0, e_hi, o_hi), (HALF, e_hi, o_hi), (2 * HALF, e_lo, o_lo)):
            ecat[at(base, i), ls] = ev
            ocat[at(base, i), ls] = ov

    def first(t):
        for im, ls, hs in sub_tiles(t):
            for i in range(HALF // 16):
                put_pair(ls, i, ctx[at(im * IMG, i), hs], ctx[at(im * IMG + HALF, i), hs])

    def transform(t):
        ts = slice(t * CHAIN, (t + 1) * CHAIN)
        s_a[:, ts] = dot(fe[...], ecat[:, ts])
        s_b[:, ts] = dot(fo[...], ocat[:, ts])

    def back(t):
        ts = slice(t * CHAIN, (t + 1) * CHAIN)
        s_e[:, ts] = dot(ge[...], yca[:, ts])
        s_o[:, ts] = dot(go[...], ycb[:, ts])

    def filt(t, level):
        base = level * SR
        for im, ls, hs in sub_tiles(t):
            lb = lbs[level][im]
            for i in range(Q // 16):
                a_re, a_im = s_a[at(0, i), ls], s_a[at(Q + 16, i), ls]
                b_re, b_im = s_b[at(0, i), ls], s_b[at(Q, i), ls]
                xp_re, xp_im = a_re + b_im, a_im - b_re
                xm_re, xm_im = a_re - b_im, a_im + b_re
                spec_o[at(base, i), ls] = xp_re.astype(bf16)
                spec_o[at(base + Q, i), ls] = xp_im.astype(bf16)
                spec_o[at(base + 2 * Q, i), ls] = xm_re.astype(bf16)
                spec_o[at(base + 3 * Q, i), ls] = xm_im.astype(bf16)
                p_re, p_im = h_o[lb, at(0, i), hs], h_o[lb, at(Q, i), hs]
                q_re, q_im = h_o[lb, at(2 * Q, i), hs], h_o[lb, at(3 * Q, i), hs]
                yp_re, yp_im = p_re * xp_re - p_im * xp_im, p_re * xp_im + p_im * xp_re
                ym_re, ym_im = q_re * xm_re - q_im * xm_im, q_re * xm_im + q_im * xm_re
                for dst, off, width, val in (
                    (yca, 0, AR, yp_re + ym_re),
                    (yca, Q + 16, AR, yp_im + ym_im),
                    (ycb, 0, BR, ym_im - yp_im),
                    (ycb, Q, BR, yp_re - ym_re),
                ):
                    hi, lo = split(val)
                    dst[at(off, i), ls] = hi
                    dst[at(off + width, i), ls] = hi
                    dst[at(off + 2 * width, i), ls] = lo
            x_re, x_im = s_a[Q : Q + 16, ls], s_a[2 * Q + 16 : 2 * Q + 32, ls]
            spec_o[base + 4 * Q : base + 4 * Q + 16, ls] = x_re.astype(bf16)
            spec_o[base + 4 * Q + 16 : base + 4 * Q + 32, ls] = x_im.astype(bf16)
            p_re, p_im = h_o[lb, 4 * Q : 4 * Q + 16, hs], h_o[lb, 4 * Q + 16 : 4 * Q + 32, hs]
            for off, val in ((Q, p_re * x_re - p_im * x_im), (2 * Q + 16, p_re * x_im + p_im * x_re)):
                hi, lo = split(val)
                yca[off : off + 16, ls] = hi
                yca[off + AR : off + AR + 16, ls] = hi
                yca[off + 2 * AR : off + 2 * AR + 16, ls] = lo

    def act(t, level):
        for im, ls, hs in sub_tiles(t):
            total = jnp.zeros((8, 128), f32)
            for i in range(HALF // 16):
                even, odd = s_e[at(0, i), ls], s_o[at(0, i), ls]
                both = []
                for h, a in ((0, even + odd), (HALF, even - odd)):
                    z, g = gelu_pair(a)
                    z_o[at(level * IMG + h, i), ls] = z.astype(bf16)
                    g_o[at(level * IMG + h, i), ls] = g.astype(bf16)
                    s = at(im * IMG + h, i)
                    part = z * wide[level, s, :]
                    mix[s, hs] = part if level == 0 else mix[s, hs] + part
                    both.append(z)
                if level < 2:
                    put_pair(ls, i, both[0], both[1])
                else:
                    total = total + sum8(both[0]) + sum8(both[1])
            if level == 2:
                mean = jnp.sum(total, axis=0, keepdims=True) * (1.0 / (GH * GW))
                mean_o[:, ls] = jnp.broadcast_to(mean, (8, 128))
                glob, _ = gelu_pair(mean)
                for i in range(IMG // 16):
                    s = at(im * IMG, i)
                    mixed_o[s, hs] = (mix[s, hs] + wide[3, s, :] * glob).astype(bf16)

    def phases(t):
        steps = [lambda: first(t)]
        for level in range(3):
            steps += [
                lambda: transform(t),
                lambda level=level: filt(t, level),
                lambda: back(t),
                lambda level=level: act(t, level),
            ]
        return steps

    staggered(phases)


def kernel_middle(
    gx, gy, mlp_len, pos, x_ref, up, mixed, q_ref, wh, wp, w1, w2, vec, bm1,
    dmid_o, out_o, dq_o, dmix_o, own, oth, gwh, gwp, sums, bsum,
    mod, modulated, branch, mid, second, dshr, shr, dsec, act, dexp, hid, vacc, bacc, gw1, gw2, flat,
):
    step = pl.program_id(0)

    @pl.when(step == 0)
    def _():
        for ref in (gw1, gw2, gwh, gwp, vacc, bacc):
            ref[...] = jnp.zeros_like(ref)

    g2, b2 = vec[V_G2 : V_G2 + 1, :], vec[V_B2 : V_B2 + 1, :]
    s1, s2 = vec[V_S1 : V_S1 + 1, :], vec[V_S2 : V_S2 + 1, :]
    bm2 = vec[V_BM2 : V_BM2 + 1, :]
    zero = jnp.zeros((8, C), f32)

    mod[...] = dot(mixed[...], wh[...]) + vec[V_HB : V_HB + 1, :]
    for i in range(BROWS // 32):
        s = at(0, i, 32)
        modulated[s, :] = (q_ref[s, :] * mod[s, :]).astype(bf16)
        dshr[s, :] = (up[s, :].astype(f32) * s2).astype(bf16)
    branch[...] = dot(modulated[...], wp[...]) + vec[V_PB : V_PB + 1, :]
    for i in range(BROWS // 32):
        s = at(0, i, 32)
        middle = x_ref[s, :].astype(f32) + s1 * branch[s, :]
        mid[s, :] = middle
        n, _ = norm_stats(middle)
        second[s, :] = (n * g2 + b2).astype(bf16)

    for h in range(HID // HCHUNK):
        hs = slice(h * HCHUNK, (h + 1) * HCHUNK)
        hid[...] = dot(second[...], w1[:, hs]) + bm1[0:1, hs]
        dact = dot_nt(dshr[...], w2[hs, :])
        total = jnp.zeros((8, HCHUNK), f32)
        for i in range(BROWS // 16):
            s = at(0, i)
            z, g = gelu_pair(hid[s, :])
            act[s, :] = z.astype(bf16)
            d = dact[s, :] * g
            dexp[s, :] = d.astype(bf16)
            total = total + sum8(d)
        bacc[:, hs] += total
        part = dot(act[...], w2[hs, :])
        back = dot_nt(dexp[...], w1[:, hs])
        if h == 0:
            shr[...] = part
            dsec[...] = back
        else:
            shr[...] += part
            dsec[...] += back
        gw1[:, hs] += dot_tn(second[...], dexp[...])
        gw2[hs, :] += dot_tn(act[...], dshr[...])

    t_s1 = t_g2 = t_b2 = t_bm2 = t_s2 = t_pb = t_hb = t_bq = zero
    dbr = second
    for i in range(BROWS // 32):
        s = at(0, i, 32)
        middle = mid[s, :]
        u = up[s, :].astype(f32)
        shrunk = shr[s, :] + bm2
        out_o[s, :] = middle + s2 * shrunk
        n, r = norm_stats(middle)
        d = dsec[s, :]
        e = d * g2
        dn = d * n
        dv = r * (e - jnp.mean(e, axis=-1, keepdims=True) - n * jnp.mean(e * n, axis=-1, keepdims=True))
        dm = u + dv
        dmid_o[s, :] = dm
        db = s1 * dm
        dbr[s, :] = db.astype(bf16)
        t_s1 = t_s1 + sum8(dm * branch[s, :])
        t_g2 = t_g2 + sum8(dn)
        t_b2 = t_b2 + sum8(d)
        t_bm2 = t_bm2 + sum8(dshr[s, :].astype(f32))
        t_s2 = t_s2 + sum8(u * shrunk)
        t_pb = t_pb + sum8(db)

    gwp[...] += dot_tn(modulated[...], dbr[...])
    dmod = dot_nt(dbr[...], wp[...])
    dm2 = dshr
    for i in range(BROWS // 32):
        s = at(0, i, 32)
        dm = dmod[s, :]
        dq = dm * mod[s, :]
        dd = dm * q_ref[s, :]
        dq_o[s, :] = dq.astype(bf16)
        dm2[s, :] = dd.astype(bf16)
        t_bq = t_bq + sum8(dq)
        t_hb = t_hb + sum8(dd)
    gwh[...] += dot_tn(mixed[...], dm2[...])
    dmix_o[...] = dot_nt(dm2[...], wh[...])

    for k, t in ((S_HB, t_hb), (S_PB, t_pb), (S_S1, t_s1), (S_G2, t_g2), (S_B2, t_b2), (S_BM2, t_bm2), (S_S2, t_s2), (S_BQ, t_bq)):
        vacc[k] += t

    @pl.when(step == pl.num_programs(0) - 1)
    def _():
        for k in range(8):
            sums[k : k + 1, :] = jnp.sum(vacc[k], axis=0, keepdims=True)
        bsum[...] = jnp.broadcast_to(jnp.sum(bacc[...], axis=0, keepdims=True), bsum.shape)
        pack_mlp(gx, gy, mlp_len, pos, gw1, gw2, own, oth, flat)


def kernel_backward(
    gx, gy, mod_len, small_len,
    bucket, pos, nb_ref, dq_ref, dmix, gates, z_ref, g_ref, spec, mean_ref, kcat, wf, vec, sums, bsum, gwh, gwp, es, weights,
    fe, fo, ge, go,
    dmer, own, oth,
    gwf, fsum, gb, dk, h_ref, ecat, ocat, s_a, s_b, s_e, s_o, yca, ycb, acc, facc, wide, flat, small, moved, spread,
):
    step = pl.program_id(0)
    last = pl.num_programs(0) - 1

    @pl.when(step == 0)
    def _():
        for ref in (gwf, facc, acc):
            ref[...] = jnp.zeros_like(ref)
        for lb in range(6):
            h_ref[lb] = dot(es[lb], kcat[lb // 2])

    spread_gates(gates, wide)
    lbs = [[level * 2 + bucket[step * 2 + im] for im in range(2)] for level in range(3)]
    globs = [gelu_pair(mean_ref[0:1, lanes(im)]) for im in range(2)]
    lane = lax.broadcasted_iota(jnp.int32, (16, GATES), 1)
    dmeans = {}

    def mean_grad(t):
        for im, ls, hs in sub_tiles(t):
            total = jnp.zeros((8, 128), f32)
            for i in range(IMG // 16):
                s = at(im * IMG, i)
                total = total + sum8(dmix[s, hs] * wide[3, s, :])
            dmeans[ls.start] = jnp.sum(total, axis=0, keepdims=True) * globs[im][1][:, hs] * (1.0 / (GH * GW))

    def gate_grad(part):
        t_g = jnp.zeros((8, GATES), f32)
        n = 2 * (HALF // 16) // CHAINS
        for im, i in [(im, i) for im in range(2) for i in range(HALF // 16)][part * n : part * n + n]:
            for h in (0, HALF):
                s = at(im * IMG + h, i)
                dm = dmix[s, :]
                dg = jnp.zeros((16, GATES), f32)
                for k in range(4):
                    other = z_ref[at(k * IMG + h, i), lanes(im)].astype(f32) if k < 3 else globs[im][0]
                    col = jnp.sum(dm * other, axis=-1, keepdims=True)
                    dg = jnp.where(lane == k, col, dg)
                dmer[s, :C] = dq_ref[s, :]
                dmer[s, C2:] = dg.astype(bf16)
                t_g = t_g + sum8(dg)
        facc[:, C2:] += t_g

    def before(t, level):
        for im, ls, hs in sub_tiles(t):
            for i in range(HALF // 16):
                if level < 2:
                    even, odd = s_e[at(0, i), ls], s_o[at(0, i), ls]
                    through = (even + odd, even - odd)
                else:
                    through = (dmeans[ls.start], dmeans[ls.start])
                parts = []
                for k, h in enumerate((0, HALF)):
                    s = at(im * IMG + h, i)
                    dz = wide[level, s, :] * dmix[s, hs] + through[k]
                    parts.append(dz * g_ref[at(level * IMG + h, i), ls].astype(f32))
                ecat[at(0, i), ls] = (parts[0] + parts[1]).astype(bf16)
                ocat[at(0, i), ls] = (parts[0] - parts[1]).astype(bf16)

    def transform(t):
        ts = slice(t * CHAIN, (t + 1) * CHAIN)
        s_a[:, ts] = dot(fe[...], ecat[:, ts])
        s_b[:, ts] = dot(fo[...], ocat[:, ts])

    def back(t):
        ts = slice(t * CHAIN, (t + 1) * CHAIN)
        s_e[:, ts] = dot(ge[...], yca[:, ts])
        s_o[:, ts] = dot(go[...], ycb[:, ts])

    def filt(t, level):
        base = level * SR
        for im, ls, hs in sub_tiles(t):
            lb = lbs[level][im]
            for i in range(Q // 16):
                a_re, a_im = s_a[at(0, i), ls], s_a[at(Q + 16, i), ls]
                b_re, b_im = s_b[at(0, i), ls], s_b[at(Q, i), ls]
                dp_re, dp_im = a_re + b_im, a_im - b_re
                dm_re, dm_im = a_re - b_im, a_im + b_re
                xp_re, xp_im = spec[at(base, i), ls].astype(f32), spec[at(base + Q, i), ls].astype(f32)
                xm_re, xm_im = spec[at(base + 2 * Q, i), ls].astype(f32), spec[at(base + 3 * Q, i), ls].astype(f32)
                acc[lb, at(0, i), hs] += xp_re * dp_re + xp_im * dp_im
                acc[lb, at(Q, i), hs] += xp_im * dp_re - xp_re * dp_im
                acc[lb, at(2 * Q, i), hs] += xm_re * dm_re + xm_im * dm_im
                acc[lb, at(3 * Q, i), hs] += xm_im * dm_re - xm_re * dm_im
                p_re, p_im = h_ref[lb, at(0, i), hs], h_ref[lb, at(Q, i), hs]
                q_re, q_im = h_ref[lb, at(2 * Q, i), hs], h_ref[lb, at(3 * Q, i), hs]
                yp_re, yp_im = p_re * dp_re + p_im * dp_im, p_re * dp_im - p_im * dp_re
                ym_re, ym_im = q_re * dm_re + q_im * dm_im, q_re * dm_im - q_im * dm_re
                yca[at(0, i), ls] = (yp_re + ym_re).astype(bf16)
                yca[at(Q + 16, i), ls] = (yp_im + ym_im).astype(bf16)
                ycb[at(0, i), ls] = (ym_im - yp_im).astype(bf16)
                ycb[at(Q, i), ls] = (yp_re - ym_re).astype(bf16)
            d_re, d_im = s_a[Q : Q + 16, ls], s_a[2 * Q + 16 : 2 * Q + 32, ls]
            x_re = spec[base + 4 * Q : base + 4 * Q + 16, ls].astype(f32)
            x_im = spec[base + 4 * Q + 16 : base + 4 * Q + 32, ls].astype(f32)
            acc[lb, 4 * Q : 4 * Q + 16, hs] += x_re * d_re + x_im * d_im
            acc[lb, 4 * Q + 16 : 4 * Q + 32, hs] += x_im * d_re - x_re * d_im
            p_re, p_im = h_ref[lb, 4 * Q : 4 * Q + 16, hs], h_ref[lb, 4 * Q + 16 : 4 * Q + 32, hs]
            yca[Q : Q + 16, ls] = (p_re * d_re + p_im * d_im).astype(bf16)
            yca[2 * Q + 16 : 2 * Q + 32, ls] = (p_re * d_im - p_im * d_re).astype(bf16)

    def context(t):
        for im, ls, hs in sub_tiles(t):
            ds = slice(C + hs.start, C + hs.stop)
            total = jnp.zeros((8, 128), f32)
            for i in range(HALF // 16):
                even, odd = s_e[at(0, i), ls], s_o[at(0, i), ls]
                top, bot = even + odd, even - odd
                dmer[at(im * IMG, i), ds] = top.astype(bf16)
                dmer[at(im * IMG + HALF, i), ds] = bot.astype(bf16)
                total = total + sum8(top) + sum8(bot)
            facc[:, ds] += total

    def phases(t):
        steps = [lambda: mean_grad(t)]
        for level in (2, 1, 0):
            steps += [
                lambda level=level: before(t, level),
                lambda: transform(t),
                lambda level=level: filt(t, level),
                lambda: back(t),
            ]
            if level == 2:
                steps.append(lambda: gate_grad(t))
        return steps + [lambda: context(t)]

    staggered(phases)
    gwf[...] += dot_tn(nb_ref[...], dmer[...])

    @pl.when(step == last)
    def _():
        facc[:, :C] = jnp.broadcast_to(sums[S_BQ : S_BQ + 1, :] * 0.125, (8, C))
        colsum = jnp.sum(facc[...], axis=0, keepdims=True)
        fsum[...] = jnp.broadcast_to(colsum, fsum.shape)
        wide = wf[...].astype(f32)
        t_hi, t_lo = split(wide * gwf[...])
        ones = jnp.ones((8, MERGED), bf16)
        gb[0:8, :] = dot_nt(ones, t_hi) + dot_nt(ones, t_lo)
        c_hi, c_lo = split(fsum[...])
        gb[8:16, :] = dot_nt(c_hi, wf[...]) + dot_nt(c_lo, wf[...])
        g1 = jnp.transpose(jnp.broadcast_to(vec[V_G1 : V_G1 + 1, :], (128, C)))
        b1 = jnp.transpose(jnp.broadcast_to(vec[V_B1 : V_B1 + 1, :], (128, C)))
        for t in range(MERGED // 128):
            ls = slice(128 * t, 128 * t + 128)
            gwf[:, ls] = gwf[:, ls] * g1 + b1 * fsum[0:1, ls]
        for level in range(3):
            total = None
            for lb in (level * 2, level * 2 + 1):
                hi, lo = split(acc[lb] * jnp.concatenate([weights[...]] * (C // 128), 1))
                first = dot_tn(es[lb], hi)
                term = first[:TAPS] + first[TAPS:] + dot_tn(es[lb][:, :TAPS], lo)
                total = term if total is None else total + term
            dk[level] = total
        pack_mod(gx, gy, mod_len, small_len, pos, gwf, gwh, gwp, sums, bsum, fsum, gb, dk, own, oth, flat, small, moved, spread)


def to_native(rows_ref, first, native, slot, slots, gain):
    line = GW * slots
    for y in range(GH):
        a = first + grid_rows(0, y)
        for lt in range(C // 128):
            v = rows_ref[a : a + GW, 128 * lt : 128 * lt + 128]
            native[lt, pl.ds(line * y + slot, GW, stride=slots), :] = v if gain is None else v * gain


def write_native(native, out, slots):
    line = GW * slots
    for y in range(GH):
        for lt in range(C // 128):
            v = native[lt, line * y : line * (y + 1), :].reshape(GW, slots, 128)
            out[y, :, :, 128 * lt : 128 * lt + 128] = v.astype(out.dtype)


def kernel_tail(dmer, wf, x_ref, stat, dmid, vec, gtok_o, stage, native):
    step = pl.program_id(0)
    slots = gtok_o.shape[2]
    g1 = vec[V_G1 : V_G1 + 1, :]
    d_normed = dot_nt(dmer[...], wf[...])
    for i in range(PAIR // 32):
        s = at(0, i, 32)
        r = stat[s, 1:2]
        n = (x_ref[s, :].astype(f32) - stat[s, 0:1]) * r
        e = d_normed[s, :] * g1
        dv = e - jnp.mean(e, axis=-1, keepdims=True) - n * jnp.mean(e * n, axis=-1, keepdims=True)
        stage[s, :] = dmid[s, :] + r * dv
    for im in range(2):
        to_native(stage, im * IMG, native, step * 2 + im, slots, None)

    @pl.when(step == pl.num_programs(0) - 1)
    def _():
        write_native(native, gtok_o, slots)


def kernel_out(counts, rows_ref, out_o, native):
    slots = out_o.shape[2]
    for im in range(slots):
        to_native(rows_ref, im * IMG, native, im, slots, (im < counts[0]).astype(f32))
    write_native(native, out_o, slots)


def block_rows(length):
    return 8 * (length // 1024 if length % 1024 == 0 else (length + 1022) // 1024 + 1)


def place(shard, device):
    length = shard.shape[0]
    n = block_rows(length) * 128
    if n == length:
        return shard.reshape(-1, 128)
    offset = lax.rem(device * length, 1024)
    return lax.dynamic_update_slice(jnp.zeros((n,), shard.dtype), shard, (offset,)).reshape(-1, 128)


def take(block, length, device):
    flat = block.reshape(-1)
    if flat.shape[0] == length:
        return flat
    return lax.dynamic_slice(flat, (lax.rem(device * length, 1024),), (length,))


def first_row(length, device):
    return pl.multiple_of((device * length) // 1024 * 8, 8)


def device_at(pos, gy, i, j, c):
    return (pos[0] ^ j) * gy + (pos[1] ^ (2 * i + c))


def shift_left(first, second, sh):
    if sh == 0:
        return first
    lane = lax.broadcasted_iota(jnp.int32, first.shape, 1)
    return jnp.where(lane < 128 - sh, pltpu.roll(first, 128 - sh, 1), pltpu.roll(second, 128 - sh, 1))


def shift_right(first, second, sh):
    lane = lax.broadcasted_iota(jnp.int32, first.shape, 1)
    return jnp.where(lane < sh, pltpu.roll(first, sh, 1), pltpu.roll(second, sh, 1))


WIDE = C2 + 4
WF_ROWS = C * WIDE // 128
W_ROWS = C * C // 128
PERIOD = 32
STRIDE = PERIOD * WIDE // 128
K_ROW = 12
TAIL_ROW = K_ROW + 83 * C // 128
B_HB, B_PB, B_S1, B_G2, B_B2, B_BM1 = (TAIL_ROW + 3 * k for k in range(6))
B_BM2 = B_BM1 + HID // 128
B_S2 = B_BM2 + 3
END_ROW = B_S2 + 3


def kernel_unpack_mod(gx, gy, mod_len, small_len, pos, own, oth, wf_o, wh_o, wp_o, vec_o, bm1_o, kcat_o, flat, small, moved, wide):
    flat[...] = jnp.zeros_like(flat)
    small[...] = jnp.zeros_like(small)
    mr, sr = block_rows(mod_len), block_rows(small_len)
    for i in range(gy // 2):
        for j in range(gx):
            for c, src in enumerate((own, oth)):
                d = device_at(pos, gy, i, j, c)
                block = src[i, j].astype(f32)
                flat[pl.ds(first_row(mod_len, d), mr), :] += block[:mr]
                small[pl.ds(first_row(small_len, d), sr), :] += block[mr : mr + sr]
    lane = lax.broadcasted_iota(jnp.int32, (16, 128), 1)
    for p in range(PERIOD):
        for j in range(MERGED // 128):
            f = WIDE * p + 128 * j
            row, sh = f // 128, f % 128
            a = flat[pl.ds(row, 16, stride=STRIDE), :]
            b = flat[pl.ds(row + 1, 16, stride=STRIDE), :] if sh else a
            v = shift_left(a, b, sh)
            if j == MERGED // 128 - 1:
                v = jnp.where(lane < 4, v, 0.0)
            wide[j, pl.ds(p, 16, stride=PERIOD), :] = v
    for j in range(MERGED // 128):
        wf_o[:, 128 * j : 128 * j + 128] = wide[j, :C, :].astype(bf16)
    for j in range(3):
        ls = slice(128 * j, 128 * j + 128)
        wh_o[:, ls] = flat[pl.ds(WF_ROWS + j, C, stride=3), :].astype(bf16)
        wp_o[:, ls] = flat[pl.ds(WF_ROWS + W_ROWS + j, C, stride=3), :].astype(bf16)
    n = moved.shape[0]
    moved[...] = shift_left(small[0:n, :], small[1 : n + 1, :], 4)
    vec_o[...] = jnp.zeros_like(vec_o)
    for row, src, start in (
        (V_G1, small, 0), (V_B1, small, 3), (V_BQ, small, 6), (V_BC, small, 9),
        (V_HB, moved, B_HB), (V_PB, moved, B_PB), (V_S1, moved, B_S1), (V_G2, moved, B_G2), (V_B2, moved, B_B2),
        (V_BM2, moved, B_BM2), (V_S2, moved, B_S2),
    ):
        for j in range(3):
            vec_o[row : row + 1, 128 * j : 128 * j + 128] = src[start + j : start + j + 1, :]
    vec_o[V_BG : V_BG + 1, 0:128] = jnp.where(lane[0:1] < 4, small[K_ROW : K_ROW + 1, :], 0.0)
    for t in range(HID // 128):
        bm1_o[:, 128 * t : 128 * t + 128] = jnp.broadcast_to(moved[B_BM1 + t : B_BM1 + t + 1, :], (8, 128))
    start = 0
    for level, k in enumerate(LEVELS):
        for j in range(3):
            taps = moved[pl.ds(K_ROW + 3 * start + j, TAPS, stride=3), :].astype(bf16)
            kcat_o[level, 0:TAPS, 128 * j : 128 * j + 128] = taps
            kcat_o[level, TAPS:, 128 * j : 128 * j + 128] = taps
        start += k * k


def kernel_unpack_mlp(gx, gy, mlp_len, pos, *refs):
    blocks, (w1_o, w2_o, flat) = refs[: gy // 2], refs[gy // 2 :]
    mr = block_rows(mlp_len)
    aligned = mr * 128 == mlp_len
    if not aligned:
        flat[...] = jnp.zeros_like(flat)
    for i, src in enumerate(blocks):
        for j in range(gx):
            for c in range(2):
                rows_at = pl.ds(first_row(mlp_len, device_at(pos, gy, i, j, c)), mr)
                if aligned:
                    flat[rows_at, :] = src[c, j].astype(f32)
                else:
                    flat[rows_at, :] += src[c, j].astype(f32)
    for t in range(HID // 128):
        w1_o[:, 128 * t : 128 * t + 128] = flat[pl.ds(t, C, stride=HID // 128), :].astype(bf16)
    for t in range(C // 128):
        w2_o[:, 128 * t : 128 * t + 128] = flat[pl.ds(C * HID // 128 + t, HID, stride=C // 128), :].astype(bf16)


def send_slots(gx, gy, pos, flat, length, base, own, oth):
    mr = block_rows(length)
    for i in range(gy // 2):
        for j in range(gx):
            for c, dst in enumerate((own, oth)):
                d = device_at(pos, gy, i, j, c)
                dst[i, j, base : base + mr, :] = flat[pl.ds(first_row(length, d), mr), :].astype(bf16)


def pack_mlp(gx, gy, mlp_len, pos, gw1, gw2, own, oth, flat):
    used = 2 * C * HID // 128
    if flat.shape[0] > used:
        flat[used:, :] = jnp.zeros_like(flat[used:, :])
    for t in range(HID // 128):
        flat[pl.ds(t, C, stride=HID // 128), :] = gw1[:, 128 * t : 128 * t + 128]
    for t in range(C // 128):
        flat[pl.ds(C * HID // 128 + t, HID, stride=C // 128), :] = gw2[:, 128 * t : 128 * t + 128]
    send_slots(gx, gy, pos, flat, mlp_len, 0, own, oth)


def pack_mod(gx, gy, mod_len, small_len, pos, gwf, gwh, gwp, sums, bsum, fsum, gb, dk, own, oth, flat, small, moved, wide):
    lane = lax.broadcasted_iota(jnp.int32, (16, 128), 1)
    used = WF_ROWS + 2 * W_ROWS
    if flat.shape[0] > used:
        flat[used:, :] = jnp.zeros_like(flat[used:, :])
    for j in range(MERGED // 128):
        wide[j, :C, :] = gwf[:, 128 * j : 128 * j + 128]
    for f in range(STRIDE):
        p = 128 * f // WIDE
        col = 128 * f - WIDE * p
        t, sh = col // 128, col % 128

        def piece(row, tile):
            tile = min(tile, MERGED // 128 - 1)
            return wide[tile, pl.ds(row, 16, stride=PERIOD), :]

        v = shift_left(piece(p, t), piece(p, t + 1), sh)
        left = WIDE - col
        if left < 128:
            v = jnp.where(lane < left, v, pltpu.roll(piece(p + 1, 0), left, 1))
        flat[pl.ds(f, 16, stride=STRIDE), :] = v
    for j in range(3):
        ls = slice(128 * j, 128 * j + 128)
        flat[pl.ds(WF_ROWS + j, C, stride=3), :] = gwh[:, ls]
        flat[pl.ds(WF_ROWS + W_ROWS + j, C, stride=3), :] = gwp[:, ls]
    moved[...] = jnp.zeros_like(moved)
    small[...] = jnp.zeros_like(small)
    start = 0
    for level, k in enumerate(LEVELS):
        for j in range(3):
            moved[pl.ds(K_ROW + 3 * start + j, k * k, stride=3), :] = dk[level, 0 : k * k, 128 * j : 128 * j + 128]
        start += k * k
    for start, row in (
        (B_HB, S_HB), (B_PB, S_PB), (B_S1, S_S1), (B_G2, S_G2), (B_B2, S_B2), (B_BM2, S_BM2), (B_S2, S_S2),
    ):
        for j in range(3):
            moved[start + j : start + j + 1, :] = sums[row : row + 1, 128 * j : 128 * j + 128]
    for t in range(HID // 128):
        moved[B_BM1 + t : B_BM1 + t + 1, :] = bsum[0:1, 128 * t : 128 * t + 128]
    n = moved.shape[0]
    small[8:n, :] = shift_right(moved[7 : n - 1, :], moved[8:n, :], 4)
    for j in range(3):
        ls = slice(128 * j, 128 * j + 128)
        small[j : j + 1, :] = gb[0:1, ls]
        small[3 + j : 4 + j, :] = gb[8:9, ls]
        small[6 + j : 7 + j, :] = fsum[0:1, ls]
        small[9 + j : 10 + j, :] = fsum[0:1, C + 128 * j : C + 128 * j + 128]
    gate_lane = lane[0:1] < 4
    small[K_ROW : K_ROW + 1, :] = jnp.where(gate_lane, fsum[0:1, C2:], small[K_ROW : K_ROW + 1, :])
    mr, sr = block_rows(mod_len), block_rows(small_len)
    send_slots(gx, gy, pos, flat, mod_len, 0, own, oth)
    for i in range(gy // 2):
        for j in range(gx):
            for c, dst in enumerate((own, oth)):
                block = small[pl.ds(first_row(small_len, device_at(pos, gy, i, j, c)), sr), :]
                pad = own.shape[2] - mr - sr
                if pad:
                    block = jnp.concatenate([block, jnp.zeros((pad, 128), f32)], 0)
                dst[i, j, mr:, :] = block.astype(bf16)


def kernel_add(n_in, *refs):
    for k, o in enumerate(refs[n_in:]):
        total = None
        for ref in refs[:n_in]:
            v = ref[k].astype(f32)
            total = v if total is None else total + v
        o[...] = total.astype(o.dtype)


def kernel_cut(cuts, *refs):
    outs = refs[-len(cuts) :]
    for o, (first, n) in zip(outs, cuts):
        total = None
        for ref in refs[: -len(cuts)]:
            v = ref[first : first + n, :].astype(f32)
            total = v if total is None else total + v
        o[...] = total


def full(shape):
    return pl.BlockSpec(shape, lambda *i, n=len(shape): (0,) * n)


def rows(n, width):
    return pl.BlockSpec((n, width), lambda i: (i, 0))


def smem():
    return pl.BlockSpec(memory_space=pltpu.SMEM)


def sds(shape, dtype):
    return jax.ShapeDtypeStruct(shape, dtype)


def call(kernel, name, grid, ins, outs, scratch, mib, micros):
    return pl.pallas_call(
        kernel,
        grid=grid,
        in_specs=[s for _, s in ins],
        out_shape=[o for o, _ in outs],
        out_specs=[s for _, s in outs],
        scratch_shapes=[pltpu.VMEM(shape, dtype) for shape, dtype in scratch],
        compiler_params=pltpu.CompilerParams(vmem_limit_bytes=mib * 2**20),
        cost_estimate=pl.CostEstimate(flops=int(micros * 1e9), bytes_accessed=int(micros * 1e6), transcendentals=0),
        name=name,
    )(*[a for a, _ in ins])


def whole(*arrays):
    return [(a, full(a.shape)) for a in arrays]


def by_rows(n, *arrays):
    return [(a, rows(n, a.shape[1])) for a in arrays]


def native_rows(slots):
    return ((C // 128, GH * GW * slots, 128), f32)


def prep(tokens):
    slots = tokens.shape[2]
    n = slots * IMG
    outs = [(sds((n, w), t), rows(IMG, w)) for w, t in ((C, bf16), (C, bf16), (128, f32))]
    return call(kernel_prep, "prep", (slots,), whole(tokens), outs, [native_rows(slots), ((IMG, C), f32)], 60, 6)


def upstream(counts, cotangent):
    slots = cotangent.shape[2]
    ins = [(counts, smem())] + whole(cotangent)
    outs = [(sds((slots * IMG, C), bf16), rows(IMG, C))]
    return call(kernel_upstream, "upstream", (slots,), ins, outs, [native_rows(slots), ((IMG, C), f32)], 60, 5)[0]


def forward(xrow, stat, bucket, wf, vec, kcat):
    con = constants()
    pairs = xrow.shape[0] // PAIR
    n = pairs * PAIR
    outs = [
        (sds((n, C), f32), rows(PAIR, C)),
        (sds((n, GATES), f32), rows(PAIR, GATES)),
        (sds((n, C), bf16), rows(PAIR, C)),
        (sds((pairs * 3 * IMG, C2), bf16), rows(3 * IMG, C2)),
        (sds((pairs * 3 * IMG, C2), bf16), rows(3 * IMG, C2)),
        (sds((pairs * 3 * SR, C2), bf16), rows(3 * SR, C2)),
        (sds((pairs * 8, C2), f32), rows(8, C2)),
    ]
    mats = [jnp.asarray(con[k]) for k in ("es", "fe", "fo", "ge", "go")]
    ins = [(bucket, smem())] + by_rows(PAIR, xrow, stat) + whole(wf, vec, kcat, *mats)
    scratch = [
        ((6, SR, C), f32), ((PAIR, C), bf16), ((PAIR, C), f32), ((3 * HALF, C2), bf16), ((3 * HALF, C2), bf16), ((AR, C2), f32), ((BR, C2), f32),
        ((HALF, C2), f32), ((HALF, C2), f32), ((3 * AR, C2), bf16), ((3 * BR, C2), bf16), ((PAIR, C), f32),
        ((4, PAIR, 128), f32),
    ]
    return call(kernel_forward, "focal_forward", (pairs,), ins, outs, scratch, 60, 32)


def middle(gx, gy, pos, xrow, up, mixed, q, wh, wp, w1, w2, vec, bm1, mlp_len):
    n = xrow.shape[0]
    outs = [
        (sds((n, C), f32), rows(BROWS, C)),
        (sds((n, C), f32), rows(BROWS, C)),
        (sds((n, C), bf16), rows(BROWS, C)),
        (sds((n, C), f32), rows(BROWS, C)),
    ]
    slots = (gy // 2, gx, block_rows(mlp_len), 128)
    outs += [(sds(slots, bf16), full(slots))] * 2
    outs += [(sds(s, f32), full(s)) for s in ((C, C), (C, C), (8, C), (8, HID))]
    ins = [(pos, smem())] + by_rows(BROWS, xrow, up, mixed, q) + whole(wh, wp, w1, w2, vec, bm1)
    blk = (BROWS, C)
    scratch = [
        (blk, f32), (blk, bf16), (blk, f32), (blk, f32), (blk, bf16), (blk, bf16), (blk, f32), (blk, f32),
        ((BROWS, HCHUNK), bf16), ((BROWS, HCHUNK), bf16), ((BROWS, HCHUNK), f32), ((8, 8, C), f32), ((8, HID), f32),
        ((C, HID), f32), ((HID, C), f32), ((span(mlp_len, gx * gy), 128), f32),
    ]
    kernel = functools.partial(kernel_middle, gx, gy, mlp_len)
    return call(kernel, "middle", (n // BROWS,), ins, outs, scratch, 62, 42)


def backward(gx, gy, pos, bucket, nb, dq, dmix, gates, z, g, spec, mean, kcat, wf, vec, sums, bsum, gwh, gwp, mod_len, small_len):
    con = constants()
    ndev = gx * gy
    pairs = nb.shape[0] // PAIR
    mats = [jnp.asarray(con["es"]), jnp.asarray(con["weights"]), jnp.asarray(con["fe"][:, :HALF]), jnp.asarray(con["fo"][:, :HALF])]
    mats += [jnp.asarray(con["ge"][:, :AR]), jnp.asarray(con["go"][:, :BR])]
    slots = (gy // 2, gx, -(-(block_rows(mod_len) + block_rows(small_len)) // 16) * 16, 128)
    outs = [(sds((nb.shape[0], MERGED), bf16), rows(PAIR, MERGED))] + [(sds(slots, bf16), full(slots))] * 2
    ins = [(bucket, smem()), (pos, smem())] + by_rows(PAIR, nb, dq, dmix, gates) + by_rows(3 * IMG, z, g) + by_rows(3 * SR, spec)
    ins += by_rows(8, mean) + whole(kcat, wf, vec, sums, bsum, gwh, gwp, *mats)
    small_rows = -(-max(span(small_len, ndev), END_ROW + 2) // 8) * 8
    scratch = [
        ((C, MERGED), f32), ((8, MERGED), f32), ((16, C), f32), ((3, TAPS, C), f32), ((6, SR, C), f32),
        ((HALF, C2), bf16), ((HALF, C2), bf16), ((AR, C2), f32), ((BR, C2), f32), ((HALF, C2), f32), ((HALF, C2), f32),
        ((AR, C2), bf16), ((BR, C2), bf16), ((6, SR, C), f32), ((8, MERGED), f32), ((4, PAIR, 128), f32),
        ((max(span(mod_len, ndev), STRIDE * 16 + 8), 128), f32), ((small_rows, 128), f32), ((small_rows, 128), f32),
        ((MERGED // 128, PERIOD * 16, 128), f32),
    ]
    kernel = functools.partial(kernel_backward, gx, gy, mod_len, small_len)
    return call(kernel, "focal_backward", (pairs,), ins, outs, scratch, 62, 28)


def tail(shape, dmer, wf, xrow, stat, dmid, vec):
    slots = shape[2]
    ins = by_rows(PAIR, dmer) + whole(wf) + by_rows(PAIR, xrow, stat, dmid) + whole(vec)
    return call(kernel_tail, "tail", (slots // 2,), ins, [(sds(shape, f32), full(shape))], [((PAIR, C), f32), native_rows(slots)], 60, 8)[0]


def out_tokens(shape, counts, out_rows):
    ins = [(counts, smem())] + whole(out_rows)
    return call(kernel_out, "out_tokens", (), ins, [(sds(shape, bf16), full(shape))], [native_rows(shape[2])], 60, 5)[0]


def span(length, ndev):
    return ((ndev - 1) * length) // 1024 * 8 + block_rows(length)


def unpack_mod(gx, gy, pos, own, oth, mod_len, small_len):
    ndev = gx * gy
    outs = [sds((C, MERGED), bf16), sds((C, C), bf16), sds((C, C), bf16), sds((VROWS, C), f32), sds((8, HID), f32), sds((3, 2 * TAPS, C), bf16)]
    top = STRIDE * 15 + STRIDE + 8
    flat_rows = max(span(mod_len, ndev), top)
    small_rows = max(span(small_len, ndev), END_ROW + 26)
    scratch = [((flat_rows, 128), f32), ((small_rows + 8, 128), f32), ((small_rows, 128), f32), ((MERGED // 128, PERIOD * 16, 128), f32)]
    kernel = functools.partial(kernel_unpack_mod, gx, gy, mod_len, small_len)
    return call(kernel, "unpack_mod", (), [(pos, smem())] + whole(own, oth), [(o, full(o.shape)) for o in outs], scratch, 60, 4)


def unpack_mlp(gx, gy, pos, blocks, mlp_len):
    outs = [sds((C, HID), bf16), sds((HID, C), bf16)]
    kernel = functools.partial(kernel_unpack_mlp, gx, gy, mlp_len)
    scratch = [((span(mlp_len, gx * gy), 128), f32)]
    return call(kernel, "unpack_mlp", (), [(pos, smem())] + whole(*blocks), [(o, full(o.shape)) for o in outs], scratch, 60, 3)


def add(arrays, outs, name):
    return call(functools.partial(kernel_add, len(arrays)), name, (), whole(*arrays), [(o, full(o.shape)) for o in outs], [], 24, 2)


def swap(x, mask, ndev):
    return lax.ppermute(x, AXES, [(k, k ^ mask) for k in range(ndev)])


def around(x, step, count, ndev):
    return [x] + [swap(x, step * k, ndev) for k in range(1, count)]


def after(values):
    return lax.optimization_barrier(values)


def travel(parts, step, ndev):
    return [parts[0]] + [swap(p, step * k, ndev) for k, p in enumerate(parts) if k]


def sum_core(own, oth, gx, gy, name):
    got = swap(oth, 1, gx * gy)
    return add([own, got], [sds(own.shape[1:], f32 if k == 0 else bf16) for k in range(gy // 2)], name + "_sum_core")


def sum_plane(parts, gx, name):
    shape = parts[0].shape[1:]
    return add(parts, [sds(shape, f32 if k == 0 else bf16) for k in range(gx)], name + "_sum_plane")


def sum_line(parts, cuts, name):
    outs = [(sds((n, 128), f32), full((n, 128))) for _, n in cuts]
    return call(functools.partial(kernel_cut, cuts), name + "_sum_line", (), whole(*parts), outs, [], 24, 2)


def local(gx, gy, tokens, bucket, counts, mod_weights, mlp_weights, small_params, cotangent):
    ndev = gx * gy
    gxi, gyi = lax.axis_index("gx"), lax.axis_index("gy")
    device = gxi * gy + gyi
    pos = jnp.stack([gxi, gyi]).astype(jnp.int32)
    mod_len, small_len, mlp_len = mod_weights.shape[0], small_params.shape[0], mlp_weights.shape[0]
    mr, sr = block_rows(mod_len), block_rows(small_len)

    blocks = [place(mod_weights, device), place(small_params, device)]
    pad = -(mr + sr) % 16
    if pad:
        blocks.append(jnp.zeros((pad, 128), bf16))
    cut = mr + sr + pad
    line = around(jnp.concatenate(blocks + [place(mlp_weights, device)], 0), gy, gx, ndev)
    native, back = (1, 2, 0, 3), (2, 0, 1, 3)
    shape = (GH, GW) + tokens.shape[:1] + (C,)
    prepared = prep(jnp.transpose(tokens, native))
    line, prepared = after((line, prepared))
    xrow, nb, stat = prepared
    plane = around(jnp.stack([v[:cut] for v in line]), 2, gy // 2, ndev)
    mlp_line = jnp.stack([v[cut:] for v in line])
    mlp_other = swap(mlp_line, 1, ndev)
    up = upstream(counts, jnp.transpose(cotangent, native))
    plane, mlp_other, up = after((plane, mlp_other, up))
    plane = jnp.stack(plane)
    other = swap(plane, 1, ndev)
    mlp_both = jnp.stack([mlp_line, mlp_other])
    other, mlp_both = after((other, mlp_both))
    mlp_blocks = around(mlp_both, 2, gy // 2, ndev)

    wf, wh, wp, vec, bm1, kcat = unpack_mod(gx, gy, pos, plane, other, mod_len, small_len)
    q, gates, mixed, z, g, spec, mean = forward(xrow, stat, bucket, wf, vec, kcat)
    mlp_blocks, mixed = after((mlp_blocks, mixed))
    w1, w2 = unpack_mlp(gx, gy, pos, mlp_blocks, mlp_len)
    dmid, out_rows, dq, dmix, own, oth, gwh, gwp, sums, bsum = middle(
        gx, gy, pos, xrow, up, mixed, q, wh, wp, w1, w2, vec, bm1, mlp_len
    )
    parts = sum_core(own, oth, gx, gy, "mlp")
    parts, dmix = after((parts, dmix))
    mlp_plane = travel(parts, 2, ndev)
    dmer, own, oth = backward(
        gx, gy, pos, bucket, nb, dq, dmix, gates, z, g, spec, mean, kcat, wf, vec, sums, bsum, gwh, gwp, mod_len, small_len
    )
    mlp_plane, own, oth = after((mlp_plane, own, oth))
    parts = sum_plane(mlp_plane, gx, "mlp")
    mod_parts = sum_core(own, oth, gx, gy, "mod")
    mlp_line = travel(parts, gy, ndev)
    mod_plane = travel(mod_parts, 2, ndev)
    gtok = tail(shape, dmer, wf, xrow, stat, dmid, vec)
    mod_plane, mlp_line, gtok, out_rows = after((mod_plane, mlp_line, gtok, out_rows))
    mod_line = travel(sum_plane(mod_plane, gx, "mod"), gy, ndev)
    grad_mlp = take(sum_line(mlp_line, [(0, mlp_line[0].shape[0])], "mlp")[0], mlp_len, device)
    out = out_tokens(shape, counts, out_rows)
    mod_line, out, grad_mlp = after((mod_line, out, grad_mlp))
    total_mod, total_small = sum_line(mod_line, [(0, mr), (mr, sr)], "mod")
    grad_mod = take(total_mod, mod_len, device)
    grad_small = take(total_small, small_len, device)
    return jnp.transpose(out, back), jnp.transpose(gtok, back), grad_mod, grad_mlp, grad_small


def solution(mesh):
    images = P(AXES, None, None, None)
    flat = P(AXES)
    return jax.shard_map(
        functools.partial(local, mesh.shape["gx"], mesh.shape["gy"]),
        mesh=mesh,
        in_specs=(images, flat, flat, flat, flat, flat, images),
        out_specs=(images, images, flat, flat, flat),
        check_vma=False,
    )
```

```python
import functools

import jax
import jax.numpy as jnp
import numpy as np
from jax import lax
from jax.experimental import pallas as pl
from jax.experimental.pallas import tpu as pltpu
from jax.sharding import PartitionSpec as P

C = 384
HID = 1536
GH = 14
GW = 20
HALF = 144
IMG = 2 * HALF
PAIR = 2 * IMG
C2 = 2 * C
NY = 17
NX = 23
NV = 12
NU = 8
Q = NU * NV
AR = 2 * (Q + 16)
BR = 2 * Q
SR = 4 * Q + 32
LEVELS = (3, 5, 7)
TAPS = 64
GATES = 128
MERGED = C2 + GATES
BROWS = 768
HCHUNK = 512
AXES = ("gx", "gy")
f32 = jnp.float32
bf16 = jnp.bfloat16
EPS = 1e-05
ROOT_HALF = 0.7071067811865476
INV_ROOT_2PI = 0.3989422804014327


def _hi(a):
    return a.astype(bf16)


def _lo(a):
    return (a - a.astype(bf16).astype(np.float64)).astype(bf16)


@functools.lru_cache(maxsize=None)
def constants():
    row = np.arange(HALF)
    real = (row < 7 * GW).astype(np.float64)
    yy = np.minimum(row // GW, 6) - (GH - 1) / 2
    xx = row % GW - (GW - 1) / 2
    uv = [(u, v) for u in range(1, NU + 1) for v in range(NV)]
    u0 = [(0, v) for v in range(NV)]
    wu = 2 * np.pi / NY
    wv = 2 * np.pi / NX

    def trig(pairs, pad):
        u = np.array([p[0] for p in pairs] + [0] * pad, np.float64)[:, None]
        v = np.array([p[1] for p in pairs] + [0] * pad, np.float64)[:, None]
        use = np.array([1.0] * len(pairs) + [0.0] * pad)[:, None] * real[None]
        cy, sy = np.cos(wu * u * yy) * use, np.sin(wu * u * yy) * use
        cx, sx = np.cos(wv * v * xx), np.sin(wv * v * xx)
        weight = np.where(u > 0, 2.0, 1.0) * np.where(v > 0, 2.0, 1.0) / (NY * NX)
        return cy * cx, -cy * sx, sy * cx, -sy * sx, weight

    e_re, e_im, o_re, o_im, w1 = trig(uv, 0)
    z_re, z_im, _, _, w0 = trig(u0, 16 - NV)
    fe = np.concatenate([e_re, z_re, e_im, z_im], 0)
    fo = np.concatenate([o_re, o_im], 0)
    half = np.concatenate([0.5 * w1, w0, 0.5 * w1, w0], 0)
    ge = (fe * half).T
    go = (fo * np.concatenate([0.5 * w1, 0.5 * w1], 0)).T

    u = np.array([p[0] for p in uv], np.float64)[:, None]
    v = np.array([p[1] for p in uv], np.float64)[:, None]
    v0 = np.array(list(range(NV)) + [0] * (16 - NV), np.float64)[:, None]
    use0 = np.array([1.0] * NV + [0.0] * (16 - NV))[:, None]
    wp = np.where(v > 0, 2.0, 1.0) / (NY * NX)
    wz = np.where(v0 > 0, 2.0, 1.0) * use0 / (NY * NX)
    weights = np.concatenate([wp, -wp, wp, -wp, wz, -wz], 0)
    es = []
    for k in LEVELS:
        h = k // 2
        ty, tx = np.meshgrid(np.arange(k) - h, np.arange(k) - h, indexing="ij")
        for bucket in (0, 1):
            sy, sx = (ty, tx) if bucket == 0 else (tx, ty)
            py = sy.reshape(1, -1) * wu
            px = sx.reshape(1, -1) * wv
            plus = u * py + v * px
            minus = -u * py + v * px
            zero = v0 * px
            e = [np.cos(plus), np.sin(plus), np.cos(minus), np.sin(minus), np.cos(zero) * use0, np.sin(zero) * use0]
            whole_e = np.zeros((SR, TAPS))
            whole_e[:, : k * k] = np.concatenate(e, 0)
            es.append(np.concatenate([_hi(whole_e), _lo(whole_e)], 1))
    return dict(
        fe=np.concatenate([_hi(fe), _lo(fe), _hi(fe)], 1),
        fo=np.concatenate([_hi(fo), _lo(fo), _hi(fo)], 1),
        ge=np.concatenate([_hi(ge), _lo(ge), _hi(ge)], 1),
        go=np.concatenate([_hi(go), _lo(go), _hi(go)], 1),
        es=np.stack(es),
        est=np.stack([np.ascontiguousarray(e.T) for e in es]),
        weights=np.broadcast_to(weights, (SR, 128)).astype(np.float32),
    )


def dot(a, b):
    return jnp.dot(a, b, preferred_element_type=f32)


def dot_nt(a, b):
    return lax.dot_general(a, b, (((1,), (1,)), ((), ())), preferred_element_type=f32)


def dot_tn(a, b):
    return lax.dot_general(a, b, (((0,), (0,)), ((), ())), preferred_element_type=f32)


def gelu_pair(x):
    cdf = 0.5 * lax.erf(x * ROOT_HALF) + 0.5
    return x * cdf, cdf + x * (jnp.exp(x * x * -0.5) * INV_ROOT_2PI)


def split(x):
    hi = x.astype(bf16)
    return hi, (x - hi.astype(f32)).astype(bf16)


def at(base, i, n=16):
    return slice(base + i * n, base + i * n + n)


def weave(products, vector):
    n, m = len(products), len(vector)
    done = 0
    for k, step in enumerate(products):
        step()
        upto = (k + 1) * m // n
        for other in vector[done:upto]:
            other()
        done = upto


def norm_stats(x):
    mean = jnp.mean(x, axis=-1, keepdims=True)
    centred = x - mean
    var = jnp.mean(centred * centred, axis=-1, keepdims=True)
    r = lax.rsqrt(var + EPS)
    return centred * r, r


def sum8(x):
    total = x[0:8]
    for k in range(1, x.shape[0] // 8):
        total = total + x[8 * k : 8 * k + 8]
    return total


def grid_rows(im, y):
    return im * IMG + (y * GW if y < 7 else HALF + (GH - 1 - y) * GW)


def lanes(im):
    return slice(im * C, im * C + C)


(V_G1, V_B1, V_BQ, V_BC, V_HB, V_PB, V_S1, V_G2, V_B2, V_BM2, V_S2, V_BG) = range(12)
VROWS = 16
(S_HB, S_PB, S_S1, S_G2, S_B2, S_BM2, S_S2, S_BQ) = range(8)


def from_native(src, native):
    slots = src.shape[2]
    line = GW * slots
    for y in range(GH):
        for lt in range(C // 128):
            ls = slice(128 * lt, 128 * lt + 128)
            native[lt, line * y : line * (y + 1), :] = src[y, :, :, ls].astype(f32).reshape(line, 128)


def image_rows(native, image, first, slot, slots, gain):
    for h in (GH // 2 * GW, HALF + GH // 2 * GW):
        image[first + h : first + h + 4, :] = jnp.zeros((4, C), f32)
    for y in range(GH):
        a = first + grid_rows(0, y)
        for lt in range(C // 128):
            v = native[lt, pl.ds(GW * slots * y + slot, GW, stride=slots), :]
            image[a : a + GW, 128 * lt : 128 * lt + 128] = v if gain is None else v * gain


def kernel_prep(x_ref, xrow_o, nb_o, stat_o, native, image):
    slot = pl.program_id(0)

    @pl.when(slot == 0)
    def _():
        from_native(x_ref, native)

    for im in range(2):
        image_rows(native, image, im * IMG, slot * 2 + im, x_ref.shape[2], None)
    lane = lax.broadcasted_iota(jnp.int32, (32, 128), 1)
    for i in range(PAIR // 32):
        s = at(0, i, 32)
        x = image[s, :]
        xrow_o[s, :] = x.astype(bf16)
        mean = jnp.mean(x, axis=-1, keepdims=True)
        centred = x - mean
        r = lax.rsqrt(jnp.mean(centred * centred, axis=-1, keepdims=True) + EPS)
        nb_o[s, :] = (centred * r).astype(bf16)
        stat_o[s, :] = jnp.where(lane == 0, mean, r)


def kernel_upstream(counts, cot_ref, up_o, native, image):
    slot = pl.program_id(0)

    @pl.when(slot == 0)
    def _():
        from_native(cot_ref, native)

    for im in range(2):
        live = (slot * 2 + im < counts[0]).astype(f32)
        image_rows(native, image, im * IMG, slot * 2 + im, cot_ref.shape[2], live)
    for i in range(PAIR // 32):
        s = at(0, i, 32)
        up_o[s, :] = image[s, :].astype(bf16)


CHAINS = 3
CHAIN = C2 // CHAINS


def staggered(phases):
    lists = [phases(t) for t in range(CHAINS)]
    for turn in range(len(lists[0]) + CHAINS - 1):
        for t in range(CHAINS):
            if 0 <= turn - t < len(lists[t]):
                lists[t][turn - t]()


def sub_tiles(t):
    for k in range(t * CHAIN // 128, (t + 1) * CHAIN // 128):
        lt = k % (C // 128)
        yield k // (C // 128), slice(128 * k, 128 * k + 128), slice(128 * lt, 128 * lt + 128)


def spread_gates(gates, wide):
    for k in range(4):
        for i in range(PAIR // 32):
            s = at(0, i, 32)
            wide[k, s, :] = jnp.broadcast_to(gates[s, k : k + 1], (32, 128))


def kernel_forward(
    gx, gy, mod_len, small_len, bucket, pos, x_ref, stat, own, oth, es, fe, fo, ge, go,
    q_o, gates_o, mixed_o, z_o, g_o, spec_o, mean_o, wf, wh, wp, vec, bm1, kcat,
    h_o, normed, ctx, ecat, ocat, s_a, s_b, s_e, s_o, yca, ycb, mix, wide, flat, small, moved, spread,
):
    step = pl.program_id(0)

    @pl.when(step == 0)
    def _():
        unpack_mod(gx, gy, mod_len, small_len, pos, own, oth, wf, wh, wp, vec, bm1, kcat, flat, small, moved, spread)
        for lb in range(6):
            h_o[lb] = dot(es[lb], kcat[lb // 2])

    g1, b1 = vec[V_G1 : V_G1 + 1, :], vec[V_B1 : V_B1 + 1, :]
    for i in range(PAIR // 32):
        s = at(0, i, 32)
        n = (x_ref[s, :].astype(f32) - stat[s, 0:1]) * stat[s, 1:2]
        normed[s, :] = (n * g1 + b1).astype(bf16)
    right = dot(normed[...], wf[:, C + 128 :])
    left = dot(normed[...], wf[:, : C + 128])
    ctx[:, :128] = left[:, C:] + vec[V_BC : V_BC + 1, :128]
    ctx[:, 128:] = right[:, : C - 128] + vec[V_BC : V_BC + 1, 128:]
    gates_o[...] = right[:, C - 128 :] + vec[V_BG : V_BG + 1, :GATES]
    q_o[...] = left[:, :C] + vec[V_BQ : V_BQ + 1, :]
    spread_gates(gates_o, wide)
    lbs = [[level * 2 + bucket[step * 2 + im] for im in range(2)] for level in range(3)]

    def put_pair(ls, i, top, bot):
        e_hi, e_lo = split(top + bot)
        o_hi, o_lo = split(top - bot)
        for base, ev, ov in ((0, e_hi, o_hi), (HALF, e_hi, o_hi), (2 * HALF, e_lo, o_lo)):
            ecat[at(base, i), ls] = ev
            ocat[at(base, i), ls] = ov

    def first(t):
        for im, ls, hs in sub_tiles(t):
            for i in range(HALF // 16):
                put_pair(ls, i, ctx[at(im * IMG, i), hs], ctx[at(im * IMG + HALF, i), hs])

    def transform(t):
        ts = slice(t * CHAIN, (t + 1) * CHAIN)
        s_a[:, ts] = dot(fe[...], ecat[:, ts])
        s_b[:, ts] = dot(fo[...], ocat[:, ts])

    def back(t):
        ts = slice(t * CHAIN, (t + 1) * CHAIN)
        s_e[:, ts] = dot(ge[...], yca[:, ts])
        s_o[:, ts] = dot(go[...], ycb[:, ts])

    def filt(t, level):
        base = level * SR
        for im, ls, hs in sub_tiles(t):
            lb = lbs[level][im]
            for i in range(Q // 16):
                a_re, a_im = s_a[at(0, i), ls], s_a[at(Q + 16, i), ls]
                b_re, b_im = s_b[at(0, i), ls], s_b[at(Q, i), ls]
                xp_re, xp_im = a_re + b_im, a_im - b_re
                xm_re, xm_im = a_re - b_im, a_im + b_re
                spec_o[at(base, i), ls] = xp_re.astype(bf16)
                spec_o[at(base + Q, i), ls] = xp_im.astype(bf16)
                spec_o[at(base + 2 * Q, i), ls] = xm_re.astype(bf16)
                spec_o[at(base + 3 * Q, i), ls] = xm_im.astype(bf16)
                p_re, p_im = h_o[lb, at(0, i), hs], h_o[lb, at(Q, i), hs]
                q_re, q_im = h_o[lb, at(2 * Q, i), hs], h_o[lb, at(3 * Q, i), hs]
                yp_re, yp_im = p_re * xp_re - p_im * xp_im, p_re * xp_im + p_im * xp_re
                ym_re, ym_im = q_re * xm_re - q_im * xm_im, q_re * xm_im + q_im * xm_re
                for dst, off, width, val in (
                    (yca, 0, AR, yp_re + ym_re),
                    (yca, Q + 16, AR, yp_im + ym_im),
                    (ycb, 0, BR, ym_im - yp_im),
                    (ycb, Q, BR, yp_re - ym_re),
                ):
                    hi, lo = split(val)
                    dst[at(off, i), ls] = hi
                    dst[at(off + width, i), ls] = hi
                    dst[at(off + 2 * width, i), ls] = lo
            x_re, x_im = s_a[Q : Q + 16, ls], s_a[2 * Q + 16 : 2 * Q + 32, ls]
            spec_o[base + 4 * Q : base + 4 * Q + 16, ls] = x_re.astype(bf16)
            spec_o[base + 4 * Q + 16 : base + 4 * Q + 32, ls] = x_im.astype(bf16)
            p_re, p_im = h_o[lb, 4 * Q : 4 * Q + 16, hs], h_o[lb, 4 * Q + 16 : 4 * Q + 32, hs]
            for off, val in ((Q, p_re * x_re - p_im * x_im), (2 * Q + 16, p_re * x_im + p_im * x_re)):
                hi, lo = split(val)
                yca[off : off + 16, ls] = hi
                yca[off + AR : off + AR + 16, ls] = hi
                yca[off + 2 * AR : off + 2 * AR + 16, ls] = lo

    def act(t, level):
        for im, ls, hs in sub_tiles(t):
            total = jnp.zeros((8, 128), f32)
            for i in range(HALF // 16):
                even, odd = s_e[at(0, i), ls], s_o[at(0, i), ls]
                both = []
                for h, a in ((0, even + odd), (HALF, even - odd)):
                    z, g = gelu_pair(a)
                    z_o[at(level * IMG + h, i), ls] = z.astype(bf16)
                    g_o[at(level * IMG + h, i), ls] = g.astype(bf16)
                    s = at(im * IMG + h, i)
                    part = z * wide[level, s, :]
                    mix[s, hs] = part if level == 0 else mix[s, hs] + part
                    both.append(z)
                if level < 2:
                    put_pair(ls, i, both[0], both[1])
                else:
                    total = total + sum8(both[0]) + sum8(both[1])
            if level == 2:
                mean = jnp.sum(total, axis=0, keepdims=True) * (1.0 / (GH * GW))
                mean_o[:, ls] = jnp.broadcast_to(mean, (8, 128))
                glob, _ = gelu_pair(mean)
                for i in range(IMG // 16):
                    s = at(im * IMG, i)
                    mixed_o[s, hs] = (mix[s, hs] + wide[3, s, :] * glob).astype(bf16)

    def phases(t):
        steps = [lambda: first(t)]
        for level in range(3):
            steps += [
                lambda: transform(t),
                lambda level=level: filt(t, level),
                lambda: back(t),
                lambda level=level: act(t, level),
            ]
        return steps

    staggered(phases)


def kernel_middle(
    gx, gy, mlp_len, pos, x_ref, up, mixed, q_ref, wh, wp, vec, bm1, *refs,
):
    blocks = refs[: gy // 2]
    (
        dmid_o, out_o, dq_o, dmix_o, own, oth, gwh, gwp, sums, bsum,
        mod, modulated, branch, mid, second, dshr, shr, dsec, act, dexp, hid, dact, dbr, dm2, dmod, vacc, bacc, gw1, gw2, flat,
        w1, w2,
    ) = refs[gy // 2 :]
    step = pl.program_id(0)
    start = step == 0

    @pl.when(start)
    def _():
        for ref in (gwh, gwp, vacc, bacc):
            ref[...] = jnp.zeros_like(ref)
        unpack_mlp(gx, gy, mlp_len, pos, blocks, w1, w2, flat)

    def add_to(ref, rows_at, cols, v):
        ref[rows_at, cols] = jnp.where(start, 0.0, ref[rows_at, cols]) + v

    g2, b2 = vec[V_G2 : V_G2 + 1, :], vec[V_B2 : V_B2 + 1, :]
    s1, s2 = vec[V_S1 : V_S1 + 1, :], vec[V_S2 : V_S2 + 1, :]
    bm2 = vec[V_BM2 : V_BM2 + 1, :]

    mod[...] = dot(mixed[...], wh[...]) + vec[V_HB : V_HB + 1, :]
    for i in range(BROWS // 32):
        s = at(0, i, 32)
        modulated[s, :] = (q_ref[s, :] * mod[s, :]).astype(bf16)
        dshr[s, :] = (up[s, :].astype(f32) * s2).astype(bf16)
    branch[...] = dot(modulated[...], wp[...]) + vec[V_PB : V_PB + 1, :]
    for i in range(BROWS // 32):
        s = at(0, i, 32)
        middle = x_ref[s, :].astype(f32) + s1 * branch[s, :]
        mid[s, :] = middle
        n, _ = norm_stats(middle)
        second[s, :] = (n * g2 + b2).astype(bf16)

    chunks = [slice(h * HCHUNK, (h + 1) * HCHUNK) for h in range(HID // HCHUNK)]

    def enter(h):
        def into(t, k):
            ls = slice(h * HCHUNK + 256 * t, h * HCHUNK + 256 * t + 256)
            if k == 0:
                hid[h % 2, :, 256 * t : 256 * t + 256] = dot(second[...], w1[:, ls]) + bm1[0:1, ls]
            else:
                dact[h % 2, :, 256 * t : 256 * t + 256] = dot_nt(dshr[...], w2[ls, :])

        return [functools.partial(into, t, k) for t in range(HCHUNK // 256) for k in range(2)]

    def gelu(h):
        totals = []

        def rows_of(i):
            s = at(0, i)
            z, g = gelu_pair(hid[h % 2, s, :])
            act[s, chunks[h]] = z.astype(bf16)
            d = dact[h % 2, s, :] * g
            dexp[s, chunks[h]] = d.astype(bf16)
            totals.append(sum8(d) if not totals else totals.pop() + sum8(d))

        def close():
            bacc[:, chunks[h]] += totals[0]

        return [functools.partial(rows_of, i) for i in range(BROWS // 16)] + [close]

    def weight_grads(h):
        def one(t):
            ls = slice(h * HCHUNK + 256 * t, h * HCHUNK + 256 * t + 256)
            add_to(gw1, slice(None), ls, dot_tn(second[...], dexp[:, ls]))

        def two():
            add_to(gw2, chunks[h], slice(None), dot_tn(act[:, chunks[h]], dshr[...]))

        return [functools.partial(one, t) for t in range(HCHUNK // 256)] + [two]

    for step_of in enter(0):
        step_of()
    weave(enter(1), gelu(0))
    weave(enter(2) + weight_grads(0), gelu(1))
    weave(weight_grads(1), gelu(2))
    shr[...] = dot(act[...], w2[...])
    dsec[...] = dot_nt(dexp[...], w1[...])

    tally = {}

    def count(key, v):
        tally[key] = tally[key] + sum8(v) if key in tally else sum8(v)

    def finish(i):
        s = at(0, i, 32)
        middle = mid[s, :]
        u = up[s, :].astype(f32)
        shrunk = shr[s, :] + bm2
        out_o[s, :] = (middle + s2 * shrunk).astype(bf16)
        n, r = norm_stats(middle)
        d = dsec[s, :]
        e = d * g2
        dn = d * n
        dv = r * (e - jnp.mean(e, axis=-1, keepdims=True) - n * jnp.mean(e * n, axis=-1, keepdims=True))
        dm = u + dv
        dmid_o[s, :] = dm
        db = s1 * dm
        dbr[s, :] = db.astype(bf16)
        count(S_S1, dm * branch[s, :])
        count(S_G2, dn)
        count(S_B2, d)
        count(S_BM2, dshr[s, :].astype(f32))
        count(S_S2, u * shrunk)
        count(S_PB, db)

    weave(weight_grads(2), [functools.partial(finish, i) for i in range(BROWS // 32)])
    dmod[...] = dot_nt(dbr[...], wp[...])

    def demod(i):
        s = at(0, i, 32)
        dm = dmod[s, :]
        dq = dm * mod[s, :]
        dd = dm * q_ref[s, :]
        dq_o[s, :] = dq.astype(bf16)
        dm2[s, :] = dd.astype(bf16)
        count(S_BQ, dq)
        count(S_HB, dd)

    def grad_wp():
        gwp[...] += dot_tn(modulated[...], dbr[...])

    weave([grad_wp], [functools.partial(demod, i) for i in range(BROWS // 32)])
    dmix_o[...] = dot_nt(dm2[...], wh[...])
    gwh[...] += dot_tn(mixed[...], dm2[...])

    for key, v in tally.items():
        vacc[key] += v

    @pl.when(step == pl.num_programs(0) - 1)
    def _():
        for k in range(8):
            sums[k : k + 1, :] = jnp.sum(vacc[k], axis=0, keepdims=True)
        bsum[...] = jnp.broadcast_to(jnp.sum(bacc[...], axis=0, keepdims=True), bsum.shape)
        pack_mlp(gx, gy, mlp_len, pos, gw1, gw2, own, oth, flat)


def kernel_backward(
    gx, gy, mod_len, small_len,
    bucket, pos, nb_ref, dq_ref, dmix, gates, z_ref, g_ref, spec, mean_ref, kcat, vec, sums, bsum, es, weights,
    fe, fo, ge, go, wf_far, gwh_far, gwp_far, est_far,
    dmer, own, oth,
    gwf, fsum, gb, dk, h_ref, ecat, ocat, s_a, s_b, s_e, s_o, yca, ycb, acc, facc, wide, flat, small, moved, spread,
    wf, gwh, gwp, est, sems,
):
    step = pl.program_id(0)
    last = pl.num_programs(0) - 1
    late = [
        pltpu.make_async_copy(src, dst, sems.at[k])
        for k, (src, dst) in enumerate(((wf_far, wf), (gwh_far, gwh), (gwp_far, gwp), (est_far, est)))
    ]

    @pl.when(step == 0)
    def _():
        for copy in late:
            copy.start()
        for ref in (gwf, facc, acc):
            ref[...] = jnp.zeros_like(ref)
        for lb in range(6):
            h_ref[lb] = dot(es[lb], kcat[lb // 2])

    spread_gates(gates, wide)
    lbs = [[level * 2 + bucket[step * 2 + im] for im in range(2)] for level in range(3)]
    globs = [gelu_pair(mean_ref[0:1, lanes(im)]) for im in range(2)]
    lane = lax.broadcasted_iota(jnp.int32, (16, GATES), 1)
    dmeans = {}

    def mean_grad(t):
        for im, ls, hs in sub_tiles(t):
            total = jnp.zeros((8, 128), f32)
            for i in range(IMG // 16):
                s = at(im * IMG, i)
                total = total + sum8(dmix[s, hs] * wide[3, s, :])
            dmeans[ls.start] = jnp.sum(total, axis=0, keepdims=True) * globs[im][1][:, hs] * (1.0 / (GH * GW))

    def gate_grad(part):
        t_g = jnp.zeros((8, GATES), f32)
        n = 2 * (HALF // 16) // CHAINS
        for im, i in [(im, i) for im in range(2) for i in range(HALF // 16)][part * n : part * n + n]:
            for h in (0, HALF):
                s = at(im * IMG + h, i)
                dm = dmix[s, :]
                dg = jnp.zeros((16, GATES), f32)
                for k in range(4):
                    other = z_ref[at(k * IMG + h, i), lanes(im)].astype(f32) if k < 3 else globs[im][0]
                    col = jnp.sum(dm * other, axis=-1, keepdims=True)
                    dg = jnp.where(lane == k, col, dg)
                dmer[s, :C] = dq_ref[s, :]
                dmer[s, C2:] = dg.astype(bf16)
                t_g = t_g + sum8(dg)
        facc[:, C2:] += t_g

    def before(t, level):
        for im, ls, hs in sub_tiles(t):
            for i in range(HALF // 16):
                if level < 2:
                    even, odd = s_e[at(0, i), ls], s_o[at(0, i), ls]
                    through = (even + odd, even - odd)
                else:
                    through = (dmeans[ls.start], dmeans[ls.start])
                parts = []
                for k, h in enumerate((0, HALF)):
                    s = at(im * IMG + h, i)
                    dz = wide[level, s, :] * dmix[s, hs] + through[k]
                    parts.append(dz * g_ref[at(level * IMG + h, i), ls].astype(f32))
                ecat[at(0, i), ls] = (parts[0] + parts[1]).astype(bf16)
                ocat[at(0, i), ls] = (parts[0] - parts[1]).astype(bf16)

    def transform(t):
        ts = slice(t * CHAIN, (t + 1) * CHAIN)
        s_a[:, ts] = dot(fe[...], ecat[:, ts])
        s_b[:, ts] = dot(fo[...], ocat[:, ts])

    def back(t):
        ts = slice(t * CHAIN, (t + 1) * CHAIN)
        s_e[:, ts] = dot(ge[...], yca[:, ts])
        s_o[:, ts] = dot(go[...], ycb[:, ts])

    def filt(t, level):
        base = level * SR
        for im, ls, hs in sub_tiles(t):
            lb = lbs[level][im]
            for i in range(Q // 16):
                a_re, a_im = s_a[at(0, i), ls], s_a[at(Q + 16, i), ls]
                b_re, b_im = s_b[at(0, i), ls], s_b[at(Q, i), ls]
                dp_re, dp_im = a_re + b_im, a_im - b_re
                dm_re, dm_im = a_re - b_im, a_im + b_re
                xp_re, xp_im = spec[at(base, i), ls].astype(f32), spec[at(base + Q, i), ls].astype(f32)
                xm_re, xm_im = spec[at(base + 2 * Q, i), ls].astype(f32), spec[at(base + 3 * Q, i), ls].astype(f32)
                acc[lb, at(0, i), hs] += xp_re * dp_re + xp_im * dp_im
                acc[lb, at(Q, i), hs] += xp_im * dp_re - xp_re * dp_im
                acc[lb, at(2 * Q, i), hs] += xm_re * dm_re + xm_im * dm_im
                acc[lb, at(3 * Q, i), hs] += xm_im * dm_re - xm_re * dm_im
                p_re, p_im = h_ref[lb, at(0, i), hs], h_ref[lb, at(Q, i), hs]
                q_re, q_im = h_ref[lb, at(2 * Q, i), hs], h_ref[lb, at(3 * Q, i), hs]
                yp_re, yp_im = p_re * dp_re + p_im * dp_im, p_re * dp_im - p_im * dp_re
                ym_re, ym_im = q_re * dm_re + q_im * dm_im, q_re * dm_im - q_im * dm_re
                yca[at(0, i), ls] = (yp_re + ym_re).astype(bf16)
                yca[at(Q + 16, i), ls] = (yp_im + ym_im).astype(bf16)
                ycb[at(0, i), ls] = (ym_im - yp_im).astype(bf16)
                ycb[at(Q, i), ls] = (yp_re - ym_re).astype(bf16)
            d_re, d_im = s_a[Q : Q + 16, ls], s_a[2 * Q + 16 : 2 * Q + 32, ls]
            x_re = spec[base + 4 * Q : base + 4 * Q + 16, ls].astype(f32)
            x_im = spec[base + 4 * Q + 16 : base + 4 * Q + 32, ls].astype(f32)
            acc[lb, 4 * Q : 4 * Q + 16, hs] += x_re * d_re + x_im * d_im
            acc[lb, 4 * Q + 16 : 4 * Q + 32, hs] += x_im * d_re - x_re * d_im
            p_re, p_im = h_ref[lb, 4 * Q : 4 * Q + 16, hs], h_ref[lb, 4 * Q + 16 : 4 * Q + 32, hs]
            yca[Q : Q + 16, ls] = (p_re * d_re + p_im * d_im).astype(bf16)
            yca[2 * Q + 16 : 2 * Q + 32, ls] = (p_re * d_im - p_im * d_re).astype(bf16)

    def context(t):
        for im, ls, hs in sub_tiles(t):
            ds = slice(C + hs.start, C + hs.stop)
            total = jnp.zeros((8, 128), f32)
            for i in range(HALF // 16):
                even, odd = s_e[at(0, i), ls], s_o[at(0, i), ls]
                top, bot = even + odd, even - odd
                dmer[at(im * IMG, i), ds] = top.astype(bf16)
                dmer[at(im * IMG + HALF, i), ds] = bot.astype(bf16)
                total = total + sum8(top) + sum8(bot)
            facc[:, ds] += total

    def phases(t):
        steps = [lambda: mean_grad(t)]
        for level in (2, 1, 0):
            steps += [
                lambda level=level: before(t, level),
                lambda: transform(t),
                lambda level=level: filt(t, level),
                lambda: back(t),
            ]
            if level == 2:
                steps.append(lambda: gate_grad(t))
        return steps + [lambda: context(t)]

    staggered(phases)
    gwf[...] += dot_tn(nb_ref[...], dmer[...])

    @pl.when(step == last)
    def _():
        for copy in late:
            copy.wait()
        facc[:, :C] = jnp.broadcast_to(sums[S_BQ : S_BQ + 1, :] * 0.125, (8, C))
        colsum = jnp.sum(facc[...], axis=0, keepdims=True)
        fsum[...] = jnp.broadcast_to(colsum, fsum.shape)
        wide = wf[...].astype(f32)
        t_hi, t_lo = split(wide * gwf[...])
        ones = jnp.ones((8, MERGED), bf16)
        gb[0:8, :] = dot_nt(ones, t_hi) + dot_nt(ones, t_lo)
        c_hi, c_lo = split(fsum[...])
        gb[8:16, :] = dot_nt(c_hi, wf[...]) + dot_nt(c_lo, wf[...])
        g1 = jnp.transpose(jnp.broadcast_to(vec[V_G1 : V_G1 + 1, :], (128, C)))
        b1 = jnp.transpose(jnp.broadcast_to(vec[V_B1 : V_B1 + 1, :], (128, C)))
        for t in range(MERGED // 128):
            ls = slice(128 * t, 128 * t + 128)
            gwf[:, ls] = gwf[:, ls] * g1 + b1 * fsum[0:1, ls]
        for level in range(3):
            total = None
            for lb in (level * 2, level * 2 + 1):
                hi, lo = split(acc[lb] * jnp.concatenate([weights[...]] * (C // 128), 1))
                first = dot(est[lb], hi)
                term = first[:TAPS] + first[TAPS:] + dot(est[lb, :TAPS, :], lo)
                total = term if total is None else total + term
            dk[level] = total
        pack_mod(gx, gy, mod_len, small_len, pos, gwf, gwh, gwp, sums, bsum, fsum, gb, dk, own, oth, flat, small, moved, spread)


def to_native(rows_ref, first, native, slot, slots, gain):
    line = GW * slots
    for y in range(GH):
        a = first + grid_rows(0, y)
        for lt in range(C // 128):
            v = rows_ref[a : a + GW, 128 * lt : 128 * lt + 128]
            native[lt, pl.ds(line * y + slot, GW, stride=slots), :] = v if gain is None else v * gain


def write_native(native, out, slots):
    line = GW * slots
    for y in range(GH):
        for lt in range(C // 128):
            v = native[lt, line * y : line * (y + 1), :].reshape(GW, slots, 128)
            out[y, :, :, 128 * lt : 128 * lt + 128] = v.astype(out.dtype)


def kernel_tail(dmer, wf, x_ref, stat, dmid, vec, gtok_o, stage, native):
    step = pl.program_id(0)
    slots = gtok_o.shape[2]
    g1 = vec[V_G1 : V_G1 + 1, :]
    d_normed = dot_nt(dmer[...], wf[...])
    for i in range(PAIR // 32):
        s = at(0, i, 32)
        r = stat[s, 1:2]
        n = (x_ref[s, :].astype(f32) - stat[s, 0:1]) * r
        e = d_normed[s, :] * g1
        dv = e - jnp.mean(e, axis=-1, keepdims=True) - n * jnp.mean(e * n, axis=-1, keepdims=True)
        stage[s, :] = dmid[s, :] + r * dv
    for im in range(2):
        to_native(stage, im * IMG, native, step * 2 + im, slots, None)

    @pl.when(step == pl.num_programs(0) - 1)
    def _():
        write_native(native, gtok_o, slots)


def kernel_out(counts, rows_ref, out_o, native, wide):
    slots = out_o.shape[2]
    wide[...] = rows_ref[...].astype(f32)
    for im in range(slots):
        to_native(wide, im * IMG, native, im, slots, (im < counts[0]).astype(f32))
    write_native(native, out_o, slots)


def block_rows(length):
    return 8 * (length // 1024 if length % 1024 == 0 else (length + 1022) // 1024 + 1)


def place(shard, device):
    length = shard.shape[0]
    n = block_rows(length) * 128
    if n == length:
        return shard.reshape(-1, 128)
    offset = lax.rem(device * length, 1024)
    return lax.dynamic_update_slice(jnp.zeros((n,), shard.dtype), shard, (offset,)).reshape(-1, 128)


def take(block, length, device):
    flat = block.reshape(-1)
    if flat.shape[0] == length:
        return flat
    return lax.dynamic_slice(flat, (lax.rem(device * length, 1024),), (length,))


def first_row(length, device):
    return pl.multiple_of((device * length) // 1024 * 8, 8)


def device_at(pos, gy, i, j, c):
    return (pos[0] ^ j) * gy + (pos[1] ^ (2 * i + c))


def join(first, second, sh):
    lane = lax.broadcasted_iota(jnp.int32, first.shape, 1)
    return jnp.where(lane < 128 - sh, first, second)


def turn(v, sh):
    return pltpu.roll(v, 128 - sh, 1) if sh else v


def shift_right(first, second, sh):
    lane = lax.broadcasted_iota(jnp.int32, first.shape, 1)
    return jnp.where(lane < sh, pltpu.roll(first, sh, 1), pltpu.roll(second, sh, 1))


WIDE = C2 + 4
WF_ROWS = C * WIDE // 128
W_ROWS = C * C // 128
PERIOD = 32
STRIDE = PERIOD * WIDE // 128
K_ROW = 12
TAIL_ROW = K_ROW + 83 * C // 128
B_HB, B_PB, B_S1, B_G2, B_B2, B_BM1 = (TAIL_ROW + 3 * k for k in range(6))
B_BM2 = B_BM1 + HID // 128
B_S2 = B_BM2 + 3
END_ROW = B_S2 + 3


def unpack_mod(gx, gy, mod_len, small_len, pos, own, oth, wf_o, wh_o, wp_o, vec_o, bm1_o, kcat_o, flat, small, moved, wide):
    flat[...] = jnp.zeros_like(flat)
    small[...] = jnp.zeros_like(small)
    mr, sr = block_rows(mod_len), block_rows(small_len)
    for i in range(gy // 2):
        for j in range(gx):
            for c, src in enumerate((own, oth)):
                d = device_at(pos, gy, i, j, c)
                block = src[i, j].astype(f32)
                flat[pl.ds(first_row(mod_len, d), mr), :] += block[:mr]
                small[pl.ds(first_row(small_len, d), sr), :] += block[mr : mr + sr]
    lane = lax.broadcasted_iota(jnp.int32, (16, 128), 1)
    for p in range(PERIOD):
        row, sh = WIDE * p // 128, WIDE * p % 128
        tiles = [turn(flat[pl.ds(row + j, 16, stride=STRIDE), :], sh) for j in range(MERGED // 128 + (1 if sh else 0))]
        for j in range(MERGED // 128):
            v = join(tiles[j], tiles[j + 1], sh) if sh else tiles[j]
            if j == MERGED // 128 - 1:
                v = jnp.where(lane < 4, v, 0.0)
            wide[j, pl.ds(p, 16, stride=PERIOD), :] = v
    for j in range(MERGED // 128):
        wf_o[:, 128 * j : 128 * j + 128] = wide[j, :C, :].astype(bf16)
    for j in range(3):
        ls = slice(128 * j, 128 * j + 128)
        wh_o[:, ls] = flat[pl.ds(WF_ROWS + j, C, stride=3), :].astype(bf16)
        wp_o[:, ls] = flat[pl.ds(WF_ROWS + W_ROWS + j, C, stride=3), :].astype(bf16)
    n = moved.shape[0]
    moved[...] = join(turn(small[0:n, :], 4), turn(small[1 : n + 1, :], 4), 4)
    vec_o[...] = jnp.zeros_like(vec_o)
    for row, src, start in (
        (V_G1, small, 0), (V_B1, small, 3), (V_BQ, small, 6), (V_BC, small, 9),
        (V_HB, moved, B_HB), (V_PB, moved, B_PB), (V_S1, moved, B_S1), (V_G2, moved, B_G2), (V_B2, moved, B_B2),
        (V_BM2, moved, B_BM2), (V_S2, moved, B_S2),
    ):
        for j in range(3):
            vec_o[row : row + 1, 128 * j : 128 * j + 128] = src[start + j : start + j + 1, :]
    vec_o[V_BG : V_BG + 1, 0:128] = jnp.where(lane[0:1] < 4, small[K_ROW : K_ROW + 1, :], 0.0)
    for t in range(HID // 128):
        bm1_o[:, 128 * t : 128 * t + 128] = jnp.broadcast_to(moved[B_BM1 + t : B_BM1 + t + 1, :], (8, 128))
    start = 0
    for level, k in enumerate(LEVELS):
        for j in range(3):
            taps = moved[pl.ds(K_ROW + 3 * start + j, TAPS, stride=3), :].astype(bf16)
            kcat_o[level, 0:TAPS, 128 * j : 128 * j + 128] = taps
            kcat_o[level, TAPS:, 128 * j : 128 * j + 128] = taps
        start += k * k


def unpack_mlp(gx, gy, mlp_len, pos, blocks, w1_o, w2_o, flat):
    mr = block_rows(mlp_len)
    aligned = mr * 128 == mlp_len
    if not aligned:
        flat[...] = jnp.zeros_like(flat)
    for i, src in enumerate(blocks):
        for j in range(gx):
            for c in range(2):
                rows_at = pl.ds(first_row(mlp_len, device_at(pos, gy, i, j, c)), mr)
                if aligned:
                    flat[rows_at, :] = src[c, j].astype(f32)
                else:
                    flat[rows_at, :] += src[c, j].astype(f32)
    for t in range(HID // 128):
        w1_o[:, 128 * t : 128 * t + 128] = flat[pl.ds(t, C, stride=HID // 128), :].astype(bf16)
    for t in range(C // 128):
        w2_o[:, 128 * t : 128 * t + 128] = flat[pl.ds(C * HID // 128 + t, HID, stride=C // 128), :].astype(bf16)


def send_slots(gx, gy, pos, flat, length, base, own, oth):
    mr = block_rows(length)
    for i in range(gy // 2):
        for j in range(gx):
            for c, dst in enumerate((own, oth)):
                d = device_at(pos, gy, i, j, c)
                dst[i, j, base : base + mr, :] = flat[pl.ds(first_row(length, d), mr), :].astype(bf16)


def pack_mlp(gx, gy, mlp_len, pos, gw1, gw2, own, oth, flat):
    used = 2 * C * HID // 128
    if flat.shape[0] > used:
        flat[used:, :] = jnp.zeros_like(flat[used:, :])
    for t in range(HID // 128):
        flat[pl.ds(t, C, stride=HID // 128), :] = gw1[:, 128 * t : 128 * t + 128]
    for t in range(C // 128):
        flat[pl.ds(C * HID // 128 + t, HID, stride=C // 128), :] = gw2[:, 128 * t : 128 * t + 128]
    send_slots(gx, gy, pos, flat, mlp_len, 0, own, oth)


def pack_mod(gx, gy, mod_len, small_len, pos, gwf, gwh, gwp, sums, bsum, fsum, gb, dk, own, oth, flat, small, moved, wide):
    lane = lax.broadcasted_iota(jnp.int32, (16, 128), 1)
    used = WF_ROWS + 2 * W_ROWS
    if flat.shape[0] > used:
        flat[used:, :] = jnp.zeros_like(flat[used:, :])
    for j in range(MERGED // 128):
        wide[j, :C, :] = gwf[:, 128 * j : 128 * j + 128]
    turned = {}

    def piece(p, tile):
        tile = min(tile, MERGED // 128 - 1)
        if (p, tile) not in turned:
            turned[p, tile] = turn(wide[tile, pl.ds(p, 16, stride=PERIOD), :], -WIDE * p % 128)
        return turned[p, tile]

    for f in range(STRIDE):
        p = 128 * f // WIDE
        col = 128 * f - WIDE * p
        t, sh = col // 128, col % 128
        v = join(piece(p, t), piece(p, t + 1), sh) if sh else piece(p, t)
        left = WIDE - col
        if left < 128:
            v = jnp.where(lane < left, v, piece(p + 1, 0))
        flat[pl.ds(f, 16, stride=STRIDE), :] = v
    for j in range(3):
        ls = slice(128 * j, 128 * j + 128)
        flat[pl.ds(WF_ROWS + j, C, stride=3), :] = gwh[:, ls]
        flat[pl.ds(WF_ROWS + W_ROWS + j, C, stride=3), :] = gwp[:, ls]
    moved[...] = jnp.zeros_like(moved)
    small[...] = jnp.zeros_like(small)
    start = 0
    for level, k in enumerate(LEVELS):
        for j in range(3):
            moved[pl.ds(K_ROW + 3 * start + j, k * k, stride=3), :] = dk[level, 0 : k * k, 128 * j : 128 * j + 128]
        start += k * k
    for start, row in (
        (B_HB, S_HB), (B_PB, S_PB), (B_S1, S_S1), (B_G2, S_G2), (B_B2, S_B2), (B_BM2, S_BM2), (B_S2, S_S2),
    ):
        for j in range(3):
            moved[start + j : start + j + 1, :] = sums[row : row + 1, 128 * j : 128 * j + 128]
    for t in range(HID // 128):
        moved[B_BM1 + t : B_BM1 + t + 1, :] = bsum[0:1, 128 * t : 128 * t + 128]
    n = moved.shape[0]
    small[8:n, :] = shift_right(moved[7 : n - 1, :], moved[8:n, :], 4)
    for j in range(3):
        ls = slice(128 * j, 128 * j + 128)
        small[j : j + 1, :] = gb[0:1, ls]
        small[3 + j : 4 + j, :] = gb[8:9, ls]
        small[6 + j : 7 + j, :] = fsum[0:1, ls]
        small[9 + j : 10 + j, :] = fsum[0:1, C + 128 * j : C + 128 * j + 128]
    gate_lane = lane[0:1] < 4
    small[K_ROW : K_ROW + 1, :] = jnp.where(gate_lane, fsum[0:1, C2:], small[K_ROW : K_ROW + 1, :])
    mr, sr = block_rows(mod_len), block_rows(small_len)
    send_slots(gx, gy, pos, flat, mod_len, 0, own, oth)
    for i in range(gy // 2):
        for j in range(gx):
            for c, dst in enumerate((own, oth)):
                block = small[pl.ds(first_row(small_len, device_at(pos, gy, i, j, c)), sr), :]
                pad = own.shape[2] - mr - sr
                if pad:
                    block = jnp.concatenate([block, jnp.zeros((pad, 128), f32)], 0)
                dst[i, j, mr:, :] = block.astype(bf16)


def kernel_add(n_in, *refs):
    for k, o in enumerate(refs[n_in:]):
        total = None
        for ref in refs[:n_in]:
            v = ref[k].astype(f32)
            total = v if total is None else total + v
        o[...] = total.astype(o.dtype)


def kernel_cut(cuts, *refs):
    outs = refs[-len(cuts) :]
    for o, (first, n) in zip(outs, cuts):
        total = None
        for ref in refs[: -len(cuts)]:
            v = ref[first : first + n, :].astype(f32)
            total = v if total is None else total + v
        o[...] = total


def full(shape):
    return pl.BlockSpec(shape, lambda *i, n=len(shape): (0,) * n)


def rows(n, width):
    return pl.BlockSpec((n, width), lambda i: (i, 0))


def smem():
    return pl.BlockSpec(memory_space=pltpu.SMEM)


def sds(shape, dtype):
    return jax.ShapeDtypeStruct(shape, dtype)


def call(kernel, name, grid, ins, outs, scratch, mib, micros):
    return pl.pallas_call(
        kernel,
        grid=grid,
        in_specs=[s for _, s in ins],
        out_shape=[o for o, _ in outs],
        out_specs=[s for _, s in outs],
        scratch_shapes=[pltpu.VMEM(*v) if isinstance(v, tuple) else v for v in scratch],
        compiler_params=pltpu.CompilerParams(vmem_limit_bytes=mib * 2**20),
        cost_estimate=pl.CostEstimate(flops=int(micros * 1e9), bytes_accessed=int(micros * 1e6), transcendentals=0),
        name=name,
    )(*[a for a, _ in ins])


def whole(*arrays):
    return [(a, full(a.shape)) for a in arrays]


def by_rows(n, *arrays):
    return [(a, rows(n, a.shape[1])) for a in arrays]


def native_rows(slots):
    return ((C // 128, GH * GW * slots, 128), f32)


def prep(tokens):
    slots = tokens.shape[2]
    n = slots * IMG
    outs = [(sds((n, w), t), rows(PAIR, w)) for w, t in ((C, bf16), (C, bf16), (128, f32))]
    return call(kernel_prep, "prep", (slots // 2,), whole(tokens), outs, [native_rows(slots), ((PAIR, C), f32)], 60, 5)


def upstream(counts, cotangent):
    slots = cotangent.shape[2]
    ins = [(counts, smem())] + whole(cotangent)
    outs = [(sds((slots * IMG, C), bf16), rows(PAIR, C))]
    return call(kernel_upstream, "upstream", (slots // 2,), ins, outs, [native_rows(slots), ((PAIR, C), f32)], 60, 4)[0]


def forward(gx, gy, pos, xrow, stat, bucket, own, oth, mod_len, small_len):
    con = constants()
    pairs = xrow.shape[0] // PAIR
    n = pairs * PAIR
    outs = [
        (sds((n, C), f32), rows(PAIR, C)),
        (sds((n, GATES), f32), rows(PAIR, GATES)),
        (sds((n, C), bf16), rows(PAIR, C)),
        (sds((pairs * 3 * IMG, C2), bf16), rows(3 * IMG, C2)),
        (sds((pairs * 3 * IMG, C2), bf16), rows(3 * IMG, C2)),
        (sds((pairs * 3 * SR, C2), bf16), rows(3 * SR, C2)),
        (sds((pairs * 8, C2), f32), rows(8, C2)),
    ]
    weights = [((C, MERGED), bf16), ((C, C), bf16), ((C, C), bf16), ((VROWS, C), f32), ((8, HID), f32), ((3, 2 * TAPS, C), bf16)]
    outs += [(sds(shape, dtype), full(shape)) for shape, dtype in weights]
    mats = [jnp.asarray(con[k]) for k in ("es", "fe", "fo", "ge", "go")]
    ins = [(bucket, smem()), (pos, smem())] + by_rows(PAIR, xrow, stat) + whole(own, oth, *mats)
    scratch = [
        ((6, SR, C), f32), ((PAIR, C), bf16), ((PAIR, C), f32), ((3 * HALF, C2), bf16), ((3 * HALF, C2), bf16), ((AR, C2), f32), ((BR, C2), f32),
        ((HALF, C2), f32), ((HALF, C2), f32), ((3 * AR, C2), bf16), ((3 * BR, C2), bf16), ((PAIR, C), f32),
        ((4, PAIR, 128), f32),
    ]
    ndev = gx * gy
    flat_rows = max(span(mod_len, ndev), STRIDE * 16 + 8)
    small_rows = max(span(small_len, ndev), END_ROW + 26)
    scratch += [((flat_rows, 128), f32), ((small_rows + 8, 128), f32), ((small_rows, 128), f32)]
    scratch += [((MERGED // 128, PERIOD * 16, 128), f32)]
    kernel = functools.partial(kernel_forward, gx, gy, mod_len, small_len)
    return call(kernel, "focal_forward", (pairs,), ins, outs, scratch, 62, 28)


def middle(gx, gy, pos, xrow, up, mixed, q, wh, wp, vec, bm1, mlp_blocks, mlp_len):
    n = xrow.shape[0]
    outs = [
        (sds((n, C), f32), rows(BROWS, C)),
        (sds((n, C), bf16), rows(BROWS, C)),
        (sds((n, C), bf16), rows(BROWS, C)),
        (sds((n, C), f32), rows(BROWS, C)),
    ]
    slots = (gy // 2, gx, block_rows(mlp_len), 128)
    outs += [(sds(slots, bf16), full(slots))] * 2
    outs += [(sds(s, f32), full(s)) for s in ((C, C), (C, C), (8, C), (8, HID))]
    ins = [(pos, smem())] + by_rows(BROWS, xrow, up, mixed, q) + whole(wh, wp, vec, bm1, *mlp_blocks)
    blk = (BROWS, C)
    scratch = [
        (blk, f32), (blk, bf16), (blk, f32), (blk, f32), (blk, bf16), (blk, bf16), (blk, f32), (blk, f32),
        ((BROWS, HID), bf16), ((BROWS, HID), bf16), ((2, BROWS, HCHUNK), f32), ((2, BROWS, HCHUNK), f32), (blk, bf16), (blk, bf16), (blk, f32),
        ((8, 8, C), f32), ((8, HID), f32),
        ((C, HID), f32), ((HID, C), f32), ((span(mlp_len, gx * gy), 128), f32), ((C, HID), bf16), ((HID, C), bf16),
    ]
    kernel = functools.partial(kernel_middle, gx, gy, mlp_len)
    return call(kernel, "middle", (n // BROWS,), ins, outs, scratch, 62, 42)


def backward(gx, gy, pos, bucket, nb, dq, dmix, gates, z, g, spec, mean, kcat, wf, vec, sums, bsum, gwh, gwp, mod_len, small_len):
    con = constants()
    ndev = gx * gy
    pairs = nb.shape[0] // PAIR
    mats = [jnp.asarray(con[k]) for k in ("es", "weights")]
    mats += [jnp.asarray(con["fe"][:, :HALF]), jnp.asarray(con["fo"][:, :HALF])]
    mats += [jnp.asarray(con["ge"][:, :AR]), jnp.asarray(con["go"][:, :BR])]
    slots = (gy // 2, gx, -(-(block_rows(mod_len) + block_rows(small_len)) // 16) * 16, 128)
    outs = [(sds((nb.shape[0], MERGED), bf16), rows(PAIR, MERGED))] + [(sds(slots, bf16), full(slots))] * 2
    ins = [(bucket, smem()), (pos, smem())] + by_rows(PAIR, nb, dq, dmix, gates) + by_rows(3 * IMG, z, g) + by_rows(3 * SR, spec)
    ins += by_rows(8, mean) + whole(kcat, vec, sums, bsum, *mats)
    late = (wf, gwh, gwp, jnp.asarray(con["est"]))
    ins += [(v, pl.BlockSpec(memory_space=pl.ANY)) for v in late]
    small_rows = -(-max(span(small_len, ndev), END_ROW + 2) // 8) * 8
    scratch = [
        ((C, MERGED), f32), ((8, MERGED), f32), ((16, C), f32), ((3, TAPS, C), f32), ((6, SR, C), f32),
        ((HALF, C2), bf16), ((HALF, C2), bf16), ((AR, C2), f32), ((BR, C2), f32), ((HALF, C2), f32), ((HALF, C2), f32),
        ((AR, C2), bf16), ((BR, C2), bf16), ((6, SR, C), f32), ((8, MERGED), f32), ((4, PAIR, 128), f32),
        ((max(span(mod_len, ndev), STRIDE * 16 + 8), 128), f32), ((small_rows, 128), f32), ((small_rows, 128), f32),
        ((MERGED // 128, PERIOD * 16, 128), f32),
    ]
    scratch += [(v.shape, v.dtype) for v in late] + [pltpu.SemaphoreType.DMA((len(late),))]
    kernel = functools.partial(kernel_backward, gx, gy, mod_len, small_len)
    return call(kernel, "focal_backward", (pairs,), ins, outs, scratch, 62, 28)


def tail(shape, dmer, wf, xrow, stat, dmid, vec):
    slots = shape[2]
    ins = by_rows(PAIR, dmer) + whole(wf) + by_rows(PAIR, xrow, stat, dmid) + whole(vec)
    return call(kernel_tail, "tail", (slots // 2,), ins, [(sds(shape, f32), full(shape))], [((PAIR, C), f32), native_rows(slots)], 24, 8)[0]


def out_tokens(shape, counts, out_rows):
    ins = [(counts, smem())] + whole(out_rows)
    return call(kernel_out, "out_tokens", (), ins, [(sds(shape, bf16), full(shape))], [native_rows(shape[2]), ((shape[2] * IMG, C), f32)], 24, 5)[0]


def span(length, ndev):
    return ((ndev - 1) * length) // 1024 * 8 + block_rows(length)


def add(arrays, outs, name):
    return call(functools.partial(kernel_add, len(arrays)), name, (), whole(*arrays), [(o, full(o.shape)) for o in outs], [], 24, 2)


def swap(x, mask, ndev):
    return lax.ppermute(x, AXES, [(k, k ^ mask) for k in range(ndev)])


def around(x, step, count, ndev):
    return [x] + [swap(x, step * k, ndev) for k in range(1, count)]


def after(values):
    return lax.optimization_barrier(values)


def travel(parts, step, ndev):
    return [parts[0]] + [swap(p, step * k, ndev) for k, p in enumerate(parts) if k]


def sum_core(own, oth, gx, gy, name):
    got = swap(oth, 1, gx * gy)
    return add([own, got], [sds(own.shape[1:], f32 if k == 0 else bf16) for k in range(gy // 2)], name + "_sum_core")


def sum_plane(parts, gx, name):
    shape = parts[0].shape[1:]
    return add(parts, [sds(shape, f32 if k == 0 else bf16) for k in range(gx)], name + "_sum_plane")


def sum_line(parts, cuts, name):
    outs = [(sds((n, 128), f32), full((n, 128))) for _, n in cuts]
    return call(functools.partial(kernel_cut, cuts), name + "_sum_line", (), whole(*parts), outs, [], 24, 2)


def local(gx, gy, tokens, bucket, counts, mod_weights, mlp_weights, small_params, cotangent):
    ndev = gx * gy
    gxi, gyi = lax.axis_index("gx"), lax.axis_index("gy")
    device = gxi * gy + gyi
    pos = jnp.stack([gxi, gyi]).astype(jnp.int32)
    mod_len, small_len, mlp_len = mod_weights.shape[0], small_params.shape[0], mlp_weights.shape[0]
    mr, sr = block_rows(mod_len), block_rows(small_len)

    blocks = [place(mod_weights, device), place(small_params, device)]
    pad = -(mr + sr) % 16
    if pad:
        blocks.append(jnp.zeros((pad, 128), bf16))
    line = around(jnp.concatenate(blocks, 0), gy, gx, ndev)
    native, back = (1, 2, 0, 3), (2, 0, 1, 3)
    shape = (GH, GW) + tokens.shape[:1] + (C,)
    prepared = prep(jnp.transpose(tokens, native))
    line, mlp_mine, prepared = after((line, place(mlp_weights, device), prepared))
    xrow, nb, stat = prepared
    plane = around(jnp.stack(line), 2, gy // 2, ndev)
    mlp_line = jnp.stack(around(mlp_mine, gy, gx, ndev))
    up = upstream(counts, jnp.transpose(cotangent, native))
    plane, mlp_line, up = after((plane, mlp_line, up))
    mlp_other = swap(mlp_line, 1, ndev)
    plane = jnp.stack(plane)
    other = swap(plane, 1, ndev)
    mlp_both = jnp.stack([mlp_line, mlp_other])
    other, mlp_both = after((other, mlp_both))
    mlp_blocks = around(mlp_both, 2, gy // 2, ndev)

    q, gates, mixed, z, g, spec, mean, wf, wh, wp, vec, bm1, kcat = forward(
        gx, gy, pos, xrow, stat, bucket, plane, other, mod_len, small_len
    )
    mlp_blocks, mixed = after((mlp_blocks, mixed))
    dmid, out_rows, dq, dmix, own, oth, gwh, gwp, sums, bsum = middle(
        gx, gy, pos, xrow, up, mixed, q, wh, wp, vec, bm1, mlp_blocks, mlp_len
    )
    parts = sum_core(own, oth, gx, gy, "mlp")
    parts, dmix = after((parts, dmix))
    mlp_plane = travel(parts, 2, ndev)
    dmer, own, oth = backward(
        gx, gy, pos, bucket, nb, dq, dmix, gates, z, g, spec, mean, kcat, wf, vec, sums, bsum, gwh, gwp, mod_len, small_len
    )
    mlp_plane, own, oth = after((mlp_plane, own, oth))
    parts = sum_plane(mlp_plane, gx, "mlp")
    mod_parts = sum_core(own, oth, gx, gy, "mod")
    mlp_line = travel(parts, gy, ndev)
    mod_plane = travel(mod_parts, 2, ndev)
    gtok = tail(shape, dmer, wf, xrow, stat, dmid, vec)
    mod_plane, mlp_line, gtok, out_rows = after((mod_plane, mlp_line, gtok, out_rows))
    mod_line = travel(sum_plane(mod_plane, gx, "mod"), gy, ndev)
    grad_mlp = take(sum_line(mlp_line, [(0, mlp_line[0].shape[0])], "mlp")[0], mlp_len, device)
    out = out_tokens(shape, counts, out_rows)
    mod_line, out, grad_mlp = after((mod_line, out, grad_mlp))
    total_mod, total_small = sum_line(mod_line, [(0, mr), (mr, sr)], "mod")
    grad_mod = take(total_mod, mod_len, device)
    grad_small = take(total_small, small_len, device)
    return jnp.transpose(out, back), jnp.transpose(gtok, back), grad_mod, grad_mlp, grad_small


def solution(mesh):
    images = P(AXES, None, None, None)
    flat = P(AXES)
    return jax.shard_map(
        functools.partial(local, mesh.shape["gx"], mesh.shape["gy"]),
        mesh=mesh,
        in_specs=(images, flat, flat, flat, flat, flat, images),
        out_specs=(images, images, flat, flat, flat),
        check_vma=False,
    )
```

```python
import functools

import jax
import jax.numpy as jnp
import numpy as np
from jax import lax
from jax.experimental import pallas as pl
from jax.experimental.pallas import tpu as pltpu
from jax.sharding import PartitionSpec as P

C = 384
HID = 1536
GH = 14
GW = 20
HALF = 144
IMG = 2 * HALF
PAIR = 2 * IMG
C2 = 2 * C
NY = 17
NX = 23
NV = 12
NU = 8
Q = NU * NV
AR = 2 * (Q + 16)
BR = 2 * Q
SR = 4 * Q + 32
LEVELS = (3, 5, 7)
TAPS = 64
GATES = 128
MERGED = C2 + GATES
BROWS = 768
HCHUNK = 512
AXES = ("gx", "gy")
f32 = jnp.float32
bf16 = jnp.bfloat16
EPS = 1e-05
ROOT_HALF = 0.7071067811865476
INV_ROOT_2PI = 0.3989422804014327
LOG2_E = 1.4426950408889634


def _hi(a):
    return a.astype(bf16)


def _lo(a):
    return (a - a.astype(bf16).astype(np.float64)).astype(bf16)


def three(a):
    return np.concatenate([_hi(a), _lo(a), _hi(a)], 1)


@functools.lru_cache(maxsize=None)
def constants():
    row = np.arange(HALF)
    real = (row < 7 * GW).astype(np.float64)
    yy = np.minimum(row // GW, 6) - (GH - 1) / 2
    xx = row % GW - (GW - 1) / 2
    uv = [(u, v) for u in range(1, NU + 1) for v in range(NV)]
    u0 = [(0, v) for v in range(NV)]
    wu = 2 * np.pi / NY
    wv = 2 * np.pi / NX

    def trig(pairs, pad):
        u = np.array([p[0] for p in pairs] + [0] * pad, np.float64)[:, None]
        v = np.array([p[1] for p in pairs] + [0] * pad, np.float64)[:, None]
        use = np.array([1.0] * len(pairs) + [0.0] * pad)[:, None] * real[None]
        cy, sy = np.cos(wu * u * yy) * use, np.sin(wu * u * yy) * use
        cx, sx = np.cos(wv * v * xx), np.sin(wv * v * xx)
        weight = np.where(u > 0, 2.0, 1.0) * np.where(v > 0, 2.0, 1.0) / (NY * NX)
        return cy * cx, -cy * sx, sy * cx, -sy * sx, weight

    e_re, e_im, o_re, o_im, w1 = trig(uv, 0)
    z_re, z_im, _, _, w0 = trig(u0, 16 - NV)
    fe = np.concatenate([e_re, z_re, e_im, z_im], 0)
    fo = np.concatenate([o_re, o_im], 0)
    half = np.concatenate([0.5 * w1, w0, 0.5 * w1, w0], 0)
    ge = (fe * half).T
    go = (fo * np.concatenate([0.5 * w1, 0.5 * w1], 0)).T

    u = np.array([p[0] for p in uv], np.float64)[:, None]
    v = np.array([p[1] for p in uv], np.float64)[:, None]
    v0 = np.array(list(range(NV)) + [0] * (16 - NV), np.float64)[:, None]
    use0 = np.array([1.0] * NV + [0.0] * (16 - NV))[:, None]
    wp = np.where(v > 0, 2.0, 1.0) / (NY * NX)
    wz = np.where(v0 > 0, 2.0, 1.0) * use0 / (NY * NX)
    weights = np.concatenate([wp, -wp, wp, -wp, wz, -wz], 0)
    es = []
    for k in LEVELS:
        h = k // 2
        ty, tx = np.meshgrid(np.arange(k) - h, np.arange(k) - h, indexing="ij")
        for bucket in (0, 1):
            sy, sx = (ty, tx) if bucket == 0 else (tx, ty)
            py = sy.reshape(1, -1) * wu
            px = sx.reshape(1, -1) * wv
            plus = u * py + v * px
            minus = -u * py + v * px
            zero = v0 * px
            e = [np.cos(plus), np.sin(plus), np.cos(minus), np.sin(minus), np.cos(zero) * use0, np.sin(zero) * use0]
            whole_e = np.zeros((SR, TAPS))
            whole_e[:, : k * k] = np.concatenate(e, 0)
            es.append(np.concatenate([_hi(whole_e), _lo(whole_e)], 1))
    return dict(
        fe=three(fe),
        fo=three(fo),
        ge=three(ge * ROOT_HALF),
        go=three(go * ROOT_HALF),
        fe_back=_hi(fe * ROOT_HALF),
        fo_back=_hi(fo * ROOT_HALF),
        ge_back=_hi(ge),
        go_back=_hi(go),
        es=np.stack(es),
        est=np.stack([np.ascontiguousarray(e.T) for e in es]),
        weights=np.broadcast_to(weights, (SR, 128)).astype(np.float32),
    )


def dot(a, b):
    return jnp.dot(a, b, preferred_element_type=f32)


def dot_nt(a, b):
    return lax.dot_general(a, b, (((1,), (1,)), ((), ())), preferred_element_type=f32)


def dot_tn(a, b):
    return lax.dot_general(a, b, (((0,), (0,)), ((), ())), preferred_element_type=f32)


def gelu_pair(x):
    cdf = 0.5 * lax.erf(x * ROOT_HALF) + 0.5
    return x * cdf, cdf + x * (jnp.exp2(x * x * (-0.5 * LOG2_E)) * INV_ROOT_2PI)


def gelu_scaled(u):
    w = lax.erf(u) * ROOT_HALF + ROOT_HALF
    return u * w, w + u * (jnp.exp2(u * u * -LOG2_E) * (2 * INV_ROOT_2PI))


def split(x):
    hi = x.astype(bf16)
    return hi, (x - hi.astype(f32)).astype(bf16)


def at(base, i, n=16):
    return slice(base + i * n, base + i * n + n)


def weave(products, vector):
    n, m = len(products), len(vector)
    done = 0
    for k, step in enumerate(products):
        step()
        upto = (k + 1) * m // n
        for other in vector[done:upto]:
            other()
        done = upto


def norm_stats(x):
    mean = jnp.mean(x, axis=-1, keepdims=True)
    centred = x - mean
    var = jnp.mean(centred * centred, axis=-1, keepdims=True)
    r = lax.rsqrt(var + EPS)
    return centred * r, r


def sum8(x):
    total = x[0:8]
    for k in range(1, x.shape[0] // 8):
        total = total + x[8 * k : 8 * k + 8]
    return total


def grid_rows(im, y):
    return im * IMG + (y * GW if y < 7 else HALF + (GH - 1 - y) * GW)


def lanes(im):
    return slice(im * C, im * C + C)


(V_G1, V_B1, V_BQ, V_BC, V_HB, V_PB, V_S1, V_G2, V_B2, V_BM2, V_S2, V_BG) = range(12)
VROWS = 16
(S_HB, S_PB, S_S1, S_G2, S_B2, S_BM2, S_S2, S_BQ) = range(8)


def from_native(src, field):
    slots = src.shape[2]
    for lt in range(C // 128):
        for im in range(slots):
            for h in (GH // 2 * GW, HALF + GH // 2 * GW):
                field[lt, im * PITCH_IMAGE + h : im * PITCH_IMAGE + h + 4, :] = jnp.zeros((4, 128), f32)
        for y in range(GH):
            for x in range(GW):
                v = src[y, x, :, 128 * lt : 128 * lt + 128].astype(f32)
                field[lt, pl.ds(grid_rows(0, y) + x, slots, stride=PITCH_IMAGE), :] = v


def field_rows(field, first, n):
    s = pl.ds(pl.multiple_of(first, 8), n)
    return jnp.concatenate([field[lt, s, :] for lt in range(C // 128)], axis=1)


def kernel_prep(x_ref, xrow_o, nb_o, stat_o, field):
    step = pl.program_id(0)

    @pl.when(step == 0)
    def _():
        from_native(x_ref, field)

    lane = lax.broadcasted_iota(jnp.int32, (32, 128), 1)
    for k in range(PAIR // 32):
        s = at(0, k, 32)
        x = field_rows(field, (step * 2 + k // (IMG // 32)) * PITCH_IMAGE + 32 * (k % (IMG // 32)), 32)
        xrow_o[s, :] = x.astype(bf16)
        mean = jnp.mean(x, axis=-1, keepdims=True)
        centred = x - mean
        r = lax.rsqrt(jnp.mean(centred * centred, axis=-1, keepdims=True) + EPS)
        nb_o[s, :] = (centred * r).astype(bf16)
        stat_o[s, :] = jnp.where(lane == 0, mean, r)


def kernel_upstream(counts, cot_ref, up_o, field):
    step = pl.program_id(0)

    @pl.when(step == 0)
    def _():
        from_native(cot_ref, field)

    for im in range(2):
        live = (step * 2 + im < counts[0]).astype(f32)
        for i in range(IMG // 32):
            v = field_rows(field, (step * 2 + im) * PITCH_IMAGE + 32 * i, 32)
            up_o[at(im * IMG, i, 32), :] = (v * live).astype(bf16)


CHAINS = 3
CHAIN = C2 // CHAINS


def staggered(phases):
    lists = [phases(t) for t in range(CHAINS)]
    for turn in range(len(lists[0]) + CHAINS - 1):
        for t in range(CHAINS):
            if 0 <= turn - t < len(lists[t]):
                lists[t][turn - t]()


def sub_tiles(t):
    for k in range(t * CHAIN // 128, (t + 1) * CHAIN // 128):
        lt = k % (C // 128)
        yield k // (C // 128), slice(128 * k, 128 * k + 128), slice(128 * lt, 128 * lt + 128)


def spread_gates(gates, wide):
    for k in range(4):
        for i in range(PAIR // 32):
            s = at(0, i, 32)
            wide[k, s, :] = jnp.broadcast_to(gates[s, k : k + 1], (32, 128))


def kernel_forward(
    gx, gy, mod_len, small_len, bucket, pos, x_ref, stat, own, oth, es, fe, fo, ge, go,
    q_o, gates_o, mixed_o, z_o, g_o, spec_o, mean_o, wf, wh, wp, vec, bm1, kcat,
    h_o, normed, ctx, ecat, ocat, s_a, s_b, s_e, s_o, yca, ycb, mix, wide, flat, small, moved, spread, turned,
):
    step = pl.program_id(0)

    @pl.when(step == 0)
    def _():
        unpack_mod(gx, gy, mod_len, small_len, pos, own, oth, wf, wh, wp, vec, bm1, kcat, flat, small, moved, spread, turned)
        for lb in range(6):
            h_o[lb] = dot(es[lb], kcat[lb // 2])

    g1, b1 = vec[V_G1 : V_G1 + 1, :], vec[V_B1 : V_B1 + 1, :]
    for i in range(PAIR // 32):
        s = at(0, i, 32)
        n = (x_ref[s, :].astype(f32) - stat[s, 0:1]) * stat[s, 1:2]
        normed[s, :] = (n * g1 + b1).astype(bf16)
    right = dot(normed[...], wf[:, C + 128 :])
    left = dot(normed[...], wf[:, : C + 128])
    ctx[:, :128] = left[:, C:] + vec[V_BC : V_BC + 1, :128]
    ctx[:, 128:] = right[:, : C - 128] + vec[V_BC : V_BC + 1, 128:]
    gates_o[...] = right[:, C - 128 :] + vec[V_BG : V_BG + 1, :GATES]
    q_o[...] = left[:, :C] + vec[V_BQ : V_BQ + 1, :]
    spread_gates(gates_o, wide)
    lbs = [[level * 2 + bucket[step * 2 + im] for im in range(2)] for level in range(3)]

    def put_pair(ls, i, top, bot):
        e_hi, e_lo = split(top + bot)
        o_hi, o_lo = split(top - bot)
        for base, ev, ov in ((0, e_hi, o_hi), (HALF, e_lo, o_lo)):
            ecat[at(base, i), ls] = ev
            ocat[at(base, i), ls] = ov

    def first(t):
        for im, ls, hs in sub_tiles(t):
            for i in range(HALF // 16):
                put_pair(ls, i, ctx[at(im * IMG, i), hs], ctx[at(im * IMG + HALF, i), hs])

    def terms(ref, width, ts):
        hi = ref[:width, ts]
        return jnp.concatenate([hi, hi, ref[width:, ts]], axis=0)

    def transform(t):
        ts = slice(t * CHAIN, (t + 1) * CHAIN)
        s_a[:, ts] = dot(fe[...], terms(ecat, HALF, ts))
        s_b[:, ts] = dot(fo[...], terms(ocat, HALF, ts))

    def back(t):
        ts = slice(t * CHAIN, (t + 1) * CHAIN)
        s_e[:, ts] = dot(ge[...], terms(yca, AR, ts))
        s_o[:, ts] = dot(go[...], terms(ycb, BR, ts))

    def filt(t, level):
        base = level * SR
        for im, ls, hs in sub_tiles(t):
            lb = lbs[level][im]
            for i in range(Q // 16):
                a_re, a_im = s_a[at(0, i), ls], s_a[at(Q + 16, i), ls]
                b_re, b_im = s_b[at(0, i), ls], s_b[at(Q, i), ls]
                xp_re, xp_im = a_re + b_im, a_im - b_re
                xm_re, xm_im = a_re - b_im, a_im + b_re
                spec_o[at(base, i), ls] = xp_re.astype(bf16)
                spec_o[at(base + Q, i), ls] = xp_im.astype(bf16)
                spec_o[at(base + 2 * Q, i), ls] = xm_re.astype(bf16)
                spec_o[at(base + 3 * Q, i), ls] = xm_im.astype(bf16)
                p_re, p_im = h_o[lb, at(0, i), hs], h_o[lb, at(Q, i), hs]
                q_re, q_im = h_o[lb, at(2 * Q, i), hs], h_o[lb, at(3 * Q, i), hs]
                yp_re, yp_im = p_re * xp_re - p_im * xp_im, p_re * xp_im + p_im * xp_re
                ym_re, ym_im = q_re * xm_re - q_im * xm_im, q_re * xm_im + q_im * xm_re
                for dst, off, width, val in (
                    (yca, 0, AR, yp_re + ym_re),
                    (yca, Q + 16, AR, yp_im + ym_im),
                    (ycb, 0, BR, ym_im - yp_im),
                    (ycb, Q, BR, yp_re - ym_re),
                ):
                    hi, lo = split(val)
                    dst[at(off, i), ls] = hi
                    dst[at(off + width, i), ls] = lo
            x_re, x_im = s_a[Q : Q + 16, ls], s_a[2 * Q + 16 : 2 * Q + 32, ls]
            spec_o[base + 4 * Q : base + 4 * Q + 16, ls] = x_re.astype(bf16)
            spec_o[base + 4 * Q + 16 : base + 4 * Q + 32, ls] = x_im.astype(bf16)
            p_re, p_im = h_o[lb, 4 * Q : 4 * Q + 16, hs], h_o[lb, 4 * Q + 16 : 4 * Q + 32, hs]
            for off, val in ((Q, p_re * x_re - p_im * x_im), (2 * Q + 16, p_re * x_im + p_im * x_re)):
                hi, lo = split(val)
                yca[off : off + 16, ls] = hi
                yca[off + AR : off + AR + 16, ls] = lo

    def act(t, level):
        for im, ls, hs in sub_tiles(t):
            total = jnp.zeros((8, 128), f32)
            for i in range(HALF // 16):
                even, odd = s_e[at(0, i), ls], s_o[at(0, i), ls]
                both = []
                for h, a in ((0, even + odd), (HALF, even - odd)):
                    z, g = gelu_scaled(a)
                    z_o[at(level * IMG + h, i), ls] = z.astype(bf16)
                    g_o[at(level * IMG + h, i), ls] = g.astype(bf16)
                    s = at(im * IMG + h, i)
                    part = z * wide[level, s, :]
                    mix[s, hs] = part if level == 0 else mix[s, hs] + part
                    both.append(z)
                if level < 2:
                    put_pair(ls, i, both[0], both[1])
                else:
                    total = total + sum8(both[0]) + sum8(both[1])
            if level == 2:
                mean = jnp.sum(total, axis=0, keepdims=True) * (1.0 / (GH * GW))
                mean_o[:, ls] = jnp.broadcast_to(mean, (8, 128))
                glob, _ = gelu_pair(mean)
                for i in range(IMG // 16):
                    s = at(im * IMG, i)
                    mixed_o[s, hs] = (mix[s, hs] + wide[3, s, :] * glob).astype(bf16)

    def phases(t):
        steps = [lambda: first(t)]
        for level in range(3):
            steps += [
                lambda: transform(t),
                lambda level=level: filt(t, level),
                lambda: back(t),
                lambda level=level: act(t, level),
            ]
        return steps

    staggered(phases)


def kernel_middle(
    gx, gy, mlp_len, pos, x_ref, up, mixed, q_ref, wh, wp, vec, bm1, *refs,
):
    blocks = refs[: gy // 2]
    (
        dmid_o, out_o, dq_o, dmix_o, own, oth, gwh, gwp, sums, bsum,
        mod, modulated, branch, mid, second, dshr, shr, dsec, act, dexp, hid, dact, dbr, dm2, dmod, vacc, bacc, gw1, gw2, flat,
        w1, w2,
    ) = refs[gy // 2 :]
    step = pl.program_id(0)
    start = step == 0

    @pl.when(start)
    def _():
        for ref in (gwh, gwp, vacc, bacc):
            ref[...] = jnp.zeros_like(ref)
        unpack_mlp(gx, gy, mlp_len, pos, blocks, w1, w2, flat)

    def add_to(ref, rows_at, cols, v):
        ref[rows_at, cols] = jnp.where(start, 0.0, ref[rows_at, cols]) + v

    g2, b2 = vec[V_G2 : V_G2 + 1, :], vec[V_B2 : V_B2 + 1, :]
    s1, s2 = vec[V_S1 : V_S1 + 1, :], vec[V_S2 : V_S2 + 1, :]
    bm2 = vec[V_BM2 : V_BM2 + 1, :]

    mod[...] = dot(mixed[...], wh[...]) + vec[V_HB : V_HB + 1, :]
    for i in range(BROWS // 32):
        s = at(0, i, 32)
        modulated[s, :] = (q_ref[s, :] * mod[s, :]).astype(bf16)
        dshr[s, :] = (up[s, :].astype(f32) * s2).astype(bf16)
    branch[...] = dot(modulated[...], wp[...]) + vec[V_PB : V_PB + 1, :]
    for i in range(BROWS // 32):
        s = at(0, i, 32)
        middle = x_ref[s, :].astype(f32) + s1 * branch[s, :]
        mid[s, :] = middle
        n, _ = norm_stats(middle)
        second[s, :] = (n * g2 + b2).astype(bf16)

    chunks = [slice(h * HCHUNK, (h + 1) * HCHUNK) for h in range(HID // HCHUNK)]

    def enter(h):
        def into(t, k):
            ls = slice(h * HCHUNK + 256 * t, h * HCHUNK + 256 * t + 256)
            if k == 0:
                hid[h % 2, :, 256 * t : 256 * t + 256] = dot(second[...], w1[:, ls]) + bm1[0:1, ls]
            else:
                dact[h % 2, :, 256 * t : 256 * t + 256] = dot_nt(dshr[...], w2[ls, :])

        return [functools.partial(into, t, k) for t in range(HCHUNK // 256) for k in range(2)]

    def gelu(h):
        totals = []

        def rows_of(i):
            s = at(0, i)
            z, g = gelu_pair(hid[h % 2, s, :])
            act[s, chunks[h]] = z.astype(bf16)
            d = dact[h % 2, s, :] * g
            dexp[s, chunks[h]] = d.astype(bf16)
            totals.append(sum8(d) if not totals else totals.pop() + sum8(d))

        def close():
            bacc[:, chunks[h]] += totals[0]

        return [functools.partial(rows_of, i) for i in range(BROWS // 16)] + [close]

    def weight_grads(h):
        def one(t):
            ls = slice(h * HCHUNK + 256 * t, h * HCHUNK + 256 * t + 256)
            add_to(gw1, slice(None), ls, dot_tn(second[...], dexp[:, ls]))

        def two():
            add_to(gw2, chunks[h], slice(None), dot_tn(act[:, chunks[h]], dshr[...]))

        return [functools.partial(one, t) for t in range(HCHUNK // 256)] + [two]

    for step_of in enter(0):
        step_of()
    weave(enter(1), gelu(0))
    weave(enter(2) + weight_grads(0), gelu(1))
    weave(weight_grads(1), gelu(2))
    shr[...] = dot(act[...], w2[...])
    dsec[...] = dot_nt(dexp[...], w1[...])

    tally = {}

    def count(key, v):
        tally[key] = tally[key] + sum8(v) if key in tally else sum8(v)

    def finish(i):
        s = at(0, i, 32)
        middle = mid[s, :]
        u = up[s, :].astype(f32)
        shrunk = shr[s, :] + bm2
        out_o[s, :] = (middle + s2 * shrunk).astype(bf16)
        n, r = norm_stats(middle)
        d = dsec[s, :]
        e = d * g2
        dn = d * n
        dv = r * (e - jnp.mean(e, axis=-1, keepdims=True) - n * jnp.mean(e * n, axis=-1, keepdims=True))
        dm = u + dv
        dmid_o[s, :] = dm
        db = s1 * dm
        dbr[s, :] = db.astype(bf16)
        count(S_S1, dm * branch[s, :])
        count(S_G2, dn)
        count(S_B2, d)
        count(S_BM2, dshr[s, :].astype(f32))
        count(S_S2, u * shrunk)
        count(S_PB, db)

    weave(weight_grads(2), [functools.partial(finish, i) for i in range(BROWS // 32)])
    dmod[...] = dot_nt(dbr[...], wp[...])

    def demod(i):
        s = at(0, i, 32)
        dm = dmod[s, :]
        dq = dm * mod[s, :]
        dd = dm * q_ref[s, :]
        dq_o[s, :] = dq.astype(bf16)
        dm2[s, :] = dd.astype(bf16)
        count(S_BQ, dq)
        count(S_HB, dd)

    def grad_wp():
        gwp[...] += dot_tn(modulated[...], dbr[...])

    weave([grad_wp], [functools.partial(demod, i) for i in range(BROWS // 32)])
    dmix_o[...] = dot_nt(dm2[...], wh[...])
    gwh[...] += dot_tn(mixed[...], dm2[...])

    for key, v in tally.items():
        vacc[key] += v

    @pl.when(step == pl.num_programs(0) - 1)
    def _():
        for k in range(8):
            sums[k : k + 1, :] = jnp.sum(vacc[k], axis=0, keepdims=True)
        bsum[...] = jnp.broadcast_to(jnp.sum(bacc[...], axis=0, keepdims=True), bsum.shape)
        pack_mlp(gx, gy, mlp_len, pos, gw1, gw2, own, oth, flat)


def kernel_backward(
    gx, gy, mod_len, small_len,
    bucket, pos, nb_ref, dq_ref, dmix, gates, z_ref, g_ref, spec, mean_ref, kcat, vec, sums, bsum, es, weights,
    fe, fo, ge, go, wf_far, gwh_far, gwp_far, est_far,
    dmer, own, oth,
    gwf, fsum, gb, dk, h_ref, ecat, ocat, s_a, s_b, s_e, s_o, yca, ycb, acc, facc, wide, flat, small, moved, spread,
    wf, gwh, gwp, est, sems,
):
    step = pl.program_id(0)
    last = pl.num_programs(0) - 1
    late = [
        pltpu.make_async_copy(src, dst, sems.at[k])
        for k, (src, dst) in enumerate(((wf_far, wf), (gwh_far, gwh), (gwp_far, gwp), (est_far, est)))
    ]

    @pl.when(step == 0)
    def _():
        for copy in late:
            copy.start()
        for ref in (gwf, facc, acc):
            ref[...] = jnp.zeros_like(ref)
        for lb in range(6):
            h_ref[lb] = dot(es[lb], kcat[lb // 2])

    spread_gates(gates, wide)
    lbs = [[level * 2 + bucket[step * 2 + im] for im in range(2)] for level in range(3)]
    globs = [gelu_pair(mean_ref[0:1, lanes(im)]) for im in range(2)]
    lane = lax.broadcasted_iota(jnp.int32, (16, GATES), 1)
    dmeans = {}

    def mean_grad(t):
        for im, ls, hs in sub_tiles(t):
            total = jnp.zeros((8, 128), f32)
            for i in range(IMG // 16):
                s = at(im * IMG, i)
                total = total + sum8(dmix[s, hs] * wide[3, s, :])
            dmeans[ls.start] = jnp.sum(total, axis=0, keepdims=True) * globs[im][1][:, hs] * (1.0 / (GH * GW))

    def gate_grad(part):
        t_g = jnp.zeros((8, GATES), f32)
        n = 2 * (HALF // 16) // CHAINS
        for im, i in [(im, i) for im in range(2) for i in range(HALF // 16)][part * n : part * n + n]:
            for h in (0, HALF):
                s = at(im * IMG + h, i)
                dm = dmix[s, :]
                dg = jnp.zeros((16, GATES), f32)
                for k in range(4):
                    other = z_ref[at(k * IMG + h, i), lanes(im)].astype(f32) if k < 3 else globs[im][0]
                    col = jnp.sum(dm * other, axis=-1, keepdims=True)
                    dg = jnp.where(lane == k, col, dg)
                dmer[s, :C] = dq_ref[s, :]
                dmer[s, C2:] = dg.astype(bf16)
                t_g = t_g + sum8(dg)
        facc[:, C2:] += t_g

    def before(t, level):
        for im, ls, hs in sub_tiles(t):
            for i in range(HALF // 16):
                if level < 2:
                    even, odd = s_e[at(0, i), ls], s_o[at(0, i), ls]
                    through = (even + odd, even - odd)
                else:
                    through = (dmeans[ls.start], dmeans[ls.start])
                parts = []
                for k, h in enumerate((0, HALF)):
                    s = at(im * IMG + h, i)
                    dz = wide[level, s, :] * dmix[s, hs] + through[k]
                    parts.append(dz * g_ref[at(level * IMG + h, i), ls].astype(f32))
                ecat[at(0, i), ls] = (parts[0] + parts[1]).astype(bf16)
                ocat[at(0, i), ls] = (parts[0] - parts[1]).astype(bf16)

    def transform(t):
        ts = slice(t * CHAIN, (t + 1) * CHAIN)
        s_a[:, ts] = dot(fe[...], ecat[:, ts])
        s_b[:, ts] = dot(fo[...], ocat[:, ts])

    def back(t):
        ts = slice(t * CHAIN, (t + 1) * CHAIN)
        s_e[:, ts] = dot(ge[...], yca[:, ts])
        s_o[:, ts] = dot(go[...], ycb[:, ts])

    def filt(t, level):
        base = level * SR
        for im, ls, hs in sub_tiles(t):
            lb = lbs[level][im]
            for i in range(Q // 16):
                a_re, a_im = s_a[at(0, i), ls], s_a[at(Q + 16, i), ls]
                b_re, b_im = s_b[at(0, i), ls], s_b[at(Q, i), ls]
                dp_re, dp_im = a_re + b_im, a_im - b_re
                dm_re, dm_im = a_re - b_im, a_im + b_re
                xp_re, xp_im = spec[at(base, i), ls].astype(f32), spec[at(base + Q, i), ls].astype(f32)
                xm_re, xm_im = spec[at(base + 2 * Q, i), ls].astype(f32), spec[at(base + 3 * Q, i), ls].astype(f32)
                acc[lb, at(0, i), hs] += xp_re * dp_re + xp_im * dp_im
                acc[lb, at(Q, i), hs] += xp_im * dp_re - xp_re * dp_im
                acc[lb, at(2 * Q, i), hs] += xm_re * dm_re + xm_im * dm_im
                acc[lb, at(3 * Q, i), hs] += xm_im * dm_re - xm_re * dm_im
                p_re, p_im = h_ref[lb, at(0, i), hs], h_ref[lb, at(Q, i), hs]
                q_re, q_im = h_ref[lb, at(2 * Q, i), hs], h_ref[lb, at(3 * Q, i), hs]
                yp_re, yp_im = p_re * dp_re + p_im * dp_im, p_re * dp_im - p_im * dp_re
                ym_re, ym_im = q_re * dm_re + q_im * dm_im, q_re * dm_im - q_im * dm_re
                yca[at(0, i), ls] = (yp_re + ym_re).astype(bf16)
                yca[at(Q + 16, i), ls] = (yp_im + ym_im).astype(bf16)
                ycb[at(0, i), ls] = (ym_im - yp_im).astype(bf16)
                ycb[at(Q, i), ls] = (yp_re - ym_re).astype(bf16)
            d_re, d_im = s_a[Q : Q + 16, ls], s_a[2 * Q + 16 : 2 * Q + 32, ls]
            x_re = spec[base + 4 * Q : base + 4 * Q + 16, ls].astype(f32)
            x_im = spec[base + 4 * Q + 16 : base + 4 * Q + 32, ls].astype(f32)
            acc[lb, 4 * Q : 4 * Q + 16, hs] += x_re * d_re + x_im * d_im
            acc[lb, 4 * Q + 16 : 4 * Q + 32, hs] += x_im * d_re - x_re * d_im
            p_re, p_im = h_ref[lb, 4 * Q : 4 * Q + 16, hs], h_ref[lb, 4 * Q + 16 : 4 * Q + 32, hs]
            yca[Q : Q + 16, ls] = (p_re * d_re + p_im * d_im).astype(bf16)
            yca[2 * Q + 16 : 2 * Q + 32, ls] = (p_re * d_im - p_im * d_re).astype(bf16)

    def context(t):
        for im, ls, hs in sub_tiles(t):
            ds = slice(C + hs.start, C + hs.stop)
            total = jnp.zeros((8, 128), f32)
            for i in range(HALF // 16):
                even, odd = s_e[at(0, i), ls], s_o[at(0, i), ls]
                top, bot = even + odd, even - odd
                dmer[at(im * IMG, i), ds] = top.astype(bf16)
                dmer[at(im * IMG + HALF, i), ds] = bot.astype(bf16)
                total = total + sum8(top) + sum8(bot)
            facc[:, ds] += total

    def phases(t):
        steps = [lambda: mean_grad(t)]
        for level in (2, 1, 0):
            steps += [
                lambda level=level: before(t, level),
                lambda: transform(t),
                lambda level=level: filt(t, level),
                lambda: back(t),
            ]
            if level == 2:
                steps.append(lambda: gate_grad(t))
        return steps + [lambda: context(t)]

    staggered(phases)
    gwf[...] += dot_tn(nb_ref[...], dmer[...])

    @pl.when(step == last)
    def _():
        for copy in late:
            copy.wait()
        facc[:, :C] = jnp.broadcast_to(sums[S_BQ : S_BQ + 1, :] * 0.125, (8, C))
        colsum = jnp.sum(facc[...], axis=0, keepdims=True)
        fsum[...] = jnp.broadcast_to(colsum, fsum.shape)
        wide = wf[...].astype(f32)
        t_hi, t_lo = split(wide * gwf[...])
        ones = jnp.ones((8, MERGED), bf16)
        gb[0:8, :] = dot_nt(ones, t_hi) + dot_nt(ones, t_lo)
        c_hi, c_lo = split(fsum[...])
        gb[8:16, :] = dot_nt(c_hi, wf[...]) + dot_nt(c_lo, wf[...])
        g1 = jnp.transpose(jnp.broadcast_to(vec[V_G1 : V_G1 + 1, :], (128, C)))
        b1 = jnp.transpose(jnp.broadcast_to(vec[V_B1 : V_B1 + 1, :], (128, C)))
        for t in range(MERGED // 128):
            ls = slice(128 * t, 128 * t + 128)
            gwf[:, ls] = gwf[:, ls] * g1 + b1 * fsum[0:1, ls]
        for level in range(3):
            total = None
            for lb in (level * 2, level * 2 + 1):
                hi, lo = split(acc[lb] * jnp.concatenate([weights[...]] * (C // 128), 1))
                first = dot(est[lb], hi)
                term = first[:TAPS] + first[TAPS:] + dot(est[lb, :TAPS, :], lo)
                total = term if total is None else total + term
            dk[level] = total
        pack_mod(gx, gy, mod_len, small_len, pos, gwf, gwh, gwp, sums, bsum, fsum, gb, dk, own, oth, flat, small, moved, spread)


def to_native(rows_ref, first, native, slot, slots, gain):
    line = GW * slots
    for y in range(GH):
        a = first + grid_rows(0, y)
        for lt in range(C // 128):
            v = rows_ref[a : a + GW, 128 * lt : 128 * lt + 128]
            native[lt, pl.ds(line * y + slot, GW, stride=slots), :] = v if gain is None else v * gain


def write_native(native, out, slots):
    line = GW * slots
    for y in range(GH):
        for lt in range(C // 128):
            v = native[lt, line * y : line * (y + 1), :].reshape(GW, slots, 128)
            out[y, :, :, 128 * lt : 128 * lt + 128] = v.astype(out.dtype)


def kernel_tail(dmer, wf, x_ref, stat, dmid, vec, gtok_o, stage, native):
    step = pl.program_id(0)
    slots = gtok_o.shape[2]
    g1 = vec[V_G1 : V_G1 + 1, :]
    d_normed = dot_nt(dmer[...], wf[...])
    for i in range(PAIR // 32):
        s = at(0, i, 32)
        r = stat[s, 1:2]
        n = (x_ref[s, :].astype(f32) - stat[s, 0:1]) * r
        e = d_normed[s, :] * g1
        dv = e - jnp.mean(e, axis=-1, keepdims=True) - n * jnp.mean(e * n, axis=-1, keepdims=True)
        stage[s, :] = dmid[s, :] + r * dv
    for im in range(2):
        to_native(stage, im * IMG, native, step * 2 + im, slots, None)

    @pl.when(step == pl.num_programs(0) - 1)
    def _():
        write_native(native, gtok_o, slots)


def kernel_out(counts, rows_ref, out_o, native, wide):
    slots = out_o.shape[2]
    wide[...] = rows_ref[...].astype(f32)
    for im in range(slots):
        to_native(wide, im * IMG, native, im, slots, (im < counts[0]).astype(f32))
    write_native(native, out_o, slots)


def block_rows(length):
    return 8 * (length // 1024 if length % 1024 == 0 else (length + 1022) // 1024 + 1)


def place(shard, device):
    length = shard.shape[0]
    n = block_rows(length) * 128
    if n == length:
        return shard.reshape(-1, 128)
    offset = lax.rem(device * length, 1024)
    return lax.dynamic_update_slice(jnp.zeros((n,), shard.dtype), shard, (offset,)).reshape(-1, 128)


def take(block, length, device):
    flat = block.reshape(-1)
    if flat.shape[0] == length:
        return flat
    return lax.dynamic_slice(flat, (lax.rem(device * length, 1024),), (length,))


def first_row(length, device):
    return pl.multiple_of((device * length) // 1024 * 8, 8)


def device_at(pos, gy, i, j, c):
    return (pos[0] ^ j) * gy + (pos[1] ^ (2 * i + c))


def join(first, second, sh):
    lane = lax.broadcasted_iota(jnp.int32, first.shape, 1)
    return jnp.where(lane < 128 - sh, first, second)


def turn(v, sh):
    return pltpu.roll(v, 128 - sh, 1) if sh else v


def shift_right(first, second, sh):
    lane = lax.broadcasted_iota(jnp.int32, first.shape, 1)
    return jnp.where(lane < sh, pltpu.roll(first, sh, 1), pltpu.roll(second, sh, 1))


WIDE = C2 + 4
WF_ROWS = C * WIDE // 128
W_ROWS = C * C // 128
PERIOD = 32
PITCH_IMAGE = IMG + 8
PITCH_Q = 24
PITCH_P = 40
STRIDE = PERIOD * WIDE // 128
K_ROW = 12
TAIL_ROW = K_ROW + 83 * C // 128
B_HB, B_PB, B_S1, B_G2, B_B2, B_BM1 = (TAIL_ROW + 3 * k for k in range(6))
B_BM2 = B_BM1 + HID // 128
B_S2 = B_BM2 + 3
END_ROW = B_S2 + 3


def by_threes(flat, base, n, temp, out):
    for g in range(n // 64):
        room = 192 * (g % 4)
        for k in range(8):
            for b in range(3):
                src = base + 192 * g + 24 * k + 8 * b
                temp[pl.ds(room + 64 * b + k, 8, stride=8), :] = flat[src : src + 8, :]
        for i in range(24):
            rows_at = 768 + 64 * ((g % 4) * 3 + i % 3) + i // 3
            temp[pl.ds(rows_at, 8, stride=8), :] = temp[room + 8 * i : room + 8 * i + 8, :]
        for t in range(3):
            first = 768 + 64 * ((g % 4) * 3 + t)
            out[64 * g : 64 * g + 64, 128 * t : 128 * t + 128] = temp[first : first + 64, :].astype(bf16)


def unpack_mod(gx, gy, mod_len, small_len, pos, own, oth, wf_o, wh_o, wp_o, vec_o, bm1_o, kcat_o, flat, small, moved, wide, turned):
    flat[...] = jnp.zeros_like(flat)
    small[...] = jnp.zeros_like(small)
    mr, sr = block_rows(mod_len), block_rows(small_len)
    for i in range(gy // 2):
        for j in range(gx):
            for c, src in enumerate((own, oth)):
                d = device_at(pos, gy, i, j, c)
                block = src[i, j].astype(f32)
                flat[pl.ds(first_row(mod_len, d), mr), :] += block[:mr]
                small[pl.ds(first_row(small_len, d), sr), :] += block[mr : mr + sr]
    lane = lax.broadcasted_iota(jnp.int32, (16, 128), 1)
    for q in range(C // PERIOD):
        for f in range(0, STRIDE + 7, 8):
            turned[pl.ds(PITCH_Q * f + q, 8, stride=PITCH_Q), :] = flat[STRIDE * q + f : STRIDE * q + f + 8, :]
    for p in range(PERIOD):
        row, sh = WIDE * p // 128, WIDE * p % 128
        first = [PITCH_Q * (row + j) for j in range(MERGED // 128 + (1 if sh else 0))]
        tiles = [turn(turned[k : k + 16, :], sh) for k in first]
        for j in range(MERGED // 128):
            v = join(tiles[j], tiles[j + 1], sh) if sh else tiles[j]
            if j == MERGED // 128 - 1:
                v = jnp.where(lane < 4, v, 0.0)
            wide[j, pl.ds(p, 16, stride=PITCH_P), :] = v
    for j in range(MERGED // 128):
        for q in range(C // PERIOD):
            v = wide[j, PITCH_P * q : PITCH_P * q + PERIOD, :]
            wf_o[PERIOD * q : PERIOD * q + PERIOD, 128 * j : 128 * j + 128] = v.astype(bf16)
    by_threes(flat, WF_ROWS, C, turned, wh_o)
    by_threes(flat, WF_ROWS + W_ROWS, C, turned, wp_o)
    n = moved.shape[0]
    moved[...] = join(turn(small[0:n, :], 4), turn(small[1 : n + 1, :], 4), 4)
    vec_o[...] = jnp.zeros_like(vec_o)
    for row, src, start in (
        (V_G1, small, 0), (V_B1, small, 3), (V_BQ, small, 6), (V_BC, small, 9),
        (V_HB, moved, B_HB), (V_PB, moved, B_PB), (V_S1, moved, B_S1), (V_G2, moved, B_G2), (V_B2, moved, B_B2),
        (V_BM2, moved, B_BM2), (V_S2, moved, B_S2),
    ):
        for j in range(3):
            vec_o[row : row + 1, 128 * j : 128 * j + 128] = src[start + j : start + j + 1, :]
    vec_o[V_BG : V_BG + 1, 0:128] = jnp.where(lane[0:1] < 4, small[K_ROW : K_ROW + 1, :], 0.0)
    for t in range(HID // 128):
        bm1_o[:, 128 * t : 128 * t + 128] = jnp.broadcast_to(moved[B_BM1 + t : B_BM1 + t + 1, :], (8, 128))
    start = 0
    for level, k in enumerate(LEVELS):
        for j in range(3):
            taps = moved[pl.ds(K_ROW + 3 * start + j, TAPS, stride=3), :].astype(bf16)
            kcat_o[level, 0:TAPS, 128 * j : 128 * j + 128] = taps
            kcat_o[level, TAPS:, 128 * j : 128 * j + 128] = taps
        start += k * k


def unpack_mlp(gx, gy, mlp_len, pos, blocks, w1_o, w2_o, flat):
    mr = block_rows(mlp_len)
    aligned = mr * 128 == mlp_len
    if not aligned:
        flat[...] = jnp.zeros_like(flat)
    for i, src in enumerate(blocks):
        for j in range(gx):
            for c in range(2):
                rows_at = pl.ds(first_row(mlp_len, device_at(pos, gy, i, j, c)), mr)
                if aligned:
                    flat[rows_at, :] = src[c, j].astype(f32)
                else:
                    flat[rows_at, :] += src[c, j].astype(f32)
    for t in range(HID // 128):
        w1_o[:, 128 * t : 128 * t + 128] = flat[pl.ds(t, C, stride=HID // 128), :].astype(bf16)
    for t in range(C // 128):
        w2_o[:, 128 * t : 128 * t + 128] = flat[pl.ds(C * HID // 128 + t, HID, stride=C // 128), :].astype(bf16)


def send_slots(gx, gy, pos, flat, length, base, own, oth):
    mr = block_rows(length)
    for i in range(gy // 2):
        for j in range(gx):
            for c, dst in enumerate((own, oth)):
                d = device_at(pos, gy, i, j, c)
                dst[i, j, base : base + mr, :] = flat[pl.ds(first_row(length, d), mr), :].astype(bf16)


def pack_mlp(gx, gy, mlp_len, pos, gw1, gw2, own, oth, flat):
    used = 2 * C * HID // 128
    if flat.shape[0] > used:
        flat[used:, :] = jnp.zeros_like(flat[used:, :])
    for t in range(HID // 128):
        flat[pl.ds(t, C, stride=HID // 128), :] = gw1[:, 128 * t : 128 * t + 128]
    for t in range(C // 128):
        flat[pl.ds(C * HID // 128 + t, HID, stride=C // 128), :] = gw2[:, 128 * t : 128 * t + 128]
    send_slots(gx, gy, pos, flat, mlp_len, 0, own, oth)


def pack_mod(gx, gy, mod_len, small_len, pos, gwf, gwh, gwp, sums, bsum, fsum, gb, dk, own, oth, flat, small, moved, wide):
    lane = lax.broadcasted_iota(jnp.int32, (16, 128), 1)
    used = WF_ROWS + 2 * W_ROWS
    if flat.shape[0] > used:
        flat[used:, :] = jnp.zeros_like(flat[used:, :])
    for j in range(MERGED // 128):
        for row in range(0, C, 8):
            dst = pl.ds(PITCH_Q * (row % PERIOD) + row // PERIOD, 8, stride=PITCH_Q)
            wide[j, dst, :] = gwf[row : row + 8, 128 * j : 128 * j + 128]
    turned = {}

    def piece(p, tile):
        tile = min(tile, MERGED // 128 - 1)
        if (p, tile) not in turned:
            turned[p, tile] = turn(wide[tile, PITCH_Q * p : PITCH_Q * p + 16, :], -WIDE * p % 128)
        return turned[p, tile]

    for f in range(STRIDE):
        p = 128 * f // WIDE
        col = 128 * f - WIDE * p
        t, sh = col // 128, col % 128
        v = join(piece(p, t), piece(p, t + 1), sh) if sh else piece(p, t)
        left = WIDE - col
        if left < 128:
            v = jnp.where(lane < left, v, piece(p + 1, 0))
        flat[pl.ds(f, 16, stride=STRIDE), :] = v
    for j in range(3):
        ls = slice(128 * j, 128 * j + 128)
        flat[pl.ds(WF_ROWS + j, C, stride=3), :] = gwh[:, ls]
        flat[pl.ds(WF_ROWS + W_ROWS + j, C, stride=3), :] = gwp[:, ls]
    moved[...] = jnp.zeros_like(moved)
    small[...] = jnp.zeros_like(small)
    start = 0
    for level, k in enumerate(LEVELS):
        for j in range(3):
            moved[pl.ds(K_ROW + 3 * start + j, k * k, stride=3), :] = dk[level, 0 : k * k, 128 * j : 128 * j + 128]
        start += k * k
    for start, row in (
        (B_HB, S_HB), (B_PB, S_PB), (B_S1, S_S1), (B_G2, S_G2), (B_B2, S_B2), (B_BM2, S_BM2), (B_S2, S_S2),
    ):
        for j in range(3):
            moved[start + j : start + j + 1, :] = sums[row : row + 1, 128 * j : 128 * j + 128]
    for t in range(HID // 128):
        moved[B_BM1 + t : B_BM1 + t + 1, :] = bsum[0:1, 128 * t : 128 * t + 128]
    n = moved.shape[0]
    small[8:n, :] = shift_right(moved[7 : n - 1, :], moved[8:n, :], 4)
    for j in range(3):
        ls = slice(128 * j, 128 * j + 128)
        small[j : j + 1, :] = gb[0:1, ls]
        small[3 + j : 4 + j, :] = gb[8:9, ls]
        small[6 + j : 7 + j, :] = fsum[0:1, ls]
        small[9 + j : 10 + j, :] = fsum[0:1, C + 128 * j : C + 128 * j + 128]
    gate_lane = lane[0:1] < 4
    small[K_ROW : K_ROW + 1, :] = jnp.where(gate_lane, fsum[0:1, C2:], small[K_ROW : K_ROW + 1, :])
    mr, sr = block_rows(mod_len), block_rows(small_len)
    send_slots(gx, gy, pos, flat, mod_len, 0, own, oth)
    for i in range(gy // 2):
        for j in range(gx):
            for c, dst in enumerate((own, oth)):
                block = small[pl.ds(first_row(small_len, device_at(pos, gy, i, j, c)), sr), :]
                pad = own.shape[2] - mr - sr
                if pad:
                    block = jnp.concatenate([block, jnp.zeros((pad, 128), f32)], 0)
                dst[i, j, mr:, :] = block.astype(bf16)


def kernel_add(n_in, *refs):
    for k, o in enumerate(refs[n_in:]):
        total = None
        for ref in refs[:n_in]:
            v = ref[k].astype(f32)
            total = v if total is None else total + v
        o[...] = total.astype(o.dtype)


def kernel_cut(cuts, *refs):
    outs = refs[-len(cuts) :]
    for o, (first, n) in zip(outs, cuts):
        total = None
        for ref in refs[: -len(cuts)]:
            v = ref[first : first + n, :].astype(f32)
            total = v if total is None else total + v
        o[...] = total


def full(shape):
    return pl.BlockSpec(shape, lambda *i, n=len(shape): (0,) * n)


def rows(n, width):
    return pl.BlockSpec((n, width), lambda i: (i, 0))


def smem():
    return pl.BlockSpec(memory_space=pltpu.SMEM)


def sds(shape, dtype):
    return jax.ShapeDtypeStruct(shape, dtype)


def call(kernel, name, grid, ins, outs, scratch, mib, micros):
    return pl.pallas_call(
        kernel,
        grid=grid,
        in_specs=[s for _, s in ins],
        out_shape=[o for o, _ in outs],
        out_specs=[s for _, s in outs],
        scratch_shapes=[pltpu.VMEM(*v) if isinstance(v, tuple) else v for v in scratch],
        compiler_params=pltpu.CompilerParams(vmem_limit_bytes=mib * 2**20),
        cost_estimate=pl.CostEstimate(flops=int(micros * 1e9), bytes_accessed=int(micros * 1e6), transcendentals=0),
        name=name,
    )(*[a for a, _ in ins])


def whole(*arrays):
    return [(a, full(a.shape)) for a in arrays]


def by_rows(n, *arrays):
    return [(a, rows(n, a.shape[1])) for a in arrays]


def native_rows(slots):
    return ((C // 128, GH * GW * slots, 128), f32)


def prep(tokens):
    slots = tokens.shape[2]
    n = slots * IMG
    outs = [(sds((n, w), t), rows(PAIR, w)) for w, t in ((C, bf16), (C, bf16), (128, f32))]
    return call(kernel_prep, "prep", (slots // 2,), whole(tokens), outs, [((C // 128, slots * PITCH_IMAGE, 128), f32)], 60, 4)


def upstream(counts, cotangent):
    slots = cotangent.shape[2]
    ins = [(counts, smem())] + whole(cotangent)
    outs = [(sds((slots * IMG, C), bf16), rows(PAIR, C))]
    return call(kernel_upstream, "upstream", (slots // 2,), ins, outs, [((C // 128, slots * PITCH_IMAGE, 128), f32)], 60, 3)[0]


def forward(gx, gy, pos, xrow, stat, bucket, own, oth, mod_len, small_len):
    con = constants()
    pairs = xrow.shape[0] // PAIR
    n = pairs * PAIR
    outs = [
        (sds((n, C), f32), rows(PAIR, C)),
        (sds((n, GATES), f32), rows(PAIR, GATES)),
        (sds((n, C), bf16), rows(PAIR, C)),
        (sds((pairs * 3 * IMG, C2), bf16), rows(3 * IMG, C2)),
        (sds((pairs * 3 * IMG, C2), bf16), rows(3 * IMG, C2)),
        (sds((pairs * 3 * SR, C2), bf16), rows(3 * SR, C2)),
        (sds((pairs * 8, C2), f32), rows(8, C2)),
    ]
    weights = [((C, MERGED), bf16), ((C, C), bf16), ((C, C), bf16), ((VROWS, C), f32), ((8, HID), f32), ((3, 2 * TAPS, C), bf16)]
    outs += [(sds(shape, dtype), full(shape)) for shape, dtype in weights]
    mats = [jnp.asarray(con[k]) for k in ("es", "fe", "fo", "ge", "go")]
    ins = [(bucket, smem()), (pos, smem())] + by_rows(PAIR, xrow, stat) + whole(own, oth, *mats)
    scratch = [
        ((6, SR, C), f32), ((PAIR, C), bf16), ((PAIR, C), f32), ((2 * HALF, C2), bf16), ((2 * HALF, C2), bf16), ((AR, C2), f32), ((BR, C2), f32),
        ((HALF, C2), f32), ((HALF, C2), f32), ((2 * AR, C2), bf16), ((2 * BR, C2), bf16), ((PAIR, C), f32),
        ((4, PAIR, 128), f32),
    ]
    ndev = gx * gy
    flat_rows = max(span(mod_len, ndev), STRIDE * 16 + 8)
    small_rows = max(span(small_len, ndev), END_ROW + 26)
    scratch += [((flat_rows, 128), f32), ((small_rows + 8, 128), f32), ((small_rows, 128), f32)]
    scratch += [((MERGED // 128, max(PITCH_Q * PERIOD, PITCH_P * 16), 128), f32), ((PITCH_Q * (STRIDE + 7), 128), f32)]
    kernel = functools.partial(kernel_forward, gx, gy, mod_len, small_len)
    return call(kernel, "focal_forward", (pairs,), ins, outs, scratch, 58, 28)


def middle(gx, gy, pos, xrow, up, mixed, q, wh, wp, vec, bm1, mlp_blocks, mlp_len):
    n = xrow.shape[0]
    outs = [
        (sds((n, C), f32), rows(BROWS, C)),
        (sds((n, C), bf16), rows(BROWS, C)),
        (sds((n, C), bf16), rows(BROWS, C)),
        (sds((n, C), f32), rows(BROWS, C)),
    ]
    slots = (gy // 2, gx, block_rows(mlp_len), 128)
    outs += [(sds(slots, bf16), full(slots))] * 2
    outs += [(sds(s, f32), full(s)) for s in ((C, C), (C, C), (8, C), (8, HID))]
    ins = [(pos, smem())] + by_rows(BROWS, xrow, up, mixed, q) + whole(wh, wp, vec, bm1, *mlp_blocks)
    blk = (BROWS, C)
    scratch = [
        (blk, f32), (blk, bf16), (blk, f32), (blk, f32), (blk, bf16), (blk, bf16), (blk, f32), (blk, f32),
        ((BROWS, HID), bf16), ((BROWS, HID), bf16), ((2, BROWS, HCHUNK), f32), ((2, BROWS, HCHUNK), f32), (blk, bf16), (blk, bf16), (blk, f32),
        ((8, 8, C), f32), ((8, HID), f32),
        ((C, HID), f32), ((HID, C), f32), ((span(mlp_len, gx * gy), 128), f32), ((C, HID), bf16), ((HID, C), bf16),
    ]
    kernel = functools.partial(kernel_middle, gx, gy, mlp_len)
    return call(kernel, "middle", (n // BROWS,), ins, outs, scratch, 60, 42)


def backward(gx, gy, pos, bucket, nb, dq, dmix, gates, z, g, spec, mean, kcat, wf, vec, sums, bsum, gwh, gwp, mod_len, small_len):
    con = constants()
    ndev = gx * gy
    pairs = nb.shape[0] // PAIR
    mats = [jnp.asarray(con[k]) for k in ("es", "weights", "fe_back", "fo_back", "ge_back", "go_back")]
    slots = (gy // 2, gx, -(-(block_rows(mod_len) + block_rows(small_len)) // 16) * 16, 128)
    outs = [(sds((nb.shape[0], MERGED), bf16), rows(PAIR, MERGED))] + [(sds(slots, bf16), full(slots))] * 2
    ins = [(bucket, smem()), (pos, smem())] + by_rows(PAIR, nb, dq, dmix, gates) + by_rows(3 * IMG, z, g) + by_rows(3 * SR, spec)
    ins += by_rows(8, mean) + whole(kcat, vec, sums, bsum, *mats)
    late = (wf, gwh, gwp, jnp.asarray(con["est"]))
    ins += [(v, pl.BlockSpec(memory_space=pl.ANY)) for v in late]
    small_rows = -(-max(span(small_len, ndev), END_ROW + 2) // 8) * 8
    scratch = [
        ((C, MERGED), f32), ((8, MERGED), f32), ((16, C), f32), ((3, TAPS, C), f32), ((6, SR, C), f32),
        ((HALF, C2), bf16), ((HALF, C2), bf16), ((AR, C2), f32), ((BR, C2), f32), ((HALF, C2), f32), ((HALF, C2), f32),
        ((AR, C2), bf16), ((BR, C2), bf16), ((6, SR, C), f32), ((8, MERGED), f32), ((4, PAIR, 128), f32),
        ((max(span(mod_len, ndev), STRIDE * 16 + 8), 128), f32), ((small_rows, 128), f32), ((small_rows, 128), f32),
        ((MERGED // 128, max(PITCH_Q * PERIOD, PITCH_P * 16), 128), f32),
    ]
    scratch += [(v.shape, v.dtype) for v in late] + [pltpu.SemaphoreType.DMA((len(late),))]
    kernel = functools.partial(kernel_backward, gx, gy, mod_len, small_len)
    return call(kernel, "focal_backward", (pairs,), ins, outs, scratch, 58, 28)


def tail(shape, dmer, wf, xrow, stat, dmid, vec):
    slots = shape[2]
    ins = by_rows(PAIR, dmer) + whole(wf) + by_rows(PAIR, xrow, stat, dmid) + whole(vec)
    return call(kernel_tail, "tail", (slots // 2,), ins, [(sds(shape, f32), full(shape))], [((PAIR, C), f32), native_rows(slots)], 24, 8)[0]


def out_tokens(shape, counts, out_rows):
    ins = [(counts, smem())] + whole(out_rows)
    return call(kernel_out, "out_tokens", (), ins, [(sds(shape, bf16), full(shape))], [native_rows(shape[2]), ((shape[2] * IMG, C), f32)], 24, 5)[0]


def span(length, ndev):
    return ((ndev - 1) * length) // 1024 * 8 + block_rows(length)


def add(arrays, outs, name):
    return call(functools.partial(kernel_add, len(arrays)), name, (), whole(*arrays), [(o, full(o.shape)) for o in outs], [], 24, 2)


def swap(x, mask, ndev):
    return lax.ppermute(x, AXES, [(k, k ^ mask) for k in range(ndev)])


def around(x, step, count, ndev):
    return [x] + [swap(x, step * k, ndev) for k in range(1, count)]


def after(values):
    return lax.optimization_barrier(values)


def travel(parts, step, ndev):
    return [parts[0]] + [swap(p, step * k, ndev) for k, p in enumerate(parts) if k]


def sum_core(own, oth, gx, gy, name):
    got = swap(oth, 1, gx * gy)
    return add([own, got], [sds(own.shape[1:], f32 if k == 0 else bf16) for k in range(gy // 2)], name + "_sum_core")


def sum_plane(parts, gx, name):
    shape = parts[0].shape[1:]
    return add(parts, [sds(shape, f32 if k == 0 else bf16) for k in range(gx)], name + "_sum_plane")


def sum_line(parts, cuts, name):
    outs = [(sds((n, 128), f32), full((n, 128))) for _, n in cuts]
    return call(functools.partial(kernel_cut, cuts), name + "_sum_line", (), whole(*parts), outs, [], 24, 2)


def local(gx, gy, tokens, bucket, counts, mod_weights, mlp_weights, small_params, cotangent):
    ndev = gx * gy
    gxi, gyi = lax.axis_index("gx"), lax.axis_index("gy")
    device = gxi * gy + gyi
    pos = jnp.stack([gxi, gyi]).astype(jnp.int32)
    mod_len, small_len, mlp_len = mod_weights.shape[0], small_params.shape[0], mlp_weights.shape[0]
    mr, sr = block_rows(mod_len), block_rows(small_len)

    blocks = [place(mod_weights, device), place(small_params, device)]
    pad = -(mr + sr) % 16
    if pad:
        blocks.append(jnp.zeros((pad, 128), bf16))
    line = around(jnp.concatenate(blocks, 0), gy, gx, ndev)
    native, back = (1, 2, 0, 3), (2, 0, 1, 3)
    shape = (GH, GW) + tokens.shape[:1] + (C,)
    prepared = prep(jnp.transpose(tokens, native))
    line, mlp_mine, prepared = after((line, place(mlp_weights, device), prepared))
    xrow, nb, stat = prepared
    plane = around(jnp.stack(line), 2, gy // 2, ndev)
    mlp_line = jnp.stack(around(mlp_mine, gy, gx, ndev))
    up = upstream(counts, jnp.transpose(cotangent, native))
    plane, mlp_line, up = after((plane, mlp_line, up))
    mlp_other = swap(mlp_line, 1, ndev)
    plane = jnp.stack(plane)
    other = swap(plane, 1, ndev)
    mlp_both = jnp.stack([mlp_line, mlp_other])
    other, mlp_both = after((other, mlp_both))
    mlp_blocks = around(mlp_both, 2, gy // 2, ndev)

    q, gates, mixed, z, g, spec, mean, wf, wh, wp, vec, bm1, kcat = forward(
        gx, gy, pos, xrow, stat, bucket, plane, other, mod_len, small_len
    )
    mlp_blocks, mixed = after((mlp_blocks, mixed))
    dmid, out_rows, dq, dmix, own, oth, gwh, gwp, sums, bsum = middle(
        gx, gy, pos, xrow, up, mixed, q, wh, wp, vec, bm1, mlp_blocks, mlp_len
    )
    parts = sum_core(own, oth, gx, gy, "mlp")
    parts, dmix = after((parts, dmix))
    mlp_plane = travel(parts, 2, ndev)
    dmer, own, oth = backward(
        gx, gy, pos, bucket, nb, dq, dmix, gates, z, g, spec, mean, kcat, wf, vec, sums, bsum, gwh, gwp, mod_len, small_len
    )
    mlp_plane, own, oth = after((mlp_plane, own, oth))
    parts = sum_plane(mlp_plane, gx, "mlp")
    mod_parts = sum_core(own, oth, gx, gy, "mod")
    mlp_line = travel(parts, gy, ndev)
    mod_plane = travel(mod_parts, 2, ndev)
    gtok = tail(shape, dmer, wf, xrow, stat, dmid, vec)
    mod_plane, mlp_line, gtok, out_rows = after((mod_plane, mlp_line, gtok, out_rows))
    mod_line = travel(sum_plane(mod_plane, gx, "mod"), gy, ndev)
    grad_mlp = take(sum_line(mlp_line, [(0, mlp_line[0].shape[0])], "mlp")[0], mlp_len, device)
    out = out_tokens(shape, counts, out_rows)
    mod_line, out, grad_mlp = after((mod_line, out, grad_mlp))
    total_mod, total_small = sum_line(mod_line, [(0, mr), (mr, sr)], "mod")
    grad_mod = take(total_mod, mod_len, device)
    grad_small = take(total_small, small_len, device)
    return jnp.transpose(out, back), jnp.transpose(gtok, back), grad_mod, grad_mlp, grad_small


def solution(mesh):
    images = P(AXES, None, None, None)
    flat = P(AXES)
    return jax.shard_map(
        functools.partial(local, mesh.shape["gx"], mesh.shape["gy"]),
        mesh=mesh,
        in_specs=(images, flat, flat, flat, flat, flat, images),
        out_specs=(images, images, flat, flat, flat),
        check_vma=False,
    )
```

```python
import functools

import jax
import jax.numpy as jnp
import numpy as np
from jax import lax
from jax.experimental import pallas as pl
from jax.experimental.pallas import tpu as pltpu
from jax.sharding import PartitionSpec as P

C = 384
HID = 1536
GH = 14
GW = 20
HALF = 144
IMG = 2 * HALF
PAIR = 2 * IMG
C2 = 2 * C
NY = 17
NX = 23
NV = 12
NU = 8
Q = NU * NV
AR = 2 * (Q + 16)
BR = 2 * Q
SR = 4 * Q + 32
LEVELS = (3, 5, 7)
TAPS = 64
GATES = 128
MERGED = C2 + GATES
BROWS = 768
HCHUNK = 512
AXES = ("gx", "gy")
f32 = jnp.float32
bf16 = jnp.bfloat16
EPS = 1e-05
ROOT_HALF = 0.7071067811865476
INV_ROOT_2PI = 0.3989422804014327
LOG2_E = 1.4426950408889634


def _hi(a):
    return a.astype(bf16)


def _lo(a):
    return (a - a.astype(bf16).astype(np.float64)).astype(bf16)


def three(a):
    return np.concatenate([_hi(a), _lo(a), _hi(a)], 1)


@functools.lru_cache(maxsize=None)
def constants():
    row = np.arange(HALF)
    real = (row < 7 * GW).astype(np.float64)
    yy = np.minimum(row // GW, 6) - (GH - 1) / 2
    xx = row % GW - (GW - 1) / 2
    uv = [(u, v) for u in range(1, NU + 1) for v in range(NV)]
    u0 = [(0, v) for v in range(NV)]
    wu = 2 * np.pi / NY
    wv = 2 * np.pi / NX

    def trig(pairs, pad):
        u = np.array([p[0] for p in pairs] + [0] * pad, np.float64)[:, None]
        v = np.array([p[1] for p in pairs] + [0] * pad, np.float64)[:, None]
        use = np.array([1.0] * len(pairs) + [0.0] * pad)[:, None] * real[None]
        cy, sy = np.cos(wu * u * yy) * use, np.sin(wu * u * yy) * use
        cx, sx = np.cos(wv * v * xx), np.sin(wv * v * xx)
        weight = np.where(u > 0, 2.0, 1.0) * np.where(v > 0, 2.0, 1.0) / (NY * NX)
        return cy * cx, -cy * sx, sy * cx, -sy * sx, weight

    e_re, e_im, o_re, o_im, w1 = trig(uv, 0)
    z_re, z_im, _, _, w0 = trig(u0, 16 - NV)
    fe = np.concatenate([e_re, z_re, e_im, z_im], 0)
    fo = np.concatenate([o_re, o_im], 0)
    half = np.concatenate([0.5 * w1, w0, 0.5 * w1, w0], 0)
    ge = (fe * half).T
    go = (fo * np.concatenate([0.5 * w1, 0.5 * w1], 0)).T

    u = np.array([p[0] for p in uv], np.float64)[:, None]
    v = np.array([p[1] for p in uv], np.float64)[:, None]
    v0 = np.array(list(range(NV)) + [0] * (16 - NV), np.float64)[:, None]
    use0 = np.array([1.0] * NV + [0.0] * (16 - NV))[:, None]
    wp = np.where(v > 0, 2.0, 1.0) / (NY * NX)
    wz = np.where(v0 > 0, 2.0, 1.0) * use0 / (NY * NX)
    weights = np.concatenate([wp, -wp, wp, -wp, wz, -wz], 0)
    es = []
    for k in LEVELS:
        h = k // 2
        ty, tx = np.meshgrid(np.arange(k) - h, np.arange(k) - h, indexing="ij")
        for bucket in (0, 1):
            sy, sx = (ty, tx) if bucket == 0 else (tx, ty)
            py = sy.reshape(1, -1) * wu
            px = sx.reshape(1, -1) * wv
            plus = u * py + v * px
            minus = -u * py + v * px
            zero = v0 * px
            e = [np.cos(plus), np.sin(plus), np.cos(minus), np.sin(minus), np.cos(zero) * use0, np.sin(zero) * use0]
            whole_e = np.zeros((SR, TAPS))
            whole_e[:, : k * k] = np.concatenate(e, 0)
            es.append(np.concatenate([_hi(whole_e), _lo(whole_e)], 1))
    return dict(
        fe=three(fe),
        fo=three(fo),
        ge=three(ge * ROOT_HALF),
        go=three(go * ROOT_HALF),
        fe_back=_hi(fe * ROOT_HALF),
        fo_back=_hi(fo * ROOT_HALF),
        ge_back=_hi(ge),
        go_back=_hi(go),
        es=np.stack(es),
        est=np.stack([np.ascontiguousarray(e.T) for e in es]),
        weights=np.broadcast_to(weights, (SR, 128)).astype(np.float32),
    )


def dot(a, b):
    return jnp.dot(a, b, preferred_element_type=f32)


def dot_nt(a, b):
    return lax.dot_general(a, b, (((1,), (1,)), ((), ())), preferred_element_type=f32)


def dot_tn(a, b):
    return lax.dot_general(a, b, (((0,), (0,)), ((), ())), preferred_element_type=f32)


def gelu_pair(x):
    cdf = 0.5 * lax.erf(x * ROOT_HALF) + 0.5
    return x * cdf, cdf + x * (jnp.exp2(x * x * (-0.5 * LOG2_E)) * INV_ROOT_2PI)


def gelu_scaled(u):
    w = lax.erf(u) * ROOT_HALF + ROOT_HALF
    return u * w, w + u * (jnp.exp2(u * u * -LOG2_E) * (2 * INV_ROOT_2PI))


def split(x):
    hi = x.astype(bf16)
    return hi, (x - hi.astype(f32)).astype(bf16)


def at(base, i, n=16):
    return slice(base + i * n, base + i * n + n)


def weave(products, vector):
    n, m = len(products), len(vector)
    done = 0
    for k, step in enumerate(products):
        step()
        upto = (k + 1) * m // n
        for other in vector[done:upto]:
            other()
        done = upto


def norm_stats(x):
    mean = jnp.mean(x, axis=-1, keepdims=True)
    centred = x - mean
    var = jnp.mean(centred * centred, axis=-1, keepdims=True)
    r = lax.rsqrt(var + EPS)
    return centred * r, r


def sum8(x):
    total = x[0:8]
    for k in range(1, x.shape[0] // 8):
        total = total + x[8 * k : 8 * k + 8]
    return total


def grid_rows(im, y):
    return im * IMG + (y * GW if y < 7 else HALF + (GH - 1 - y) * GW)


def lanes(im):
    return slice(im * C, im * C + C)


(V_G1, V_B1, V_BQ, V_BC, V_HB, V_PB, V_S1, V_G2, V_B2, V_BM2, V_S2, V_BG) = range(12)
VROWS = 16
(S_HB, S_PB, S_S1, S_G2, S_B2, S_BM2, S_S2, S_BQ) = range(8)


def from_native(src, field):
    slots = src.shape[2]
    for lt in range(C // 128):
        for im in range(slots):
            for h in (GH // 2 * GW, HALF + GH // 2 * GW):
                field[lt, im * PITCH_IMAGE + h : im * PITCH_IMAGE + h + 4, :] = jnp.zeros((4, 128), f32)
        for y in range(GH):
            for x in range(GW):
                v = src[y, x, :, 128 * lt : 128 * lt + 128].astype(f32)
                field[lt, pl.ds(grid_rows(0, y) + x, slots, stride=PITCH_IMAGE), :] = v


def field_rows(field, first, n):
    s = pl.ds(pl.multiple_of(first, 8), n)
    return jnp.concatenate([field[lt, s, :] for lt in range(C // 128)], axis=1)


def kernel_prep(x_ref, xrow_o, nb_o, stat_o, field):
    step = pl.program_id(0)

    @pl.when(step == 0)
    def _():
        from_native(x_ref, field)

    lane = lax.broadcasted_iota(jnp.int32, (32, 128), 1)
    for k in range(PAIR // 32):
        s = at(0, k, 32)
        x = field_rows(field, (step * 2 + k // (IMG // 32)) * PITCH_IMAGE + 32 * (k % (IMG // 32)), 32)
        xrow_o[s, :] = x.astype(bf16)
        mean = jnp.mean(x, axis=-1, keepdims=True)
        centred = x - mean
        r = lax.rsqrt(jnp.mean(centred * centred, axis=-1, keepdims=True) + EPS)
        nb_o[s, :] = (centred * r).astype(bf16)
        stat_o[s, :] = jnp.where(lane == 0, mean, r)


def kernel_upstream(counts, cot_ref, up_o, field):
    step = pl.program_id(0)

    @pl.when(step == 0)
    def _():
        from_native(cot_ref, field)

    for im in range(2):
        live = (step * 2 + im < counts[0]).astype(f32)
        for i in range(IMG // 32):
            v = field_rows(field, (step * 2 + im) * PITCH_IMAGE + 32 * i, 32)
            up_o[at(im * IMG, i, 32), :] = (v * live).astype(bf16)


CHAINS = 3
CHAIN = C2 // CHAINS


def staggered(phases):
    lists = [phases(t) for t in range(CHAINS)]
    for turn in range(len(lists[0]) + CHAINS - 1):
        for t in range(CHAINS):
            if 0 <= turn - t < len(lists[t]):
                lists[t][turn - t]()


def sub_tiles(t):
    for k in range(t * CHAIN // 128, (t + 1) * CHAIN // 128):
        lt = k % (C // 128)
        yield k // (C // 128), slice(128 * k, 128 * k + 128), slice(128 * lt, 128 * lt + 128)


def spread_gates(gates, wide):
    for k in range(4):
        for i in range(PAIR // 32):
            s = at(0, i, 32)
            wide[k, s, :] = jnp.broadcast_to(gates[s, k : k + 1], (32, 128))


def kernel_forward(
    gx, gy, mod_len, small_len, bucket, pos, x_ref, stat, own, oth, es, fe, fo, ge, go,
    q_o, gates_o, mixed_o, z_o, g_o, spec_o, mean_o, wf, wh, wp, vec, bm1, kcat,
    h_o, normed, ctx, ecat, ocat, s_a, s_b, s_e, s_o, yca, ycb, mix, wide, flat, small, moved, spread, turned,
):
    step = pl.program_id(0)

    @pl.when(step == 0)
    def _():
        unpack_mod(gx, gy, mod_len, small_len, pos, own, oth, wf, wh, wp, vec, bm1, kcat, flat, small, moved, spread, turned)
        for lb in range(6):
            h_o[lb] = dot(es[lb], kcat[lb // 2])

    g1, b1 = vec[V_G1 : V_G1 + 1, :], vec[V_B1 : V_B1 + 1, :]
    for i in range(PAIR // 32):
        s = at(0, i, 32)
        n = (x_ref[s, :].astype(f32) - stat[s, 0:1]) * stat[s, 1:2]
        normed[s, :] = (n * g1 + b1).astype(bf16)
    right = dot(normed[...], wf[:, C + 128 :])
    left = dot(normed[...], wf[:, : C + 128])
    ctx[:, :128] = left[:, C:] + vec[V_BC : V_BC + 1, :128]
    ctx[:, 128:] = right[:, : C - 128] + vec[V_BC : V_BC + 1, 128:]
    gates_o[...] = right[:, C - 128 :] + vec[V_BG : V_BG + 1, :GATES]
    q_o[...] = left[:, :C] + vec[V_BQ : V_BQ + 1, :]
    spread_gates(gates_o, wide)
    lbs = [[level * 2 + bucket[step * 2 + im] for im in range(2)] for level in range(3)]

    def put(dst, off, width, ls, i, val, level):
        if level == 2:
            dst[at(off, i), ls] = val.astype(bf16)
            return
        hi, lo = split(val)
        dst[at(off, i), ls] = hi
        dst[at(off + width, i), ls] = lo

    def put_pair(ls, i, top, bot, level):
        put(ecat, 0, HALF, ls, i, top + bot, level)
        put(ocat, 0, HALF, ls, i, top - bot, level)

    def first(t):
        for im, ls, hs in sub_tiles(t):
            for i in range(HALF // 16):
                put_pair(ls, i, ctx[at(im * IMG, i), hs], ctx[at(im * IMG + HALF, i), hs], 0)

    def product(mat, ref, width, ts, level):
        hi = ref[:width, ts]
        if level == 2:
            return dot(mat[:, :width], hi)
        return dot(mat[...], jnp.concatenate([hi, hi, ref[width:, ts]], axis=0))

    def transform(t, level):
        ts = slice(t * CHAIN, (t + 1) * CHAIN)
        s_a[:, ts] = product(fe, ecat, HALF, ts, level)
        s_b[:, ts] = product(fo, ocat, HALF, ts, level)

    def back(t, level):
        ts = slice(t * CHAIN, (t + 1) * CHAIN)
        s_e[:, ts] = product(ge, yca, AR, ts, level)
        s_o[:, ts] = product(go, ycb, BR, ts, level)

    def filt(t, level):
        base = level * SR
        for im, ls, hs in sub_tiles(t):
            lb = lbs[level][im]
            for i in range(Q // 16):
                a_re, a_im = s_a[at(0, i), ls], s_a[at(Q + 16, i), ls]
                b_re, b_im = s_b[at(0, i), ls], s_b[at(Q, i), ls]
                xp_re, xp_im = a_re + b_im, a_im - b_re
                xm_re, xm_im = a_re - b_im, a_im + b_re
                spec_o[at(base, i), ls] = xp_re.astype(bf16)
                spec_o[at(base + Q, i), ls] = xp_im.astype(bf16)
                spec_o[at(base + 2 * Q, i), ls] = xm_re.astype(bf16)
                spec_o[at(base + 3 * Q, i), ls] = xm_im.astype(bf16)
                p_re, p_im = h_o[lb, at(0, i), hs], h_o[lb, at(Q, i), hs]
                q_re, q_im = h_o[lb, at(2 * Q, i), hs], h_o[lb, at(3 * Q, i), hs]
                yp_re, yp_im = p_re * xp_re - p_im * xp_im, p_re * xp_im + p_im * xp_re
                ym_re, ym_im = q_re * xm_re - q_im * xm_im, q_re * xm_im + q_im * xm_re
                for dst, off, width, val in (
                    (yca, 0, AR, yp_re + ym_re),
                    (yca, Q + 16, AR, yp_im + ym_im),
                    (ycb, 0, BR, ym_im - yp_im),
                    (ycb, Q, BR, yp_re - ym_re),
                ):
                    put(dst, off, width, ls, i, val, level)
            x_re, x_im = s_a[Q : Q + 16, ls], s_a[2 * Q + 16 : 2 * Q + 32, ls]
            spec_o[base + 4 * Q : base + 4 * Q + 16, ls] = x_re.astype(bf16)
            spec_o[base + 4 * Q + 16 : base + 4 * Q + 32, ls] = x_im.astype(bf16)
            p_re, p_im = h_o[lb, 4 * Q : 4 * Q + 16, hs], h_o[lb, 4 * Q + 16 : 4 * Q + 32, hs]
            for off, val in ((Q, p_re * x_re - p_im * x_im), (2 * Q + 16, p_re * x_im + p_im * x_re)):
                put(yca, off, AR, ls, 0, val, level)

    def act(t, level):
        for im, ls, hs in sub_tiles(t):
            total = jnp.zeros((8, 128), f32)
            for i in range(HALF // 16):
                even, odd = s_e[at(0, i), ls], s_o[at(0, i), ls]
                both = []
                for h, a in ((0, even + odd), (HALF, even - odd)):
                    z, g = gelu_scaled(a)
                    z_o[at(level * IMG + h, i), ls] = z.astype(bf16)
                    g_o[at(level * IMG + h, i), ls] = g.astype(bf16)
                    s = at(im * IMG + h, i)
                    part = z * wide[level, s, :]
                    mix[s, hs] = part if level == 0 else mix[s, hs] + part
                    both.append(z)
                if level < 2:
                    put_pair(ls, i, both[0], both[1], level + 1)
                else:
                    total = total + sum8(both[0]) + sum8(both[1])
            if level == 2:
                mean = jnp.sum(total, axis=0, keepdims=True) * (1.0 / (GH * GW))
                mean_o[:, ls] = jnp.broadcast_to(mean, (8, 128))
                glob, _ = gelu_pair(mean)
                for i in range(IMG // 16):
                    s = at(im * IMG, i)
                    mixed_o[s, hs] = (mix[s, hs] + wide[3, s, :] * glob).astype(bf16)

    def phases(t):
        steps = [lambda: first(t)]
        for level in range(3):
            steps += [
                lambda level=level: transform(t, level),
                lambda level=level: filt(t, level),
                lambda level=level: back(t, level),
                lambda level=level: act(t, level),
            ]
        return steps

    staggered(phases)


def kernel_middle(
    gx, gy, mlp_len, pos, x_ref, up, mixed, q_ref, wh, wp, vec, bm1, *refs,
):
    blocks = refs[: gy // 2]
    (
        dmid_o, out_o, dq_o, dmix_o, own, oth, gwh, gwp, sums, bsum,
        mod, modulated, branch, mid, second, dshr, shr, dsec, act, dexp, hid, dact, dbr, dm2, dmod, vacc, bacc, gw1, gw2, flat,
        w1, w2,
    ) = refs[gy // 2 :]
    step = pl.program_id(0)
    start = step == 0

    @pl.when(start)
    def _():
        for ref in (gwh, gwp, vacc, bacc):
            ref[...] = jnp.zeros_like(ref)
        unpack_mlp(gx, gy, mlp_len, pos, blocks, w1, w2, flat)

    def add_to(ref, rows_at, cols, v):
        ref[rows_at, cols] = jnp.where(start, 0.0, ref[rows_at, cols]) + v

    g2, b2 = vec[V_G2 : V_G2 + 1, :], vec[V_B2 : V_B2 + 1, :]
    s1, s2 = vec[V_S1 : V_S1 + 1, :], vec[V_S2 : V_S2 + 1, :]
    bm2 = vec[V_BM2 : V_BM2 + 1, :]

    mod[...] = dot(mixed[...], wh[...]) + vec[V_HB : V_HB + 1, :]
    for i in range(BROWS // 32):
        s = at(0, i, 32)
        modulated[s, :] = (q_ref[s, :] * mod[s, :]).astype(bf16)
        dshr[s, :] = (up[s, :].astype(f32) * s2).astype(bf16)
    branch[...] = dot(modulated[...], wp[...]) + vec[V_PB : V_PB + 1, :]
    for i in range(BROWS // 32):
        s = at(0, i, 32)
        middle = x_ref[s, :].astype(f32) + s1 * branch[s, :]
        mid[s, :] = middle
        n, _ = norm_stats(middle)
        second[s, :] = (n * g2 + b2).astype(bf16)

    chunks = [slice(h * HCHUNK, (h + 1) * HCHUNK) for h in range(HID // HCHUNK)]

    def enter(h):
        def into(t, k):
            ls = slice(h * HCHUNK + 256 * t, h * HCHUNK + 256 * t + 256)
            if k == 0:
                hid[h % 2, :, 256 * t : 256 * t + 256] = dot(second[...], w1[:, ls]) + bm1[0:1, ls]
            else:
                dact[h % 2, :, 256 * t : 256 * t + 256] = dot_nt(dshr[...], w2[ls, :])

        return [functools.partial(into, t, k) for t in range(HCHUNK // 256) for k in range(2)]

    def gelu(h):
        totals = []

        def rows_of(i):
            s = at(0, i)
            z, g = gelu_pair(hid[h % 2, s, :])
            act[s, chunks[h]] = z.astype(bf16)
            d = dact[h % 2, s, :] * g
            dexp[s, chunks[h]] = d.astype(bf16)
            totals.append(sum8(d) if not totals else totals.pop() + sum8(d))

        def close():
            bacc[:, chunks[h]] += totals[0]

        return [functools.partial(rows_of, i) for i in range(BROWS // 16)] + [close]

    def weight_grads(h):
        def one(t):
            ls = slice(h * HCHUNK + 256 * t, h * HCHUNK + 256 * t + 256)
            add_to(gw1, slice(None), ls, dot_tn(second[...], dexp[:, ls]))

        def two():
            add_to(gw2, chunks[h], slice(None), dot_tn(act[:, chunks[h]], dshr[...]))

        return [functools.partial(one, t) for t in range(HCHUNK // 256)] + [two]

    for step_of in enter(0):
        step_of()
    weave(enter(1), gelu(0))
    weave(enter(2) + weight_grads(0), gelu(1))
    weave(weight_grads(1), gelu(2))
    shr[...] = dot(act[...], w2[...])
    dsec[...] = dot_nt(dexp[...], w1[...])

    tally = {}

    def count(key, v):
        tally[key] = tally[key] + sum8(v) if key in tally else sum8(v)

    def finish(i):
        s = at(0, i, 32)
        middle = mid[s, :]
        u = up[s, :].astype(f32)
        shrunk = shr[s, :] + bm2
        out_o[s, :] = (middle + s2 * shrunk).astype(bf16)
        n, r = norm_stats(middle)
        d = dsec[s, :]
        e = d * g2
        dn = d * n
        dv = r * (e - jnp.mean(e, axis=-1, keepdims=True) - n * jnp.mean(e * n, axis=-1, keepdims=True))
        dm = u + dv
        dmid_o[s, :] = dm
        db = s1 * dm
        dbr[s, :] = db.astype(bf16)
        count(S_S1, dm * branch[s, :])
        count(S_G2, dn)
        count(S_B2, d)
        count(S_BM2, dshr[s, :].astype(f32))
        count(S_S2, u * shrunk)
        count(S_PB, db)

    weave(weight_grads(2), [functools.partial(finish, i) for i in range(BROWS // 32)])
    dmod[...] = dot_nt(dbr[...], wp[...])

    def demod(i):
        s = at(0, i, 32)
        dm = dmod[s, :]
        dq = dm * mod[s, :]
        dd = dm * q_ref[s, :]
        dq_o[s, :] = dq.astype(bf16)
        dm2[s, :] = dd.astype(bf16)
        count(S_BQ, dq)
        count(S_HB, dd)

    def grad_wp():
        gwp[...] += dot_tn(modulated[...], dbr[...])

    weave([grad_wp], [functools.partial(demod, i) for i in range(BROWS // 32)])
    dmix_o[...] = dot_nt(dm2[...], wh[...])
    gwh[...] += dot_tn(mixed[...], dm2[...])

    for key, v in tally.items():
        vacc[key] += v

    @pl.when(step == pl.num_programs(0) - 1)
    def _():
        for k in range(8):
            sums[k : k + 1, :] = jnp.sum(vacc[k], axis=0, keepdims=True)
        bsum[...] = jnp.broadcast_to(jnp.sum(bacc[...], axis=0, keepdims=True), bsum.shape)
        pack_mlp(gx, gy, mlp_len, pos, gw1, gw2, own, oth, flat)


def kernel_backward(
    gx, gy, mod_len, small_len,
    bucket, pos, nb_ref, dq_ref, dmix, gates, z_ref, g_ref, spec, mean_ref, kcat, vec, sums, bsum, es, weights,
    fe, fo, ge, go, wf_far, gwh_far, gwp_far, est_far,
    dmer, own, oth,
    gwf, fsum, gb, dk, h_ref, ecat, ocat, s_a, s_b, s_e, s_o, yca, ycb, acc, facc, wide, flat, small, moved, spread,
    wf, gwh, gwp, est, sems,
):
    step = pl.program_id(0)
    last = pl.num_programs(0) - 1
    late = [
        pltpu.make_async_copy(src, dst, sems.at[k])
        for k, (src, dst) in enumerate(((wf_far, wf), (gwh_far, gwh), (gwp_far, gwp), (est_far, est)))
    ]

    @pl.when(step == 0)
    def _():
        for copy in late:
            copy.start()
        for ref in (gwf, facc, acc):
            ref[...] = jnp.zeros_like(ref)
        for lb in range(6):
            h_ref[lb] = dot(es[lb], kcat[lb // 2])

    spread_gates(gates, wide)
    lbs = [[level * 2 + bucket[step * 2 + im] for im in range(2)] for level in range(3)]
    globs = [gelu_pair(mean_ref[0:1, lanes(im)]) for im in range(2)]
    lane = lax.broadcasted_iota(jnp.int32, (16, GATES), 1)
    dmeans = {}

    def mean_grad(t):
        for im, ls, hs in sub_tiles(t):
            total = jnp.zeros((8, 128), f32)
            for i in range(IMG // 16):
                s = at(im * IMG, i)
                total = total + sum8(dmix[s, hs] * wide[3, s, :])
            dmeans[ls.start] = jnp.sum(total, axis=0, keepdims=True) * globs[im][1][:, hs] * (1.0 / (GH * GW))

    def gate_grad(part):
        t_g = jnp.zeros((8, GATES), f32)
        n = 2 * (HALF // 16) // CHAINS
        for im, i in [(im, i) for im in range(2) for i in range(HALF // 16)][part * n : part * n + n]:
            for h in (0, HALF):
                s = at(im * IMG + h, i)
                dm = dmix[s, :]
                dg = jnp.zeros((16, GATES), f32)
                for k in range(4):
                    other = z_ref[at(k * IMG + h, i), lanes(im)].astype(f32) if k < 3 else globs[im][0]
                    col = jnp.sum(dm * other, axis=-1, keepdims=True)
                    dg = jnp.where(lane == k, col, dg)
                dmer[s, :C] = dq_ref[s, :]
                dmer[s, C2:] = dg.astype(bf16)
                t_g = t_g + sum8(dg)
        facc[:, C2:] += t_g

    def before(t, level):
        for im, ls, hs in sub_tiles(t):
            for i in range(HALF // 16):
                if level < 2:
                    even, odd = s_e[at(0, i), ls], s_o[at(0, i), ls]
                    through = (even + odd, even - odd)
                else:
                    through = (dmeans[ls.start], dmeans[ls.start])
                parts = []
                for k, h in enumerate((0, HALF)):
                    s = at(im * IMG + h, i)
                    dz = wide[level, s, :] * dmix[s, hs] + through[k]
                    parts.append(dz * g_ref[at(level * IMG + h, i), ls].astype(f32))
                ecat[at(0, i), ls] = (parts[0] + parts[1]).astype(bf16)
                ocat[at(0, i), ls] = (parts[0] - parts[1]).astype(bf16)

    def transform(t):
        ts = slice(t * CHAIN, (t + 1) * CHAIN)
        s_a[:, ts] = dot(fe[...], ecat[:, ts])
        s_b[:, ts] = dot(fo[...], ocat[:, ts])

    def back(t):
        ts = slice(t * CHAIN, (t + 1) * CHAIN)
        s_e[:, ts] = dot(ge[...], yca[:, ts])
        s_o[:, ts] = dot(go[...], ycb[:, ts])

    def filt(t, level):
        base = level * SR
        for im, ls, hs in sub_tiles(t):
            lb = lbs[level][im]
            for i in range(Q // 16):
                a_re, a_im = s_a[at(0, i), ls], s_a[at(Q + 16, i), ls]
                b_re, b_im = s_b[at(0, i), ls], s_b[at(Q, i), ls]
                dp_re, dp_im = a_re + b_im, a_im - b_re
                dm_re, dm_im = a_re - b_im, a_im + b_re
                xp_re, xp_im = spec[at(base, i), ls].astype(f32), spec[at(base + Q, i), ls].astype(f32)
                xm_re, xm_im = spec[at(base + 2 * Q, i), ls].astype(f32), spec[at(base + 3 * Q, i), ls].astype(f32)
                acc[lb, at(0, i), hs] += xp_re * dp_re + xp_im * dp_im
                acc[lb, at(Q, i), hs] += xp_im * dp_re - xp_re * dp_im
                acc[lb, at(2 * Q, i), hs] += xm_re * dm_re + xm_im * dm_im
                acc[lb, at(3 * Q, i), hs] += xm_im * dm_re - xm_re * dm_im
                p_re, p_im = h_ref[lb, at(0, i), hs], h_ref[lb, at(Q, i), hs]
                q_re, q_im = h_ref[lb, at(2 * Q, i), hs], h_ref[lb, at(3 * Q, i), hs]
                yp_re, yp_im = p_re * dp_re + p_im * dp_im, p_re * dp_im - p_im * dp_re
                ym_re, ym_im = q_re * dm_re + q_im * dm_im, q_re * dm_im - q_im * dm_re
                yca[at(0, i), ls] = (yp_re + ym_re).astype(bf16)
                yca[at(Q + 16, i), ls] = (yp_im + ym_im).astype(bf16)
                ycb[at(0, i), ls] = (ym_im - yp_im).astype(bf16)
                ycb[at(Q, i), ls] = (yp_re - ym_re).astype(bf16)
            d_re, d_im = s_a[Q : Q + 16, ls], s_a[2 * Q + 16 : 2 * Q + 32, ls]
            x_re = spec[base + 4 * Q : base + 4 * Q + 16, ls].astype(f32)
            x_im = spec[base + 4 * Q + 16 : base + 4 * Q + 32, ls].astype(f32)
            acc[lb, 4 * Q : 4 * Q + 16, hs] += x_re * d_re + x_im * d_im
            acc[lb, 4 * Q + 16 : 4 * Q + 32, hs] += x_im * d_re - x_re * d_im
            p_re, p_im = h_ref[lb, 4 * Q : 4 * Q + 16, hs], h_ref[lb, 4 * Q + 16 : 4 * Q + 32, hs]
            yca[Q : Q + 16, ls] = (p_re * d_re + p_im * d_im).astype(bf16)
            yca[2 * Q + 16 : 2 * Q + 32, ls] = (p_re * d_im - p_im * d_re).astype(bf16)

    def context(t):
        for im, ls, hs in sub_tiles(t):
            ds = slice(C + hs.start, C + hs.stop)
            total = jnp.zeros((8, 128), f32)
            for i in range(HALF // 16):
                even, odd = s_e[at(0, i), ls], s_o[at(0, i), ls]
                top, bot = even + odd, even - odd
                dmer[at(im * IMG, i), ds] = top.astype(bf16)
                dmer[at(im * IMG + HALF, i), ds] = bot.astype(bf16)
                total = total + sum8(top) + sum8(bot)
            facc[:, ds] += total

    def phases(t):
        steps = [lambda: mean_grad(t)]
        for level in (2, 1, 0):
            steps += [
                lambda level=level: before(t, level),
                lambda: transform(t),
                lambda level=level: filt(t, level),
                lambda: back(t),
            ]
            if level == 2:
                steps.append(lambda: gate_grad(t))
        return steps + [lambda: context(t)]

    staggered(phases)
    gwf[...] += dot_tn(nb_ref[...], dmer[...])

    @pl.when(step == last)
    def _():
        for copy in late:
            copy.wait()
        facc[:, :C] = jnp.broadcast_to(sums[S_BQ : S_BQ + 1, :] * 0.125, (8, C))
        colsum = jnp.sum(facc[...], axis=0, keepdims=True)
        fsum[...] = jnp.broadcast_to(colsum, fsum.shape)
        wide = wf[...].astype(f32)
        t_hi, t_lo = split(wide * gwf[...])
        ones = jnp.ones((8, MERGED), bf16)
        gb[0:8, :] = dot_nt(ones, t_hi) + dot_nt(ones, t_lo)
        c_hi, c_lo = split(fsum[...])
        gb[8:16, :] = dot_nt(c_hi, wf[...]) + dot_nt(c_lo, wf[...])
        g1 = jnp.transpose(jnp.broadcast_to(vec[V_G1 : V_G1 + 1, :], (128, C)))
        b1 = jnp.transpose(jnp.broadcast_to(vec[V_B1 : V_B1 + 1, :], (128, C)))
        for t in range(MERGED // 128):
            ls = slice(128 * t, 128 * t + 128)
            gwf[:, ls] = gwf[:, ls] * g1 + b1 * fsum[0:1, ls]
        for level in range(3):
            total = None
            for lb in (level * 2, level * 2 + 1):
                hi, lo = split(acc[lb] * jnp.concatenate([weights[...]] * (C // 128), 1))
                first = dot(est[lb], hi)
                term = first[:TAPS] + first[TAPS:] + dot(est[lb, :TAPS, :], lo)
                total = term if total is None else total + term
            dk[level] = total
        pack_mod(gx, gy, mod_len, small_len, pos, gwf, gwh, gwp, sums, bsum, fsum, gb, dk, own, oth, flat, small, moved, spread)


def to_native(rows_ref, first, native, slot, slots, gain):
    line = GW * slots
    for y in range(GH):
        a = first + grid_rows(0, y)
        for lt in range(C // 128):
            v = rows_ref[a : a + GW, 128 * lt : 128 * lt + 128]
            native[lt, pl.ds(line * y + slot, GW, stride=slots), :] = v if gain is None else v * gain


def write_native(native, out, slots):
    line = GW * slots
    for y in range(GH):
        for lt in range(C // 128):
            v = native[lt, line * y : line * (y + 1), :].reshape(GW, slots, 128)
            out[y, :, :, 128 * lt : 128 * lt + 128] = v.astype(out.dtype)


def kernel_tail(dmer, wf, x_ref, stat, dmid, vec, gtok_o, stage, native):
    step = pl.program_id(0)
    slots = gtok_o.shape[2]
    g1 = vec[V_G1 : V_G1 + 1, :]
    d_normed = dot_nt(dmer[...], wf[...])
    for i in range(PAIR // 32):
        s = at(0, i, 32)
        r = stat[s, 1:2]
        n = (x_ref[s, :].astype(f32) - stat[s, 0:1]) * r
        e = d_normed[s, :] * g1
        dv = e - jnp.mean(e, axis=-1, keepdims=True) - n * jnp.mean(e * n, axis=-1, keepdims=True)
        stage[s, :] = dmid[s, :] + r * dv
    for im in range(2):
        to_native(stage, im * IMG, native, step * 2 + im, slots, None)

    @pl.when(step == pl.num_programs(0) - 1)
    def _():
        write_native(native, gtok_o, slots)


def kernel_out(counts, rows_ref, out_o, native, wide):
    slots = out_o.shape[2]
    wide[...] = rows_ref[...].astype(f32)
    for im in range(slots):
        to_native(wide, im * IMG, native, im, slots, (im < counts[0]).astype(f32))
    write_native(native, out_o, slots)


def block_rows(length):
    return 8 * (length // 1024 if length % 1024 == 0 else (length + 1022) // 1024 + 1)


def place(shard, device):
    length = shard.shape[0]
    n = block_rows(length) * 128
    if n == length:
        return shard.reshape(-1, 128)
    offset = lax.rem(device * length, 1024)
    return lax.dynamic_update_slice(jnp.zeros((n,), shard.dtype), shard, (offset,)).reshape(-1, 128)


def take(block, length, device):
    flat = block.reshape(-1)
    if flat.shape[0] == length:
        return flat
    return lax.dynamic_slice(flat, (lax.rem(device * length, 1024),), (length,))


def first_row(length, device):
    return pl.multiple_of((device * length) // 1024 * 8, 8)


def device_at(pos, gy, i, j, c):
    return (pos[0] ^ j) * gy + (pos[1] ^ (2 * i + c))


def join(first, second, sh):
    lane = lax.broadcasted_iota(jnp.int32, first.shape, 1)
    return jnp.where(lane < 128 - sh, first, second)


def turn(v, sh):
    return pltpu.roll(v, 128 - sh, 1) if sh else v


def shift_right(first, second, sh):
    lane = lax.broadcasted_iota(jnp.int32, first.shape, 1)
    return jnp.where(lane < sh, pltpu.roll(first, sh, 1), pltpu.roll(second, sh, 1))


WIDE = C2 + 4
WF_ROWS = C * WIDE // 128
W_ROWS = C * C // 128
PERIOD = 32
PITCH_IMAGE = IMG + 8
PITCH_Q = 24
PITCH_P = 40
STRIDE = PERIOD * WIDE // 128
K_ROW = 12
TAIL_ROW = K_ROW + 83 * C // 128
B_HB, B_PB, B_S1, B_G2, B_B2, B_BM1 = (TAIL_ROW + 3 * k for k in range(6))
B_BM2 = B_BM1 + HID // 128
B_S2 = B_BM2 + 3
END_ROW = B_S2 + 3


def by_threes(flat, base, n, temp, out):
    for g in range(n // 64):
        room = 192 * (g % 4)
        for k in range(8):
            for b in range(3):
                src = base + 192 * g + 24 * k + 8 * b
                temp[pl.ds(room + 64 * b + k, 8, stride=8), :] = flat[src : src + 8, :]
        for i in range(24):
            rows_at = 768 + 64 * ((g % 4) * 3 + i % 3) + i // 3
            temp[pl.ds(rows_at, 8, stride=8), :] = temp[room + 8 * i : room + 8 * i + 8, :]
        for t in range(3):
            first = 768 + 64 * ((g % 4) * 3 + t)
            out[64 * g : 64 * g + 64, 128 * t : 128 * t + 128] = temp[first : first + 64, :].astype(bf16)


def unpack_mod(gx, gy, mod_len, small_len, pos, own, oth, wf_o, wh_o, wp_o, vec_o, bm1_o, kcat_o, flat, small, moved, wide, turned):
    flat[...] = jnp.zeros_like(flat)
    small[...] = jnp.zeros_like(small)
    mr, sr = block_rows(mod_len), block_rows(small_len)
    for i in range(gy // 2):
        for j in range(gx):
            for c, src in enumerate((own, oth)):
                d = device_at(pos, gy, i, j, c)
                block = src[i, j].astype(f32)
                flat[pl.ds(first_row(mod_len, d), mr), :] += block[:mr]
                small[pl.ds(first_row(small_len, d), sr), :] += block[mr : mr + sr]
    lane = lax.broadcasted_iota(jnp.int32, (16, 128), 1)
    for q in range(C // PERIOD):
        for f in range(0, STRIDE + 7, 8):
            turned[pl.ds(PITCH_Q * f + q, 8, stride=PITCH_Q), :] = flat[STRIDE * q + f : STRIDE * q + f + 8, :]
    for p in range(PERIOD):
        row, sh = WIDE * p // 128, WIDE * p % 128
        first = [PITCH_Q * (row + j) for j in range(MERGED // 128 + (1 if sh else 0))]
        tiles = [turn(turned[k : k + 16, :], sh) for k in first]
        for j in range(MERGED // 128):
            v = join(tiles[j], tiles[j + 1], sh) if sh else tiles[j]
            if j == MERGED // 128 - 1:
                v = jnp.where(lane < 4, v, 0.0)
            wide[j, pl.ds(p, 16, stride=PITCH_P), :] = v
    for j in range(MERGED // 128):
        for q in range(C // PERIOD):
            v = wide[j, PITCH_P * q : PITCH_P * q + PERIOD, :]
            wf_o[PERIOD * q : PERIOD * q + PERIOD, 128 * j : 128 * j + 128] = v.astype(bf16)
    by_threes(flat, WF_ROWS, C, turned, wh_o)
    by_threes(flat, WF_ROWS + W_ROWS, C, turned, wp_o)
    n = moved.shape[0]
    moved[...] = join(turn(small[0:n, :], 4), turn(small[1 : n + 1, :], 4), 4)
    vec_o[...] = jnp.zeros_like(vec_o)
    for row, src, start in (
        (V_G1, small, 0), (V_B1, small, 3), (V_BQ, small, 6), (V_BC, small, 9),
        (V_HB, moved, B_HB), (V_PB, moved, B_PB), (V_S1, moved, B_S1), (V_G2, moved, B_G2), (V_B2, moved, B_B2),
        (V_BM2, moved, B_BM2), (V_S2, moved, B_S2),
    ):
        for j in range(3):
            vec_o[row : row + 1, 128 * j : 128 * j + 128] = src[start + j : start + j + 1, :]
    vec_o[V_BG : V_BG + 1, 0:128] = jnp.where(lane[0:1] < 4, small[K_ROW : K_ROW + 1, :], 0.0)
    for t in range(HID // 128):
        bm1_o[:, 128 * t : 128 * t + 128] = jnp.broadcast_to(moved[B_BM1 + t : B_BM1 + t + 1, :], (8, 128))
    start = 0
    for level, k in enumerate(LEVELS):
        for j in range(3):
            taps = moved[pl.ds(K_ROW + 3 * start + j, TAPS, stride=3), :].astype(bf16)
            kcat_o[level, 0:TAPS, 128 * j : 128 * j + 128] = taps
            kcat_o[level, TAPS:, 128 * j : 128 * j + 128] = taps
        start += k * k


def unpack_mlp(gx, gy, mlp_len, pos, blocks, w1_o, w2_o, flat):
    mr = block_rows(mlp_len)
    aligned = mr * 128 == mlp_len
    if not aligned:
        flat[...] = jnp.zeros_like(flat)
    for i, src in enumerate(blocks):
        for j in range(gx):
            for c in range(2):
                rows_at = pl.ds(first_row(mlp_len, device_at(pos, gy, i, j, c)), mr)
                if aligned:
                    flat[rows_at, :] = src[c, j].astype(f32)
                else:
                    flat[rows_at, :] += src[c, j].astype(f32)
    for t in range(HID // 128):
        w1_o[:, 128 * t : 128 * t + 128] = flat[pl.ds(t, C, stride=HID // 128), :].astype(bf16)
    for t in range(C // 128):
        w2_o[:, 128 * t : 128 * t + 128] = flat[pl.ds(C * HID // 128 + t, HID, stride=C // 128), :].astype(bf16)


def send_slots(gx, gy, pos, flat, length, base, own, oth):
    mr = block_rows(length)
    for i in range(gy // 2):
        for j in range(gx):
            for c, dst in enumerate((own, oth)):
                d = device_at(pos, gy, i, j, c)
                dst[i, j, base : base + mr, :] = flat[pl.ds(first_row(length, d), mr), :].astype(bf16)


def pack_mlp(gx, gy, mlp_len, pos, gw1, gw2, own, oth, flat):
    used = 2 * C * HID // 128
    if flat.shape[0] > used:
        flat[used:, :] = jnp.zeros_like(flat[used:, :])
    for t in range(HID // 128):
        flat[pl.ds(t, C, stride=HID // 128), :] = gw1[:, 128 * t : 128 * t + 128]
    for t in range(C // 128):
        flat[pl.ds(C * HID // 128 + t, HID, stride=C // 128), :] = gw2[:, 128 * t : 128 * t + 128]
    send_slots(gx, gy, pos, flat, mlp_len, 0, own, oth)


def pack_mod(gx, gy, mod_len, small_len, pos, gwf, gwh, gwp, sums, bsum, fsum, gb, dk, own, oth, flat, small, moved, wide):
    lane = lax.broadcasted_iota(jnp.int32, (16, 128), 1)
    used = WF_ROWS + 2 * W_ROWS
    if flat.shape[0] > used:
        flat[used:, :] = jnp.zeros_like(flat[used:, :])
    for j in range(MERGED // 128):
        for row in range(0, C, 8):
            dst = pl.ds(PITCH_Q * (row % PERIOD) + row // PERIOD, 8, stride=PITCH_Q)
            wide[j, dst, :] = gwf[row : row + 8, 128 * j : 128 * j + 128]
    turned = {}

    def piece(p, tile):
        tile = min(tile, MERGED // 128 - 1)
        if (p, tile) not in turned:
            turned[p, tile] = turn(wide[tile, PITCH_Q * p : PITCH_Q * p + 16, :], -WIDE * p % 128)
        return turned[p, tile]

    for f in range(STRIDE):
        p = 128 * f // WIDE
        col = 128 * f - WIDE * p
        t, sh = col // 128, col % 128
        v = join(piece(p, t), piece(p, t + 1), sh) if sh else piece(p, t)
        left = WIDE - col
        if left < 128:
            v = jnp.where(lane < left, v, piece(p + 1, 0))
        flat[pl.ds(f, 16, stride=STRIDE), :] = v
    for j in range(3):
        ls = slice(128 * j, 128 * j + 128)
        flat[pl.ds(WF_ROWS + j, C, stride=3), :] = gwh[:, ls]
        flat[pl.ds(WF_ROWS + W_ROWS + j, C, stride=3), :] = gwp[:, ls]
    moved[...] = jnp.zeros_like(moved)
    small[...] = jnp.zeros_like(small)
    start = 0
    for level, k in enumerate(LEVELS):
        for j in range(3):
            moved[pl.ds(K_ROW + 3 * start + j, k * k, stride=3), :] = dk[level, 0 : k * k, 128 * j : 128 * j + 128]
        start += k * k
    for start, row in (
        (B_HB, S_HB), (B_PB, S_PB), (B_S1, S_S1), (B_G2, S_G2), (B_B2, S_B2), (B_BM2, S_BM2), (B_S2, S_S2),
    ):
        for j in range(3):
            moved[start + j : start + j + 1, :] = sums[row : row + 1, 128 * j : 128 * j + 128]
    for t in range(HID // 128):
        moved[B_BM1 + t : B_BM1 + t + 1, :] = bsum[0:1, 128 * t : 128 * t + 128]
    n = moved.shape[0]
    small[8:n, :] = shift_right(moved[7 : n - 1, :], moved[8:n, :], 4)
    for j in range(3):
        ls = slice(128 * j, 128 * j + 128)
        small[j : j + 1, :] = gb[0:1, ls]
        small[3 + j : 4 + j, :] = gb[8:9, ls]
        small[6 + j : 7 + j, :] = fsum[0:1, ls]
        small[9 + j : 10 + j, :] = fsum[0:1, C + 128 * j : C + 128 * j + 128]
    gate_lane = lane[0:1] < 4
    small[K_ROW : K_ROW + 1, :] = jnp.where(gate_lane, fsum[0:1, C2:], small[K_ROW : K_ROW + 1, :])
    mr, sr = block_rows(mod_len), block_rows(small_len)
    send_slots(gx, gy, pos, flat, mod_len, 0, own, oth)
    for i in range(gy // 2):
        for j in range(gx):
            for c, dst in enumerate((own, oth)):
                block = small[pl.ds(first_row(small_len, device_at(pos, gy, i, j, c)), sr), :]
                pad = own.shape[2] - mr - sr
                if pad:
                    block = jnp.concatenate([block, jnp.zeros((pad, 128), f32)], 0)
                dst[i, j, mr:, :] = block.astype(bf16)


def kernel_add(n_in, *refs):
    for k, o in enumerate(refs[n_in:]):
        total = None
        for ref in refs[:n_in]:
            v = ref[k].astype(f32)
            total = v if total is None else total + v
        o[...] = total.astype(o.dtype)


def kernel_cut(cuts, *refs):
    outs = refs[-len(cuts) :]
    for o, (first, n) in zip(outs, cuts):
        total = None
        for ref in refs[: -len(cuts)]:
            v = ref[first : first + n, :].astype(f32)
            total = v if total is None else total + v
        o[...] = total


def full(shape):
    return pl.BlockSpec(shape, lambda *i, n=len(shape): (0,) * n)


def rows(n, width):
    return pl.BlockSpec((n, width), lambda i: (i, 0))


def smem():
    return pl.BlockSpec(memory_space=pltpu.SMEM)


def sds(shape, dtype):
    return jax.ShapeDtypeStruct(shape, dtype)


def call(kernel, name, grid, ins, outs, scratch, mib, micros):
    return pl.pallas_call(
        kernel,
        grid=grid,
        in_specs=[s for _, s in ins],
        out_shape=[o for o, _ in outs],
        out_specs=[s for _, s in outs],
        scratch_shapes=[pltpu.VMEM(*v) if isinstance(v, tuple) else v for v in scratch],
        compiler_params=pltpu.CompilerParams(vmem_limit_bytes=mib * 2**20),
        cost_estimate=pl.CostEstimate(flops=int(micros * 1e9), bytes_accessed=int(micros * 1e6), transcendentals=0),
        name=name,
    )(*[a for a, _ in ins])


def whole(*arrays):
    return [(a, full(a.shape)) for a in arrays]


def by_rows(n, *arrays):
    return [(a, rows(n, a.shape[1])) for a in arrays]


def native_rows(slots):
    return ((C // 128, GH * GW * slots, 128), f32)


def prep(tokens):
    slots = tokens.shape[2]
    n = slots * IMG
    outs = [(sds((n, w), t), rows(PAIR, w)) for w, t in ((C, bf16), (C, bf16), (128, f32))]
    return call(kernel_prep, "prep", (slots // 2,), whole(tokens), outs, [((C // 128, slots * PITCH_IMAGE, 128), f32)], 60, 4)


def upstream(counts, cotangent):
    slots = cotangent.shape[2]
    ins = [(counts, smem())] + whole(cotangent)
    outs = [(sds((slots * IMG, C), bf16), rows(PAIR, C))]
    return call(kernel_upstream, "upstream", (slots // 2,), ins, outs, [((C // 128, slots * PITCH_IMAGE, 128), f32)], 60, 3)[0]


def forward(gx, gy, pos, xrow, stat, bucket, own, oth, mod_len, small_len):
    con = constants()
    pairs = xrow.shape[0] // PAIR
    n = pairs * PAIR
    outs = [
        (sds((n, C), f32), rows(PAIR, C)),
        (sds((n, GATES), f32), rows(PAIR, GATES)),
        (sds((n, C), bf16), rows(PAIR, C)),
        (sds((pairs * 3 * IMG, C2), bf16), rows(3 * IMG, C2)),
        (sds((pairs * 3 * IMG, C2), bf16), rows(3 * IMG, C2)),
        (sds((pairs * 3 * SR, C2), bf16), rows(3 * SR, C2)),
        (sds((pairs * 8, C2), f32), rows(8, C2)),
    ]
    weights = [((C, MERGED), bf16), ((C, C), bf16), ((C, C), bf16), ((VROWS, C), f32), ((8, HID), f32), ((3, 2 * TAPS, C), bf16)]
    outs += [(sds(shape, dtype), full(shape)) for shape, dtype in weights]
    mats = [jnp.asarray(con[k]) for k in ("es", "fe", "fo", "ge", "go")]
    ins = [(bucket, smem()), (pos, smem())] + by_rows(PAIR, xrow, stat) + whole(own, oth, *mats)
    scratch = [
        ((6, SR, C), f32), ((PAIR, C), bf16), ((PAIR, C), f32), ((2 * HALF, C2), bf16), ((2 * HALF, C2), bf16), ((AR, C2), f32), ((BR, C2), f32),
        ((HALF, C2), f32), ((HALF, C2), f32), ((2 * AR, C2), bf16), ((2 * BR, C2), bf16), ((PAIR, C), f32),
        ((4, PAIR, 128), f32),
    ]
    ndev = gx * gy
    flat_rows = max(span(mod_len, ndev), STRIDE * 16 + 8)
    small_rows = max(span(small_len, ndev), END_ROW + 26)
    scratch += [((flat_rows, 128), f32), ((small_rows + 8, 128), f32), ((small_rows, 128), f32)]
    scratch += [((MERGED // 128, max(PITCH_Q * PERIOD, PITCH_P * 16), 128), f32), ((PITCH_Q * (STRIDE + 7), 128), f32)]
    kernel = functools.partial(kernel_forward, gx, gy, mod_len, small_len)
    return call(kernel, "focal_forward", (pairs,), ins, outs, scratch, 58, 28)


def middle(gx, gy, pos, xrow, up, mixed, q, wh, wp, vec, bm1, mlp_blocks, mlp_len):
    n = xrow.shape[0]
    outs = [
        (sds((n, C), f32), rows(BROWS, C)),
        (sds((n, C), bf16), rows(BROWS, C)),
        (sds((n, C), bf16), rows(BROWS, C)),
        (sds((n, C), f32), rows(BROWS, C)),
    ]
    slots = (gy // 2, gx, block_rows(mlp_len), 128)
    outs += [(sds(slots, bf16), full(slots))] * 2
    outs += [(sds(s, f32), full(s)) for s in ((C, C), (C, C), (8, C), (8, HID))]
    ins = [(pos, smem())] + by_rows(BROWS, xrow, up, mixed, q) + whole(wh, wp, vec, bm1, *mlp_blocks)
    blk = (BROWS, C)
    scratch = [
        (blk, f32), (blk, bf16), (blk, f32), (blk, f32), (blk, bf16), (blk, bf16), (blk, f32), (blk, f32),
        ((BROWS, HID), bf16), ((BROWS, HID), bf16), ((2, BROWS, HCHUNK), f32), ((2, BROWS, HCHUNK), f32), (blk, bf16), (blk, bf16), (blk, f32),
        ((8, 8, C), f32), ((8, HID), f32),
        ((C, HID), f32), ((HID, C), f32), ((span(mlp_len, gx * gy), 128), f32), ((C, HID), bf16), ((HID, C), bf16),
    ]
    kernel = functools.partial(kernel_middle, gx, gy, mlp_len)
    return call(kernel, "middle", (n // BROWS,), ins, outs, scratch, 60, 42)


def backward(gx, gy, pos, bucket, nb, dq, dmix, gates, z, g, spec, mean, kcat, wf, vec, sums, bsum, gwh, gwp, mod_len, small_len):
    con = constants()
    ndev = gx * gy
    pairs = nb.shape[0] // PAIR
    mats = [jnp.asarray(con[k]) for k in ("es", "weights", "fe_back", "fo_back", "ge_back", "go_back")]
    slots = (gy // 2, gx, -(-(block_rows(mod_len) + block_rows(small_len)) // 16) * 16, 128)
    outs = [(sds((nb.shape[0], MERGED), bf16), rows(PAIR, MERGED))] + [(sds(slots, bf16), full(slots))] * 2
    ins = [(bucket, smem()), (pos, smem())] + by_rows(PAIR, nb, dq, dmix, gates) + by_rows(3 * IMG, z, g) + by_rows(3 * SR, spec)
    ins += by_rows(8, mean) + whole(kcat, vec, sums, bsum, *mats)
    late = (wf, gwh, gwp, jnp.asarray(con["est"]))
    ins += [(v, pl.BlockSpec(memory_space=pl.ANY)) for v in late]
    small_rows = -(-max(span(small_len, ndev), END_ROW + 2) // 8) * 8
    scratch = [
        ((C, MERGED), f32), ((8, MERGED), f32), ((16, C), f32), ((3, TAPS, C), f32), ((6, SR, C), f32),
        ((HALF, C2), bf16), ((HALF, C2), bf16), ((AR, C2), f32), ((BR, C2), f32), ((HALF, C2), f32), ((HALF, C2), f32),
        ((AR, C2), bf16), ((BR, C2), bf16), ((6, SR, C), f32), ((8, MERGED), f32), ((4, PAIR, 128), f32),
        ((max(span(mod_len, ndev), STRIDE * 16 + 8), 128), f32), ((small_rows, 128), f32), ((small_rows, 128), f32),
        ((MERGED // 128, max(PITCH_Q * PERIOD, PITCH_P * 16), 128), f32),
    ]
    scratch += [(v.shape, v.dtype) for v in late] + [pltpu.SemaphoreType.DMA((len(late),))]
    kernel = functools.partial(kernel_backward, gx, gy, mod_len, small_len)
    return call(kernel, "focal_backward", (pairs,), ins, outs, scratch, 58, 28)


def tail(shape, dmer, wf, xrow, stat, dmid, vec):
    slots = shape[2]
    ins = by_rows(PAIR, dmer) + whole(wf) + by_rows(PAIR, xrow, stat, dmid) + whole(vec)
    return call(kernel_tail, "tail", (slots // 2,), ins, [(sds(shape, f32), full(shape))], [((PAIR, C), f32), native_rows(slots)], 24, 8)[0]


def out_tokens(shape, counts, out_rows):
    ins = [(counts, smem())] + whole(out_rows)
    return call(kernel_out, "out_tokens", (), ins, [(sds(shape, bf16), full(shape))], [native_rows(shape[2]), ((shape[2] * IMG, C), f32)], 24, 5)[0]


def span(length, ndev):
    return ((ndev - 1) * length) // 1024 * 8 + block_rows(length)


def add(arrays, outs, name):
    return call(functools.partial(kernel_add, len(arrays)), name, (), whole(*arrays), [(o, full(o.shape)) for o in outs], [], 24, 2)


def swap(x, mask, ndev):
    return lax.ppermute(x, AXES, [(k, k ^ mask) for k in range(ndev)])


def around(x, step, count, ndev):
    return [x] + [swap(x, step * k, ndev) for k in range(1, count)]


def after(values):
    return lax.optimization_barrier(values)


def travel(parts, step, ndev):
    return [parts[0]] + [swap(p, step * k, ndev) for k, p in enumerate(parts) if k]


def kernel_add_parts(n, *refs):
    for k, o in enumerate(refs[n + 1 :]):
        o[...] = (refs[k][...].astype(f32) + refs[n][k].astype(f32)).astype(o.dtype)


def sum_core_parts(own, oth, gx, gy, name):
    got = swap(oth, 1, gx * gy)
    n = gy // 2
    parts = add([own], [sds(own.shape[1:], bf16)] * n, name + "_own")
    outs = [sds(own.shape[1:], f32 if k == 0 else bf16) for k in range(n)]
    kernel = functools.partial(kernel_add_parts, n)
    return call(kernel, name + "_sum_core", (), whole(*parts, got), [(o, full(o.shape)) for o in outs], [], 24, 1)


def sum_core(own, oth, gx, gy, name):
    got = swap(oth, 1, gx * gy)
    return add([own, got], [sds(own.shape[1:], f32 if k == 0 else bf16) for k in range(gy // 2)], name + "_sum_core")


def sum_plane(parts, gx, name):
    shape = parts[0].shape[1:]
    return add(parts, [sds(shape, f32 if k == 0 else bf16) for k in range(gx)], name + "_sum_plane")


def sum_line(parts, cuts, name):
    outs = [(sds((n, 128), f32), full((n, 128))) for _, n in cuts]
    return call(functools.partial(kernel_cut, cuts), name + "_sum_line", (), whole(*parts), outs, [], 24, 2)


def local(gx, gy, tokens, bucket, counts, mod_weights, mlp_weights, small_params, cotangent):
    ndev = gx * gy
    gxi, gyi = lax.axis_index("gx"), lax.axis_index("gy")
    device = gxi * gy + gyi
    pos = jnp.stack([gxi, gyi]).astype(jnp.int32)
    mod_len, small_len, mlp_len = mod_weights.shape[0], small_params.shape[0], mlp_weights.shape[0]
    mr, sr = block_rows(mod_len), block_rows(small_len)

    blocks = [place(mod_weights, device), place(small_params, device)]
    pad = -(mr + sr) % 16
    if pad:
        blocks.append(jnp.zeros((pad, 128), bf16))
    line = around(jnp.concatenate(blocks, 0), gy, gx, ndev)
    native, back = (1, 2, 0, 3), (2, 0, 1, 3)
    shape = (GH, GW) + tokens.shape[:1] + (C,)
    prepared = prep(jnp.transpose(tokens, native))
    line, mlp_mine, prepared = after((line, place(mlp_weights, device), prepared))
    xrow, nb, stat = prepared
    plane = around(jnp.stack(line), 2, gy // 2, ndev)
    mlp_line = jnp.stack(around(mlp_mine, gy, gx, ndev))
    up = upstream(counts, jnp.transpose(cotangent, native))
    plane, mlp_line, up = after((plane, mlp_line, up))
    mlp_other = swap(mlp_line, 1, ndev)
    plane = jnp.stack(plane)
    other = swap(plane, 1, ndev)
    mlp_both = jnp.stack([mlp_line, mlp_other])
    other, mlp_both = after((other, mlp_both))
    mlp_blocks = around(mlp_both, 2, gy // 2, ndev)

    q, gates, mixed, z, g, spec, mean, wf, wh, wp, vec, bm1, kcat = forward(
        gx, gy, pos, xrow, stat, bucket, plane, other, mod_len, small_len
    )
    mlp_blocks, mixed = after((mlp_blocks, mixed))
    dmid, out_rows, dq, dmix, own, oth, gwh, gwp, sums, bsum = middle(
        gx, gy, pos, xrow, up, mixed, q, wh, wp, vec, bm1, mlp_blocks, mlp_len
    )
    parts = sum_core_parts(own, oth, gx, gy, "mlp")
    parts, dmix = after((parts, dmix))
    mlp_plane = travel(parts, 2, ndev)
    dmer, own, oth = backward(
        gx, gy, pos, bucket, nb, dq, dmix, gates, z, g, spec, mean, kcat, wf, vec, sums, bsum, gwh, gwp, mod_len, small_len
    )
    mlp_plane, own, oth = after((mlp_plane, own, oth))
    parts = sum_plane(mlp_plane, gx, "mlp")
    mod_parts = sum_core(own, oth, gx, gy, "mod")
    mlp_line = travel(parts, gy, ndev)
    mod_plane = travel(mod_parts, 2, ndev)
    gtok = tail(shape, dmer, wf, xrow, stat, dmid, vec)
    mod_plane, mlp_line, gtok, out_rows = after((mod_plane, mlp_line, gtok, out_rows))
    mod_line = travel(sum_plane(mod_plane, gx, "mod"), gy, ndev)
    grad_mlp = take(sum_line(mlp_line, [(0, mlp_line[0].shape[0])], "mlp")[0], mlp_len, device)
    out = out_tokens(shape, counts, out_rows)
    mod_line, out, grad_mlp = after((mod_line, out, grad_mlp))
    total_mod, total_small = sum_line(mod_line, [(0, mr), (mr, sr)], "mod")
    grad_mod = take(total_mod, mod_len, device)
    grad_small = take(total_small, small_len, device)
    return jnp.transpose(out, back), jnp.transpose(gtok, back), grad_mod, grad_mlp, grad_small


def solution(mesh):
    images = P(AXES, None, None, None)
    flat = P(AXES)
    return jax.shard_map(
        functools.partial(local, mesh.shape["gx"], mesh.shape["gy"]),
        mesh=mesh,
        in_specs=(images, flat, flat, flat, flat, flat, images),
        out_specs=(images, images, flat, flat, flat),
        check_vma=False,
    )
```

```python
import functools

import jax
import jax.numpy as jnp
import numpy as np
from jax import lax
from jax.experimental import pallas as pl
from jax.experimental.pallas import tpu as pltpu
from jax.sharding import PartitionSpec as P

C = 384
HID = 1536
GH = 14
GW = 20
HALF = 144
IMG = 2 * HALF
PAIR = 2 * IMG
C2 = 2 * C
NY = 17
NX = 23
NV = 12
NU = 8
Q = NU * NV
AR = 2 * (Q + 16)
BR = 2 * Q
SR = 4 * Q + 32
LEVELS = (3, 5, 7)
TAPS = 64
GATES = 128
MERGED = C2 + GATES
BROWS = 768
HCHUNK = 512
AXES = ("gx", "gy")
f32 = jnp.float32
bf16 = jnp.bfloat16
EPS = 1e-05
ROOT_HALF = 0.7071067811865476
INV_ROOT_2PI = 0.3989422804014327
LOG2_E = 1.4426950408889634


def _hi(a):
    return a.astype(bf16)


def _lo(a):
    return (a - a.astype(bf16).astype(np.float64)).astype(bf16)


def three(a):
    return np.concatenate([_hi(a), _lo(a), _hi(a)], 1)


@functools.lru_cache(maxsize=None)
def constants():
    row = np.arange(HALF)
    real = (row < 7 * GW).astype(np.float64)
    yy = np.minimum(row // GW, 6) - (GH - 1) / 2
    xx = row % GW - (GW - 1) / 2
    uv = [(u, v) for u in range(1, NU + 1) for v in range(NV)]
    u0 = [(0, v) for v in range(NV)]
    wu = 2 * np.pi / NY
    wv = 2 * np.pi / NX

    def trig(pairs, pad):
        u = np.array([p[0] for p in pairs] + [0] * pad, np.float64)[:, None]
        v = np.array([p[1] for p in pairs] + [0] * pad, np.float64)[:, None]
        use = np.array([1.0] * len(pairs) + [0.0] * pad)[:, None] * real[None]
        cy, sy = np.cos(wu * u * yy) * use, np.sin(wu * u * yy) * use
        cx, sx = np.cos(wv * v * xx), np.sin(wv * v * xx)
        weight = np.where(u > 0, 2.0, 1.0) * np.where(v > 0, 2.0, 1.0) / (NY * NX)
        return cy * cx, -cy * sx, sy * cx, -sy * sx, weight

    e_re, e_im, o_re, o_im, w1 = trig(uv, 0)
    z_re, z_im, _, _, w0 = trig(u0, 16 - NV)
    fe = np.concatenate([e_re, z_re, e_im, z_im], 0)
    fo = np.concatenate([o_re, o_im], 0)
    half = np.concatenate([0.5 * w1, w0, 0.5 * w1, w0], 0)
    ge = (fe * half).T
    go = (fo * np.concatenate([0.5 * w1, 0.5 * w1], 0)).T

    u = np.array([p[0] for p in uv], np.float64)[:, None]
    v = np.array([p[1] for p in uv], np.float64)[:, None]
    v0 = np.array(list(range(NV)) + [0] * (16 - NV), np.float64)[:, None]
    use0 = np.array([1.0] * NV + [0.0] * (16 - NV))[:, None]
    wp = np.where(v > 0, 2.0, 1.0) / (NY * NX)
    wz = np.where(v0 > 0, 2.0, 1.0) * use0 / (NY * NX)
    weights = np.concatenate([wp, -wp, wp, -wp, wz, -wz], 0)
    es = []
    for k in LEVELS:
        h = k // 2
        ty, tx = np.meshgrid(np.arange(k) - h, np.arange(k) - h, indexing="ij")
        for bucket in (0, 1):
            sy, sx = (ty, tx) if bucket == 0 else (tx, ty)
            py = sy.reshape(1, -1) * wu
            px = sx.reshape(1, -1) * wv
            plus = u * py + v * px
            minus = -u * py + v * px
            zero = v0 * px
            e = [np.cos(plus), np.sin(plus), np.cos(minus), np.sin(minus), np.cos(zero) * use0, np.sin(zero) * use0]
            whole_e = np.zeros((SR, TAPS))
            whole_e[:, : k * k] = np.concatenate(e, 0)
            es.append(np.concatenate([_hi(whole_e), _lo(whole_e)], 1))
    return dict(
        fe=three(fe),
        fo=three(fo),
        ge=three(ge * ROOT_HALF),
        go=three(go * ROOT_HALF),
        fe_back=_hi(fe * ROOT_HALF),
        fo_back=_hi(fo * ROOT_HALF),
        ge_back=_hi(ge),
        go_back=_hi(go),
        es=np.stack(es),
        est=np.stack([np.ascontiguousarray(e.T) for e in es]),
        weights=np.broadcast_to(weights, (SR, 128)).astype(np.float32),
    )


def dot(a, b):
    return jnp.dot(a, b, preferred_element_type=f32)


def dot_nt(a, b):
    return lax.dot_general(a, b, (((1,), (1,)), ((), ())), preferred_element_type=f32)


def dot_tn(a, b):
    return lax.dot_general(a, b, (((0,), (0,)), ((), ())), preferred_element_type=f32)


def gelu_pair(x):
    cdf = 0.5 * lax.erf(x * ROOT_HALF) + 0.5
    return x * cdf, cdf + x * (jnp.exp2(x * x * (-0.5 * LOG2_E)) * INV_ROOT_2PI)


def gelu_scaled(u):
    w = lax.erf(u) * ROOT_HALF + ROOT_HALF
    return u * w, w + u * (jnp.exp2(u * u * -LOG2_E) * (2 * INV_ROOT_2PI))


def split(x):
    hi = x.astype(bf16)
    return hi, (x - hi.astype(f32)).astype(bf16)


def at(base, i, n=16):
    return slice(base + i * n, base + i * n + n)


def weave(products, vector):
    n, m = len(products), len(vector)
    done = 0
    for k, step in enumerate(products):
        step()
        upto = (k + 1) * m // n
        for other in vector[done:upto]:
            other()
        done = upto


def norm_stats(x):
    mean = jnp.mean(x, axis=-1, keepdims=True)
    centred = x - mean
    var = jnp.mean(centred * centred, axis=-1, keepdims=True)
    r = lax.rsqrt(var + EPS)
    return centred * r, r


def sum8(x):
    total = x[0:8]
    for k in range(1, x.shape[0] // 8):
        total = total + x[8 * k : 8 * k + 8]
    return total


def grid_rows(im, y):
    return im * IMG + (y * GW if y < 7 else HALF + (GH - 1 - y) * GW)


def lanes(im):
    return slice(im * C, im * C + C)


(V_G1, V_B1, V_BQ, V_BC, V_HB, V_PB, V_S1, V_G2, V_B2, V_BM2, V_S2, V_BG) = range(12)
VROWS = 16
(S_HB, S_PB, S_S1, S_G2, S_B2, S_BM2, S_S2, S_BQ) = range(8)


def from_native(src, field):
    slots = src.shape[2]
    for lt in range(C // 128):
        for im in range(slots):
            for h in (GH // 2 * GW, HALF + GH // 2 * GW):
                field[lt, im * PITCH_IMAGE + h : im * PITCH_IMAGE + h + 4, :] = jnp.zeros((4, 128), f32)
        for y in range(GH):
            for x in range(GW):
                v = src[y, x, :, 128 * lt : 128 * lt + 128].astype(f32)
                field[lt, pl.ds(grid_rows(0, y) + x, slots, stride=PITCH_IMAGE), :] = v


def field_rows(field, first, n):
    s = pl.ds(pl.multiple_of(first, 8), n)
    return jnp.concatenate([field[lt, s, :] for lt in range(C // 128)], axis=1)


def kernel_prep(x_ref, xrow_o, nb_o, stat_o, field):
    step = pl.program_id(0)

    @pl.when(step == 0)
    def _():
        from_native(x_ref, field)

    lane = lax.broadcasted_iota(jnp.int32, (32, 128), 1)
    for k in range(PAIR // 32):
        s = at(0, k, 32)
        x = field_rows(field, (step * 2 + k // (IMG // 32)) * PITCH_IMAGE + 32 * (k % (IMG // 32)), 32)
        xrow_o[s, :] = x.astype(bf16)
        mean = jnp.mean(x, axis=-1, keepdims=True)
        centred = x - mean
        r = lax.rsqrt(jnp.mean(centred * centred, axis=-1, keepdims=True) + EPS)
        nb_o[s, :] = (centred * r).astype(bf16)
        stat_o[s, :] = jnp.where(lane == 0, mean, r)


def kernel_upstream(counts, cot_ref, up_o, field):
    step = pl.program_id(0)

    @pl.when(step == 0)
    def _():
        from_native(cot_ref, field)

    for im in range(2):
        live = (step * 2 + im < counts[0]).astype(f32)
        for i in range(IMG // 32):
            v = field_rows(field, (step * 2 + im) * PITCH_IMAGE + 32 * i, 32)
            up_o[at(im * IMG, i, 32), :] = (v * live).astype(bf16)


CHAINS = 3
CHAIN = C2 // CHAINS


def staggered(phases):
    lists = [phases(t) for t in range(CHAINS)]
    for turn in range(len(lists[0]) + CHAINS - 1):
        for t in range(CHAINS):
            if 0 <= turn - t < len(lists[t]):
                lists[t][turn - t]()


def sub_tiles(t):
    for k in range(t * CHAIN // 128, (t + 1) * CHAIN // 128):
        lt = k % (C // 128)
        yield k // (C // 128), slice(128 * k, 128 * k + 128), slice(128 * lt, 128 * lt + 128)


def spread_gates(gates, wide):
    for k in range(4):
        for i in range(PAIR // 32):
            s = at(0, i, 32)
            wide[k, s, :] = jnp.broadcast_to(gates[s, k : k + 1], (32, 128))


def kernel_forward(
    gx, gy, mod_len, small_len, bucket, pos, x_ref, stat, own, oth, es, fe, fo, ge, go,
    q_o, gates_o, mixed_o, z_o, g_o, spec_o, mean_o, wf, wh, wp, vec, bm1, kcat,
    h_o, normed, ctx, ecat, ocat, s_a, s_b, s_e, s_o, yca, ycb, mix, wide, flat, small, moved, spread, turned,
):
    step = pl.program_id(0)

    @pl.when(step == 0)
    def _():
        unpack_mod(gx, gy, mod_len, small_len, pos, own, oth, wf, wh, wp, vec, bm1, kcat, flat, small, moved, spread, turned)
        for lb in range(6):
            h_o[lb] = dot(es[lb], kcat[lb // 2])

    g1, b1 = vec[V_G1 : V_G1 + 1, :], vec[V_B1 : V_B1 + 1, :]
    for i in range(PAIR // 32):
        s = at(0, i, 32)
        n = (x_ref[s, :].astype(f32) - stat[s, 0:1]) * stat[s, 1:2]
        normed[s, :] = (n * g1 + b1).astype(bf16)
    right = dot(normed[...], wf[:, C + 128 :])
    left = dot(normed[...], wf[:, : C + 128])
    ctx[:, :128] = left[:, C:] + vec[V_BC : V_BC + 1, :128]
    ctx[:, 128:] = right[:, : C - 128] + vec[V_BC : V_BC + 1, 128:]
    gates_o[...] = right[:, C - 128 :] + vec[V_BG : V_BG + 1, :GATES]
    q_o[...] = left[:, :C] + vec[V_BQ : V_BQ + 1, :]
    spread_gates(gates_o, wide)
    lbs = [[level * 2 + bucket[step * 2 + im] for im in range(2)] for level in range(3)]

    def put(dst, off, width, ls, i, val, level):
        if level == 2:
            dst[at(off, i), ls] = val.astype(bf16)
            return
        hi, lo = split(val)
        dst[at(off, i), ls] = hi
        dst[at(off + width, i), ls] = lo

    def put_pair(ls, i, top, bot, level):
        put(ecat, 0, HALF, ls, i, top + bot, level)
        put(ocat, 0, HALF, ls, i, top - bot, level)

    def first(t):
        for im, ls, hs in sub_tiles(t):
            for i in range(HALF // 16):
                put_pair(ls, i, ctx[at(im * IMG, i), hs], ctx[at(im * IMG + HALF, i), hs], 0)

    def product(mat, ref, width, ts, level):
        hi = ref[:width, ts]
        if level == 2:
            return dot(mat[:, :width], hi)
        return dot(mat[...], jnp.concatenate([hi, hi, ref[width:, ts]], axis=0))

    def transform(t, level):
        ts = slice(t * CHAIN, (t + 1) * CHAIN)
        s_a[:, ts] = product(fe, ecat, HALF, ts, level)
        s_b[:, ts] = product(fo, ocat, HALF, ts, level)

    def back(t, level):
        ts = slice(t * CHAIN, (t + 1) * CHAIN)
        s_e[:, ts] = product(ge, yca, AR, ts, level)
        s_o[:, ts] = product(go, ycb, BR, ts, level)

    def filt(t, level):
        base = level * SR
        for im, ls, hs in sub_tiles(t):
            lb = lbs[level][im]
            for i in range(Q // 16):
                a_re, a_im = s_a[at(0, i), ls], s_a[at(Q + 16, i), ls]
                b_re, b_im = s_b[at(0, i), ls], s_b[at(Q, i), ls]
                xp_re, xp_im = a_re + b_im, a_im - b_re
                xm_re, xm_im = a_re - b_im, a_im + b_re
                spec_o[at(base, i), ls] = xp_re.astype(bf16)
                spec_o[at(base + Q, i), ls] = xp_im.astype(bf16)
                spec_o[at(base + 2 * Q, i), ls] = xm_re.astype(bf16)
                spec_o[at(base + 3 * Q, i), ls] = xm_im.astype(bf16)
                p_re, p_im = h_o[lb, at(0, i), hs], h_o[lb, at(Q, i), hs]
                q_re, q_im = h_o[lb, at(2 * Q, i), hs], h_o[lb, at(3 * Q, i), hs]
                yp_re, yp_im = p_re * xp_re - p_im * xp_im, p_re * xp_im + p_im * xp_re
                ym_re, ym_im = q_re * xm_re - q_im * xm_im, q_re * xm_im + q_im * xm_re
                for dst, off, width, val in (
                    (yca, 0, AR, yp_re + ym_re),
                    (yca, Q + 16, AR, yp_im + ym_im),
                    (ycb, 0, BR, ym_im - yp_im),
                    (ycb, Q, BR, yp_re - ym_re),
                ):
                    put(dst, off, width, ls, i, val, level)
            x_re, x_im = s_a[Q : Q + 16, ls], s_a[2 * Q + 16 : 2 * Q + 32, ls]
            spec_o[base + 4 * Q : base + 4 * Q + 16, ls] = x_re.astype(bf16)
            spec_o[base + 4 * Q + 16 : base + 4 * Q + 32, ls] = x_im.astype(bf16)
            p_re, p_im = h_o[lb, 4 * Q : 4 * Q + 16, hs], h_o[lb, 4 * Q + 16 : 4 * Q + 32, hs]
            for off, val in ((Q, p_re * x_re - p_im * x_im), (2 * Q + 16, p_re * x_im + p_im * x_re)):
                put(yca, off, AR, ls, 0, val, level)

    def act(t, level):
        for im, ls, hs in sub_tiles(t):
            total = jnp.zeros((8, 128), f32)
            for i in range(HALF // 16):
                even, odd = s_e[at(0, i), ls], s_o[at(0, i), ls]
                both = []
                for h, a in ((0, even + odd), (HALF, even - odd)):
                    z, g = gelu_scaled(a)
                    z_o[at(level * IMG + h, i), ls] = z.astype(bf16)
                    g_o[at(level * IMG + h, i), ls] = g.astype(bf16)
                    s = at(im * IMG + h, i)
                    part = z * wide[level, s, :]
                    mix[s, hs] = part if level == 0 else mix[s, hs] + part
                    both.append(z)
                if level < 2:
                    put_pair(ls, i, both[0], both[1], level + 1)
                else:
                    total = total + sum8(both[0]) + sum8(both[1])
            if level == 2:
                mean = jnp.sum(total, axis=0, keepdims=True) * (1.0 / (GH * GW))
                mean_o[:, ls] = jnp.broadcast_to(mean, (8, 128))
                glob, _ = gelu_pair(mean)
                for i in range(IMG // 16):
                    s = at(im * IMG, i)
                    mixed_o[s, hs] = (mix[s, hs] + wide[3, s, :] * glob).astype(bf16)

    def phases(t):
        steps = [lambda: first(t)]
        for level in range(3):
            steps += [
                lambda level=level: transform(t, level),
                lambda level=level: filt(t, level),
                lambda level=level: back(t, level),
                lambda level=level: act(t, level),
            ]
        return steps

    staggered(phases)


def kernel_middle(
    gx, gy, mlp_len, pos, x_ref, up, mixed, q_ref, wh, wp, vec, bm1, *refs,
):
    blocks = refs[: gy // 2]
    (
        dmid_o, out_o, dq_o, dmix_o, own, oth, gwh_o, gwp_o, sums, bsum,
        mod, modulated, branch, mid, second, dshr, shr, dsec, act, dexp, hid, dact, dbr, dm2, dmod, vacc, bacc, gw1, gw2, flat,
        w1, w2, gwh, gwp,
    ) = refs[gy // 2 :]
    step = pl.program_id(0)
    start = step == 0

    @pl.when(start)
    def _():
        for ref in (gwh, gwp, vacc, bacc):
            ref[...] = jnp.zeros_like(ref)
        unpack_mlp(gx, gy, mlp_len, pos, blocks, w1, w2, flat)

    def add_to(ref, rows_at, cols, v):
        ref[rows_at, cols] = jnp.where(start, 0.0, ref[rows_at, cols]) + v

    g2, b2 = vec[V_G2 : V_G2 + 1, :], vec[V_B2 : V_B2 + 1, :]
    s1, s2 = vec[V_S1 : V_S1 + 1, :], vec[V_S2 : V_S2 + 1, :]
    bm2 = vec[V_BM2 : V_BM2 + 1, :]

    mod[...] = dot(mixed[...], wh[...]) + vec[V_HB : V_HB + 1, :]
    for i in range(BROWS // 32):
        s = at(0, i, 32)
        modulated[s, :] = (q_ref[s, :] * mod[s, :]).astype(bf16)
        dshr[s, :] = (up[s, :].astype(f32) * s2).astype(bf16)
    branch[...] = dot(modulated[...], wp[...]) + vec[V_PB : V_PB + 1, :]
    for i in range(BROWS // 32):
        s = at(0, i, 32)
        middle = x_ref[s, :].astype(f32) + s1 * branch[s, :]
        mid[s, :] = middle
        n, _ = norm_stats(middle)
        second[s, :] = (n * g2 + b2).astype(bf16)

    chunks = [slice(h * HCHUNK, (h + 1) * HCHUNK) for h in range(HID // HCHUNK)]

    def enter(h):
        def into(t, k):
            ls = slice(h * HCHUNK + 256 * t, h * HCHUNK + 256 * t + 256)
            if k == 0:
                hid[h % 2, :, 256 * t : 256 * t + 256] = dot(second[...], w1[:, ls]) + bm1[0:1, ls]
            else:
                dact[h % 2, :, 256 * t : 256 * t + 256] = dot_nt(dshr[...], w2[ls, :])

        return [functools.partial(into, t, k) for t in range(HCHUNK // 256) for k in range(2)]

    def gelu(h):
        totals = []

        def rows_of(i):
            s = at(0, i)
            z, g = gelu_pair(hid[h % 2, s, :])
            act[s, chunks[h]] = z.astype(bf16)
            d = dact[h % 2, s, :] * g
            dexp[s, chunks[h]] = d.astype(bf16)
            totals.append(sum8(d) if not totals else totals.pop() + sum8(d))

        def close():
            bacc[:, chunks[h]] += totals[0]

        return [functools.partial(rows_of, i) for i in range(BROWS // 16)] + [close]

    def weight_grads(h):
        def one(t):
            ls = slice(h * HCHUNK + 256 * t, h * HCHUNK + 256 * t + 256)
            add_to(gw1, slice(None), ls, dot_tn(second[...], dexp[:, ls]))

        def two():
            add_to(gw2, chunks[h], slice(None), dot_tn(act[:, chunks[h]], dshr[...]))

        return [functools.partial(one, t) for t in range(HCHUNK // 256)] + [two]

    for step_of in enter(0):
        step_of()
    weave(enter(1), gelu(0))
    weave(enter(2) + weight_grads(0), gelu(1))
    weave(weight_grads(1), gelu(2))
    shr[...] = dot(act[...], w2[...])
    dsec[...] = dot_nt(dexp[...], w1[...])

    tally = {}

    def count(key, v):
        tally[key] = tally[key] + sum8(v) if key in tally else sum8(v)

    def finish(i):
        s = at(0, i, 32)
        middle = mid[s, :]
        u = up[s, :].astype(f32)
        shrunk = shr[s, :] + bm2
        out_o[s, :] = (middle + s2 * shrunk).astype(bf16)
        n, r = norm_stats(middle)
        d = dsec[s, :]
        e = d * g2
        dn = d * n
        dv = r * (e - jnp.mean(e, axis=-1, keepdims=True) - n * jnp.mean(e * n, axis=-1, keepdims=True))
        dm = u + dv
        dmid_o[s, :] = dm
        db = s1 * dm
        dbr[s, :] = db.astype(bf16)
        count(S_S1, dm * branch[s, :])
        count(S_G2, dn)
        count(S_B2, d)
        count(S_BM2, dshr[s, :].astype(f32))
        count(S_S2, u * shrunk)
        count(S_PB, db)

    weave(weight_grads(2), [functools.partial(finish, i) for i in range(BROWS // 32)])
    dmod[...] = dot_nt(dbr[...], wp[...])

    def demod(i):
        s = at(0, i, 32)
        dm = dmod[s, :]
        dq = dm * mod[s, :]
        dd = dm * q_ref[s, :]
        dq_o[s, :] = dq.astype(bf16)
        dm2[s, :] = dd.astype(bf16)
        count(S_BQ, dq)
        count(S_HB, dd)

    def grad_wp():
        gwp[...] += dot_tn(modulated[...], dbr[...])

    weave([grad_wp], [functools.partial(demod, i) for i in range(BROWS // 32)])
    dmix_o[...] = dot_nt(dm2[...], wh[...])
    gwh[...] += dot_tn(mixed[...], dm2[...])

    for key, v in tally.items():
        vacc[key] += v

    @pl.when(step == pl.num_programs(0) - 1)
    def _():
        for k in range(8):
            sums[k : k + 1, :] = jnp.sum(vacc[k], axis=0, keepdims=True)
        bsum[...] = jnp.broadcast_to(jnp.sum(bacc[...], axis=0, keepdims=True), bsum.shape)
        gwh_o[...] = gwh[...].astype(bf16)
        gwp_o[...] = gwp[...].astype(bf16)
        pack_mlp(gx, gy, mlp_len, pos, gw1, gw2, own, oth, flat)


def kernel_backward(
    gx, gy, mod_len, small_len,
    bucket, pos, nb_ref, dq_ref, dmix, gates, z_ref, g_ref, spec, mean_ref, kcat, vec, sums, bsum, es, weights,
    fe, fo, ge, go, wf_far, gwh_far, gwp_far, est_far,
    dmer, own, oth,
    gwf, fsum, gb, dk, h_ref, ecat, ocat, s_a, s_b, s_e, s_o, yca, ycb, acc, facc, wide, flat, small, moved, spread,
    wf, gwh, gwp, est, sems,
):
    step = pl.program_id(0)
    last = pl.num_programs(0) - 1
    late = [
        pltpu.make_async_copy(src, dst, sems.at[k])
        for k, (src, dst) in enumerate(((wf_far, wf), (gwh_far, gwh), (gwp_far, gwp), (est_far, est)))
    ]

    @pl.when(step == 0)
    def _():
        for copy in late:
            copy.start()
        for ref in (gwf, facc, acc):
            ref[...] = jnp.zeros_like(ref)
        for lb in range(6):
            h_ref[lb] = dot(es[lb], kcat[lb // 2])

    spread_gates(gates, wide)
    lbs = [[level * 2 + bucket[step * 2 + im] for im in range(2)] for level in range(3)]
    globs = [gelu_pair(mean_ref[0:1, lanes(im)]) for im in range(2)]
    lane = lax.broadcasted_iota(jnp.int32, (16, GATES), 1)
    dmeans = {}

    def mean_grad(t):
        for im, ls, hs in sub_tiles(t):
            total = jnp.zeros((8, 128), f32)
            for i in range(IMG // 16):
                s = at(im * IMG, i)
                total = total + sum8(dmix[s, hs] * wide[3, s, :])
            dmeans[ls.start] = jnp.sum(total, axis=0, keepdims=True) * globs[im][1][:, hs] * (1.0 / (GH * GW))

    def gate_grad(part):
        t_g = jnp.zeros((8, GATES), f32)
        n = 2 * (HALF // 16) // CHAINS
        for im, i in [(im, i) for im in range(2) for i in range(HALF // 16)][part * n : part * n + n]:
            for h in (0, HALF):
                s = at(im * IMG + h, i)
                dm = dmix[s, :]
                dg = jnp.zeros((16, GATES), f32)
                for k in range(4):
                    other = z_ref[at(k * IMG + h, i), lanes(im)].astype(f32) if k < 3 else globs[im][0]
                    col = jnp.sum(dm * other, axis=-1, keepdims=True)
                    dg = jnp.where(lane == k, col, dg)
                dmer[s, :C] = dq_ref[s, :]
                dmer[s, C2:] = dg.astype(bf16)
                t_g = t_g + sum8(dg)
        facc[:, C2:] += t_g

    def before(t, level):
        for im, ls, hs in sub_tiles(t):
            for i in range(HALF // 16):
                if level < 2:
                    even, odd = s_e[at(0, i), ls], s_o[at(0, i), ls]
                    through = (even + odd, even - odd)
                else:
                    through = (dmeans[ls.start], dmeans[ls.start])
                parts = []
                for k, h in enumerate((0, HALF)):
                    s = at(im * IMG + h, i)
                    dz = wide[level, s, :] * dmix[s, hs] + through[k]
                    parts.append(dz * g_ref[at(level * IMG + h, i), ls].astype(f32))
                ecat[at(0, i), ls] = (parts[0] + parts[1]).astype(bf16)
                ocat[at(0, i), ls] = (parts[0] - parts[1]).astype(bf16)

    def transform(t):
        ts = slice(t * CHAIN, (t + 1) * CHAIN)
        s_a[:, ts] = dot(fe[...], ecat[:, ts])
        s_b[:, ts] = dot(fo[...], ocat[:, ts])

    def back(t):
        ts = slice(t * CHAIN, (t + 1) * CHAIN)
        s_e[:, ts] = dot(ge[...], yca[:, ts])
        s_o[:, ts] = dot(go[...], ycb[:, ts])

    def filt(t, level):
        base = level * SR
        for im, ls, hs in sub_tiles(t):
            lb = lbs[level][im]
            for i in range(Q // 16):
                a_re, a_im = s_a[at(0, i), ls], s_a[at(Q + 16, i), ls]
                b_re, b_im = s_b[at(0, i), ls], s_b[at(Q, i), ls]
                dp_re, dp_im = a_re + b_im, a_im - b_re
                dm_re, dm_im = a_re - b_im, a_im + b_re
                xp_re, xp_im = spec[at(base, i), ls].astype(f32), spec[at(base + Q, i), ls].astype(f32)
                xm_re, xm_im = spec[at(base + 2 * Q, i), ls].astype(f32), spec[at(base + 3 * Q, i), ls].astype(f32)
                acc[lb, at(0, i), hs] += xp_re * dp_re + xp_im * dp_im
                acc[lb, at(Q, i), hs] += xp_im * dp_re - xp_re * dp_im
                acc[lb, at(2 * Q, i), hs] += xm_re * dm_re + xm_im * dm_im
                acc[lb, at(3 * Q, i), hs] += xm_im * dm_re - xm_re * dm_im
                p_re, p_im = h_ref[lb, at(0, i), hs], h_ref[lb, at(Q, i), hs]
                q_re, q_im = h_ref[lb, at(2 * Q, i), hs], h_ref[lb, at(3 * Q, i), hs]
                yp_re, yp_im = p_re * dp_re + p_im * dp_im, p_re * dp_im - p_im * dp_re
                ym_re, ym_im = q_re * dm_re + q_im * dm_im, q_re * dm_im - q_im * dm_re
                yca[at(0, i), ls] = (yp_re + ym_re).astype(bf16)
                yca[at(Q + 16, i), ls] = (yp_im + ym_im).astype(bf16)
                ycb[at(0, i), ls] = (ym_im - yp_im).astype(bf16)
                ycb[at(Q, i), ls] = (yp_re - ym_re).astype(bf16)
            d_re, d_im = s_a[Q : Q + 16, ls], s_a[2 * Q + 16 : 2 * Q + 32, ls]
            x_re = spec[base + 4 * Q : base + 4 * Q + 16, ls].astype(f32)
            x_im = spec[base + 4 * Q + 16 : base + 4 * Q + 32, ls].astype(f32)
            acc[lb, 4 * Q : 4 * Q + 16, hs] += x_re * d_re + x_im * d_im
            acc[lb, 4 * Q + 16 : 4 * Q + 32, hs] += x_im * d_re - x_re * d_im
            p_re, p_im = h_ref[lb, 4 * Q : 4 * Q + 16, hs], h_ref[lb, 4 * Q + 16 : 4 * Q + 32, hs]
            yca[Q : Q + 16, ls] = (p_re * d_re + p_im * d_im).astype(bf16)
            yca[2 * Q + 16 : 2 * Q + 32, ls] = (p_re * d_im - p_im * d_re).astype(bf16)

    def context(t):
        for im, ls, hs in sub_tiles(t):
            ds = slice(C + hs.start, C + hs.stop)
            total = jnp.zeros((8, 128), f32)
            for i in range(HALF // 16):
                even, odd = s_e[at(0, i), ls], s_o[at(0, i), ls]
                top, bot = even + odd, even - odd
                dmer[at(im * IMG, i), ds] = top.astype(bf16)
                dmer[at(im * IMG + HALF, i), ds] = bot.astype(bf16)
                total = total + sum8(top) + sum8(bot)
            facc[:, ds] += total

    def phases(t):
        steps = [lambda: mean_grad(t)]
        for level in (2, 1, 0):
            steps += [
                lambda level=level: before(t, level),
                lambda: transform(t),
                lambda level=level: filt(t, level),
                lambda: back(t),
            ]
            if level == 2:
                steps.append(lambda: gate_grad(t))
        return steps + [lambda: context(t)]

    staggered(phases)
    gwf[...] += dot_tn(nb_ref[...], dmer[...])

    @pl.when(step == last)
    def _():
        for copy in late:
            copy.wait()
        facc[:, :C] = jnp.broadcast_to(sums[S_BQ : S_BQ + 1, :] * 0.125, (8, C))
        colsum = jnp.sum(facc[...], axis=0, keepdims=True)
        fsum[...] = jnp.broadcast_to(colsum, fsum.shape)
        col = jnp.sum(wf[...].astype(f32) * gwf[...], axis=-1, keepdims=True)
        gb[0:8, :] = jnp.transpose(jnp.broadcast_to(col, (C, 128)))[0:8, :]
        c_hi, c_lo = split(fsum[...])
        both = dot_nt(jnp.concatenate([c_hi, c_lo], axis=0), wf[...])
        gb[8:16, :] = both[0:8, :] + both[8:16, :]
        g1 = jnp.transpose(jnp.broadcast_to(vec[V_G1 : V_G1 + 1, :], (128, C)))
        b1 = jnp.transpose(jnp.broadcast_to(vec[V_B1 : V_B1 + 1, :], (128, C)))
        for t in range(MERGED // 128):
            ls = slice(128 * t, 128 * t + 128)
            gwf[:, ls] = gwf[:, ls] * g1 + b1 * fsum[0:1, ls]
        for level in range(3):
            total = None
            for lb in (level * 2, level * 2 + 1):
                hi, lo = split(acc[lb] * jnp.concatenate([weights[...]] * (C // 128), 1))
                first = dot(est[lb], hi)
                term = first[:TAPS] + first[TAPS:] + dot(est[lb, :TAPS, :], lo)
                total = term if total is None else total + term
            dk[level] = total
        pack_mod(gx, gy, mod_len, small_len, pos, gwf, gwh, gwp, sums, bsum, fsum, gb, dk, own, oth, flat, small, moved, spread)


def to_native(rows_ref, first, native, slot, slots, gain):
    line = GW * slots
    for y in range(GH):
        a = first + grid_rows(0, y)
        for lt in range(C // 128):
            v = rows_ref[a : a + GW, 128 * lt : 128 * lt + 128]
            native[lt, pl.ds(line * y + slot, GW, stride=slots), :] = v if gain is None else v * gain


def write_native(native, out, slots):
    line = GW * slots
    for y in range(GH):
        for lt in range(C // 128):
            v = native[lt, line * y : line * (y + 1), :].reshape(GW, slots, 128)
            out[y, :, :, 128 * lt : 128 * lt + 128] = v.astype(out.dtype)


def kernel_tail(dmer, wf, x_ref, stat, dmid, vec, gtok_o, stage, native):
    step = pl.program_id(0)
    slots = gtok_o.shape[2]
    g1 = vec[V_G1 : V_G1 + 1, :]
    d_normed = dot_nt(dmer[...], wf[...])
    for i in range(PAIR // 32):
        s = at(0, i, 32)
        r = stat[s, 1:2]
        n = (x_ref[s, :].astype(f32) - stat[s, 0:1]) * r
        e = d_normed[s, :] * g1
        dv = e - jnp.mean(e, axis=-1, keepdims=True) - n * jnp.mean(e * n, axis=-1, keepdims=True)
        stage[s, :] = dmid[s, :] + r * dv
    for im in range(2):
        to_native(stage, im * IMG, native, step * 2 + im, slots, None)

    @pl.when(step == pl.num_programs(0) - 1)
    def _():
        write_native(native, gtok_o, slots)


def kernel_out(counts, rows_ref, out_o, native, wide):
    slots = out_o.shape[2]
    wide[...] = rows_ref[...].astype(f32)
    for im in range(slots):
        to_native(wide, im * IMG, native, im, slots, (im < counts[0]).astype(f32))
    write_native(native, out_o, slots)


def block_rows(length):
    return 8 * (length // 1024 if length % 1024 == 0 else (length + 1022) // 1024 + 1)


def place(shard, device):
    length = shard.shape[0]
    n = block_rows(length) * 128
    if n == length:
        return shard.reshape(-1, 128)
    offset = lax.rem(device * length, 1024)
    return lax.dynamic_update_slice(jnp.zeros((n,), shard.dtype), shard, (offset,)).reshape(-1, 128)


def take(block, length, device):
    flat = block.reshape(-1)
    if flat.shape[0] == length:
        return flat
    return lax.dynamic_slice(flat, (lax.rem(device * length, 1024),), (length,))


def first_row(length, device):
    return pl.multiple_of((device * length) // 1024 * 8, 8)


def device_at(pos, gy, i, j, c):
    return (pos[0] ^ j) * gy + (pos[1] ^ (2 * i + c))


def join(first, second, sh):
    lane = lax.broadcasted_iota(jnp.int32, first.shape, 1)
    return jnp.where(lane < 128 - sh, first, second)


def turn(v, sh):
    return pltpu.roll(v, 128 - sh, 1) if sh else v


def shift_right(first, second, sh):
    lane = lax.broadcasted_iota(jnp.int32, first.shape, 1)
    return jnp.where(lane < sh, pltpu.roll(first, sh, 1), pltpu.roll(second, sh, 1))


WIDE = C2 + 4
WF_ROWS = C * WIDE // 128
W_ROWS = C * C // 128
PERIOD = 32
PITCH_IMAGE = IMG + 8
PITCH_Q = 24
PITCH_P = 40
STRIDE = PERIOD * WIDE // 128
K_ROW = 12
TAIL_ROW = K_ROW + 83 * C // 128
B_HB, B_PB, B_S1, B_G2, B_B2, B_BM1 = (TAIL_ROW + 3 * k for k in range(6))
B_BM2 = B_BM1 + HID // 128
B_S2 = B_BM2 + 3
END_ROW = B_S2 + 3


def by_threes(flat, base, n, temp, out):
    for g in range(n // 64):
        room = 192 * (g % 4)
        for k in range(8):
            for b in range(3):
                src = base + 192 * g + 24 * k + 8 * b
                temp[pl.ds(room + 64 * b + k, 8, stride=8), :] = flat[src : src + 8, :]
        for i in range(24):
            rows_at = 768 + 64 * ((g % 4) * 3 + i % 3) + i // 3
            temp[pl.ds(rows_at, 8, stride=8), :] = temp[room + 8 * i : room + 8 * i + 8, :]
        for t in range(3):
            first = 768 + 64 * ((g % 4) * 3 + t)
            out[64 * g : 64 * g + 64, 128 * t : 128 * t + 128] = temp[first : first + 64, :].astype(bf16)


def unpack_mod(gx, gy, mod_len, small_len, pos, own, oth, wf_o, wh_o, wp_o, vec_o, bm1_o, kcat_o, flat, small, moved, wide, turned):
    flat[...] = jnp.zeros_like(flat)
    small[...] = jnp.zeros_like(small)
    mr, sr = block_rows(mod_len), block_rows(small_len)
    for i in range(gy // 2):
        for j in range(gx):
            for c, src in enumerate((own, oth)):
                d = device_at(pos, gy, i, j, c)
                block = src[i, j].astype(f32)
                flat[pl.ds(first_row(mod_len, d), mr), :] += block[:mr]
                small[pl.ds(first_row(small_len, d), sr), :] += block[mr : mr + sr]
    lane = lax.broadcasted_iota(jnp.int32, (16, 128), 1)
    for q in range(C // PERIOD):
        for f in range(0, STRIDE + 7, 8):
            turned[pl.ds(PITCH_Q * f + q, 8, stride=PITCH_Q), :] = flat[STRIDE * q + f : STRIDE * q + f + 8, :]
    for p in range(PERIOD):
        row, sh = WIDE * p // 128, WIDE * p % 128
        first = [PITCH_Q * (row + j) for j in range(MERGED // 128 + (1 if sh else 0))]
        tiles = [turn(turned[k : k + 16, :], sh) for k in first]
        for j in range(MERGED // 128):
            v = join(tiles[j], tiles[j + 1], sh) if sh else tiles[j]
            if j == MERGED // 128 - 1:
                v = jnp.where(lane < 4, v, 0.0)
            wide[j, pl.ds(p, 16, stride=PITCH_P), :] = v
    for j in range(MERGED // 128):
        for q in range(C // PERIOD):
            v = wide[j, PITCH_P * q : PITCH_P * q + PERIOD, :]
            wf_o[PERIOD * q : PERIOD * q + PERIOD, 128 * j : 128 * j + 128] = v.astype(bf16)
    by_threes(flat, WF_ROWS, C, turned, wh_o)
    by_threes(flat, WF_ROWS + W_ROWS, C, turned, wp_o)
    n = moved.shape[0]
    moved[...] = join(turn(small[0:n, :], 4), turn(small[1 : n + 1, :], 4), 4)
    vec_o[...] = jnp.zeros_like(vec_o)
    for row, src, start in (
        (V_G1, small, 0), (V_B1, small, 3), (V_BQ, small, 6), (V_BC, small, 9),
        (V_HB, moved, B_HB), (V_PB, moved, B_PB), (V_S1, moved, B_S1), (V_G2, moved, B_G2), (V_B2, moved, B_B2),
        (V_BM2, moved, B_BM2), (V_S2, moved, B_S2),
    ):
        for j in range(3):
            vec_o[row : row + 1, 128 * j : 128 * j + 128] = src[start + j : start + j + 1, :]
    vec_o[V_BG : V_BG + 1, 0:128] = jnp.where(lane[0:1] < 4, small[K_ROW : K_ROW + 1, :], 0.0)
    for t in range(HID // 128):
        bm1_o[:, 128 * t : 128 * t + 128] = jnp.broadcast_to(moved[B_BM1 + t : B_BM1 + t + 1, :], (8, 128))
    start = 0
    for level, k in enumerate(LEVELS):
        for j in range(3):
            taps = moved[pl.ds(K_ROW + 3 * start + j, TAPS, stride=3), :].astype(bf16)
            kcat_o[level, 0:TAPS, 128 * j : 128 * j + 128] = taps
            kcat_o[level, TAPS:, 128 * j : 128 * j + 128] = taps
        start += k * k


def unpack_mlp(gx, gy, mlp_len, pos, blocks, w1_o, w2_o, flat):
    mr = block_rows(mlp_len)
    aligned = mr * 128 == mlp_len
    if not aligned:
        flat[...] = jnp.zeros_like(flat)
    for i, src in enumerate(blocks):
        for j in range(gx):
            for c in range(2):
                rows_at = pl.ds(first_row(mlp_len, device_at(pos, gy, i, j, c)), mr)
                if aligned:
                    flat[rows_at, :] = src[c, j].astype(f32)
                else:
                    flat[rows_at, :] += src[c, j].astype(f32)
    for t in range(HID // 128):
        w1_o[:, 128 * t : 128 * t + 128] = flat[pl.ds(t, C, stride=HID // 128), :].astype(bf16)
    for t in range(C // 128):
        w2_o[:, 128 * t : 128 * t + 128] = flat[pl.ds(C * HID // 128 + t, HID, stride=C // 128), :].astype(bf16)


def send_slots(gx, gy, pos, flat, length, base, own, oth):
    mr = block_rows(length)
    for i in range(gy // 2):
        for j in range(gx):
            for c, dst in enumerate((own, oth)):
                d = device_at(pos, gy, i, j, c)
                dst[i, j, base : base + mr, :] = flat[pl.ds(first_row(length, d), mr), :].astype(bf16)


def pack_mlp(gx, gy, mlp_len, pos, gw1, gw2, own, oth, flat):
    used = 2 * C * HID // 128
    if flat.shape[0] > used:
        flat[used:, :] = jnp.zeros_like(flat[used:, :])
    for t in range(HID // 128):
        flat[pl.ds(t, C, stride=HID // 128), :] = gw1[:, 128 * t : 128 * t + 128]
    for t in range(C // 128):
        flat[pl.ds(C * HID // 128 + t, HID, stride=C // 128), :] = gw2[:, 128 * t : 128 * t + 128]
    send_slots(gx, gy, pos, flat, mlp_len, 0, own, oth)


def pack_mod(gx, gy, mod_len, small_len, pos, gwf, gwh, gwp, sums, bsum, fsum, gb, dk, own, oth, flat, small, moved, wide):
    lane = lax.broadcasted_iota(jnp.int32, (16, 128), 1)
    used = WF_ROWS + 2 * W_ROWS
    if flat.shape[0] > used:
        flat[used:, :] = jnp.zeros_like(flat[used:, :])
    for j in range(MERGED // 128):
        for row in range(0, C, 8):
            dst = pl.ds(PITCH_Q * (row % PERIOD) + row // PERIOD, 8, stride=PITCH_Q)
            wide[j, dst, :] = gwf[row : row + 8, 128 * j : 128 * j + 128]
    turned = {}

    def piece(p, tile):
        tile = min(tile, MERGED // 128 - 1)
        if (p, tile) not in turned:
            turned[p, tile] = turn(wide[tile, PITCH_Q * p : PITCH_Q * p + 16, :], -WIDE * p % 128)
        return turned[p, tile]

    for f in range(STRIDE):
        p = 128 * f // WIDE
        col = 128 * f - WIDE * p
        t, sh = col // 128, col % 128
        v = join(piece(p, t), piece(p, t + 1), sh) if sh else piece(p, t)
        left = WIDE - col
        if left < 128:
            v = jnp.where(lane < left, v, piece(p + 1, 0))
        flat[pl.ds(f, 16, stride=STRIDE), :] = v
    for j in range(3):
        ls = slice(128 * j, 128 * j + 128)
        flat[pl.ds(WF_ROWS + j, C, stride=3), :] = gwh[:, ls].astype(f32)
        flat[pl.ds(WF_ROWS + W_ROWS + j, C, stride=3), :] = gwp[:, ls].astype(f32)
    moved[...] = jnp.zeros_like(moved)
    small[...] = jnp.zeros_like(small)
    start = 0
    for level, k in enumerate(LEVELS):
        for j in range(3):
            moved[pl.ds(K_ROW + 3 * start + j, k * k, stride=3), :] = dk[level, 0 : k * k, 128 * j : 128 * j + 128]
        start += k * k
    for start, row in (
        (B_HB, S_HB), (B_PB, S_PB), (B_S1, S_S1), (B_G2, S_G2), (B_B2, S_B2), (B_BM2, S_BM2), (B_S2, S_S2),
    ):
        for j in range(3):
            moved[start + j : start + j + 1, :] = sums[row : row + 1, 128 * j : 128 * j + 128]
    for t in range(HID // 128):
        moved[B_BM1 + t : B_BM1 + t + 1, :] = bsum[0:1, 128 * t : 128 * t + 128]
    n = moved.shape[0]
    small[8:n, :] = shift_right(moved[7 : n - 1, :], moved[8:n, :], 4)
    for j in range(3):
        ls = slice(128 * j, 128 * j + 128)
        small[j : j + 1, :] = gb[0:1, ls]
        small[3 + j : 4 + j, :] = gb[8:9, ls]
        small[6 + j : 7 + j, :] = fsum[0:1, ls]
        small[9 + j : 10 + j, :] = fsum[0:1, C + 128 * j : C + 128 * j + 128]
    gate_lane = lane[0:1] < 4
    small[K_ROW : K_ROW + 1, :] = jnp.where(gate_lane, fsum[0:1, C2:], small[K_ROW : K_ROW + 1, :])
    mr, sr = block_rows(mod_len), block_rows(small_len)
    send_slots(gx, gy, pos, flat, mod_len, 0, own, oth)
    for i in range(gy // 2):
        for j in range(gx):
            for c, dst in enumerate((own, oth)):
                block = small[pl.ds(first_row(small_len, device_at(pos, gy, i, j, c)), sr), :]
                pad = own.shape[2] - mr - sr
                if pad:
                    block = jnp.concatenate([block, jnp.zeros((pad, 128), f32)], 0)
                dst[i, j, mr:, :] = block.astype(bf16)


def kernel_add(n_in, *refs):
    for k, o in enumerate(refs[n_in:]):
        total = None
        for ref in refs[:n_in]:
            v = ref[k].astype(f32)
            total = v if total is None else total + v
        o[...] = total.astype(o.dtype)


def kernel_cut(cuts, *refs):
    outs = refs[-len(cuts) :]
    for o, (first, n) in zip(outs, cuts):
        total = None
        for ref in refs[: -len(cuts)]:
            v = ref[first : first + n, :].astype(f32)
            total = v if total is None else total + v
        o[...] = total


def full(shape):
    return pl.BlockSpec(shape, lambda *i, n=len(shape): (0,) * n)


def rows(n, width):
    return pl.BlockSpec((n, width), lambda i: (i, 0))


def smem():
    return pl.BlockSpec(memory_space=pltpu.SMEM)


def sds(shape, dtype):
    return jax.ShapeDtypeStruct(shape, dtype)


def call(kernel, name, grid, ins, outs, scratch, mib, micros):
    return pl.pallas_call(
        kernel,
        grid=grid,
        in_specs=[s for _, s in ins],
        out_shape=[o for o, _ in outs],
        out_specs=[s for _, s in outs],
        scratch_shapes=[pltpu.VMEM(*v) if isinstance(v, tuple) else v for v in scratch],
        compiler_params=pltpu.CompilerParams(vmem_limit_bytes=mib * 2**20),
        cost_estimate=pl.CostEstimate(flops=int(micros * 1e9), bytes_accessed=int(micros * 1e6), transcendentals=0),
        name=name,
    )(*[a for a, _ in ins])


def whole(*arrays):
    return [(a, full(a.shape)) for a in arrays]


def by_rows(n, *arrays):
    return [(a, rows(n, a.shape[1])) for a in arrays]


def native_rows(slots):
    return ((C // 128, GH * GW * slots, 128), f32)


def prep(tokens):
    slots = tokens.shape[2]
    n = slots * IMG
    outs = [(sds((n, w), t), rows(PAIR, w)) for w, t in ((C, bf16), (C, bf16), (128, f32))]
    return call(kernel_prep, "prep", (slots // 2,), whole(tokens), outs, [((C // 128, slots * PITCH_IMAGE, 128), f32)], 60, 4)


def upstream(counts, cotangent):
    slots = cotangent.shape[2]
    ins = [(counts, smem())] + whole(cotangent)
    outs = [(sds((slots * IMG, C), bf16), rows(PAIR, C))]
    return call(kernel_upstream, "upstream", (slots // 2,), ins, outs, [((C // 128, slots * PITCH_IMAGE, 128), f32)], 60, 3)[0]


def forward(gx, gy, pos, xrow, stat, bucket, own, oth, mod_len, small_len):
    con = constants()
    pairs = xrow.shape[0] // PAIR
    n = pairs * PAIR
    outs = [
        (sds((n, C), f32), rows(PAIR, C)),
        (sds((n, GATES), f32), rows(PAIR, GATES)),
        (sds((n, C), bf16), rows(PAIR, C)),
        (sds((pairs * 3 * IMG, C2), bf16), rows(3 * IMG, C2)),
        (sds((pairs * 3 * IMG, C2), bf16), rows(3 * IMG, C2)),
        (sds((pairs * 3 * SR, C2), bf16), rows(3 * SR, C2)),
        (sds((pairs * 8, C2), f32), rows(8, C2)),
    ]
    weights = [((C, MERGED), bf16), ((C, C), bf16), ((C, C), bf16), ((VROWS, C), f32), ((8, HID), f32), ((3, 2 * TAPS, C), bf16)]
    outs += [(sds(shape, dtype), full(shape)) for shape, dtype in weights]
    mats = [jnp.asarray(con[k]) for k in ("es", "fe", "fo", "ge", "go")]
    ins = [(bucket, smem()), (pos, smem())] + by_rows(PAIR, xrow, stat) + whole(own, oth, *mats)
    scratch = [
        ((6, SR, C), f32), ((PAIR, C), bf16), ((PAIR, C), f32), ((2 * HALF, C2), bf16), ((2 * HALF, C2), bf16), ((AR, C2), f32), ((BR, C2), f32),
        ((HALF, C2), f32), ((HALF, C2), f32), ((2 * AR, C2), bf16), ((2 * BR, C2), bf16), ((PAIR, C), f32),
        ((4, PAIR, 128), f32),
    ]
    ndev = gx * gy
    flat_rows = max(span(mod_len, ndev), STRIDE * 16 + 8)
    small_rows = max(span(small_len, ndev), END_ROW + 26)
    scratch += [((flat_rows, 128), f32), ((small_rows + 8, 128), f32), ((small_rows, 128), f32)]
    scratch += [((MERGED // 128, max(PITCH_Q * PERIOD, PITCH_P * 16), 128), f32), ((PITCH_Q * (STRIDE + 7), 128), f32)]
    kernel = functools.partial(kernel_forward, gx, gy, mod_len, small_len)
    return call(kernel, "focal_forward", (pairs,), ins, outs, scratch, 58, 28)


def middle(gx, gy, pos, xrow, up, mixed, q, wh, wp, vec, bm1, mlp_blocks, mlp_len):
    n = xrow.shape[0]
    outs = [
        (sds((n, C), f32), rows(BROWS, C)),
        (sds((n, C), bf16), rows(BROWS, C)),
        (sds((n, C), bf16), rows(BROWS, C)),
        (sds((n, C), f32), rows(BROWS, C)),
    ]
    slots = (gy // 2, gx, block_rows(mlp_len), 128)
    outs += [(sds(slots, bf16), full(slots))] * 2
    outs += [(sds(s, t), full(s)) for s, t in (((C, C), bf16), ((C, C), bf16), ((8, C), f32), ((8, HID), f32))]
    ins = [(pos, smem())] + by_rows(BROWS, xrow, up, mixed, q) + whole(wh, wp, vec, bm1, *mlp_blocks)
    blk = (BROWS, C)
    scratch = [
        (blk, f32), (blk, bf16), (blk, f32), (blk, f32), (blk, bf16), (blk, bf16), (blk, f32), (blk, f32),
        ((BROWS, HID), bf16), ((BROWS, HID), bf16), ((2, BROWS, HCHUNK), f32), ((2, BROWS, HCHUNK), f32), (blk, bf16), (blk, bf16), (blk, f32),
        ((8, 8, C), f32), ((8, HID), f32),
        ((C, HID), f32), ((HID, C), f32), ((span(mlp_len, gx * gy), 128), f32), ((C, HID), bf16), ((HID, C), bf16), ((C, C), f32), ((C, C), f32),
    ]
    kernel = functools.partial(kernel_middle, gx, gy, mlp_len)
    return call(kernel, "middle", (n // BROWS,), ins, outs, scratch, 60, 42)


def backward(gx, gy, pos, bucket, nb, dq, dmix, gates, z, g, spec, mean, kcat, wf, vec, sums, bsum, gwh, gwp, mod_len, small_len):
    con = constants()
    ndev = gx * gy
    pairs = nb.shape[0] // PAIR
    mats = [jnp.asarray(con[k]) for k in ("es", "weights", "fe_back", "fo_back", "ge_back", "go_back")]
    slots = (gy // 2, gx, -(-(block_rows(mod_len) + block_rows(small_len)) // 16) * 16, 128)
    outs = [(sds((nb.shape[0], MERGED), bf16), rows(PAIR, MERGED))] + [(sds(slots, bf16), full(slots))] * 2
    ins = [(bucket, smem()), (pos, smem())] + by_rows(PAIR, nb, dq, dmix, gates) + by_rows(3 * IMG, z, g) + by_rows(3 * SR, spec)
    ins += by_rows(8, mean) + whole(kcat, vec, sums, bsum, *mats)
    late = (wf, gwh, gwp, jnp.asarray(con["est"]))
    ins += [(v, pl.BlockSpec(memory_space=pl.ANY)) for v in late]
    small_rows = -(-max(span(small_len, ndev), END_ROW + 2) // 8) * 8
    scratch = [
        ((C, MERGED), f32), ((8, MERGED), f32), ((16, C), f32), ((3, TAPS, C), f32), ((6, SR, C), f32),
        ((HALF, C2), bf16), ((HALF, C2), bf16), ((AR, C2), f32), ((BR, C2), f32), ((HALF, C2), f32), ((HALF, C2), f32),
        ((AR, C2), bf16), ((BR, C2), bf16), ((6, SR, C), f32), ((8, MERGED), f32), ((4, PAIR, 128), f32),
        ((max(span(mod_len, ndev), STRIDE * 16 + 8), 128), f32), ((small_rows, 128), f32), ((small_rows, 128), f32),
        ((MERGED // 128, max(PITCH_Q * PERIOD, PITCH_P * 16), 128), f32),
    ]
    scratch += [(v.shape, v.dtype) for v in late] + [pltpu.SemaphoreType.DMA((len(late),))]
    kernel = functools.partial(kernel_backward, gx, gy, mod_len, small_len)
    return call(kernel, "focal_backward", (pairs,), ins, outs, scratch, 58, 28)


def tail(shape, dmer, wf, xrow, stat, dmid, vec):
    slots = shape[2]
    ins = by_rows(PAIR, dmer) + whole(wf) + by_rows(PAIR, xrow, stat, dmid) + whole(vec)
    return call(kernel_tail, "tail", (slots // 2,), ins, [(sds(shape, f32), full(shape))], [((PAIR, C), f32), native_rows(slots)], 24, 8)[0]


def out_tokens(shape, counts, out_rows):
    ins = [(counts, smem())] + whole(out_rows)
    return call(kernel_out, "out_tokens", (), ins, [(sds(shape, bf16), full(shape))], [native_rows(shape[2]), ((shape[2] * IMG, C), f32)], 24, 5)[0]


def span(length, ndev):
    return ((ndev - 1) * length) // 1024 * 8 + block_rows(length)


def add(arrays, outs, name):
    return call(functools.partial(kernel_add, len(arrays)), name, (), whole(*arrays), [(o, full(o.shape)) for o in outs], [], 24, 2)


def swap(x, mask, ndev):
    return lax.ppermute(x, AXES, [(k, k ^ mask) for k in range(ndev)])


def around(x, step, count, ndev):
    return [x] + [swap(x, step * k, ndev) for k in range(1, count)]


def after(values):
    return lax.optimization_barrier(values)


def travel(parts, step, ndev):
    return [parts[0]] + [swap(p, step * k, ndev) for k, p in enumerate(parts) if k]


def kernel_add_parts(n, *refs):
    for k, o in enumerate(refs[n + 1 :]):
        o[...] = (refs[k][...].astype(f32) + refs[n][k].astype(f32)).astype(o.dtype)


def sum_core_parts(own, oth, gx, gy, name):
    got = swap(oth, 1, gx * gy)
    n = gy // 2
    parts = add([own], [sds(own.shape[1:], bf16)] * n, name + "_own")
    outs = [sds(own.shape[1:], f32 if k == 0 else bf16) for k in range(n)]
    kernel = functools.partial(kernel_add_parts, n)
    return call(kernel, name + "_sum_core", (), whole(*parts, got), [(o, full(o.shape)) for o in outs], [], 24, 1)


def sum_core(own, oth, gx, gy, name):
    got = swap(oth, 1, gx * gy)
    return add([own, got], [sds(own.shape[1:], f32 if k == 0 else bf16) for k in range(gy // 2)], name + "_sum_core")


def sum_plane(parts, gx, name):
    shape = parts[0].shape[1:]
    return add(parts, [sds(shape, f32 if k == 0 else bf16) for k in range(gx)], name + "_sum_plane")


def sum_line(parts, cuts, name):
    outs = [(sds((n, 128), f32), full((n, 128))) for _, n in cuts]
    return call(functools.partial(kernel_cut, cuts), name + "_sum_line", (), whole(*parts), outs, [], 24, 2)


def local(gx, gy, tokens, bucket, counts, mod_weights, mlp_weights, small_params, cotangent):
    ndev = gx * gy
    gxi, gyi = lax.axis_index("gx"), lax.axis_index("gy")
    device = gxi * gy + gyi
    pos = jnp.stack([gxi, gyi]).astype(jnp.int32)
    mod_len, small_len, mlp_len = mod_weights.shape[0], small_params.shape[0], mlp_weights.shape[0]
    mr, sr = block_rows(mod_len), block_rows(small_len)

    blocks = [place(mod_weights, device), place(small_params, device)]
    pad = -(mr + sr) % 16
    if pad:
        blocks.append(jnp.zeros((pad, 128), bf16))
    line = around(jnp.concatenate(blocks, 0), gy, gx, ndev)
    native, back = (1, 2, 0, 3), (2, 0, 1, 3)
    shape = (GH, GW) + tokens.shape[:1] + (C,)
    prepared = prep(jnp.transpose(tokens, native))
    line, mlp_mine, prepared = after((line, place(mlp_weights, device), prepared))
    xrow, nb, stat = prepared
    plane = around(jnp.stack(line), 2, gy // 2, ndev)
    mlp_line = jnp.stack(around(mlp_mine, gy, gx, ndev))
    up = upstream(counts, jnp.transpose(cotangent, native))
    plane, mlp_line, up = after((plane, mlp_line, up))
    mlp_other = swap(mlp_line, 1, ndev)
    plane = jnp.stack(plane)
    other = swap(plane, 1, ndev)
    mlp_both = jnp.stack([mlp_line, mlp_other])
    other, mlp_both = after((other, mlp_both))
    mlp_blocks = around(mlp_both, 2, gy // 2, ndev)

    q, gates, mixed, z, g, spec, mean, wf, wh, wp, vec, bm1, kcat = forward(
        gx, gy, pos, xrow, stat, bucket, plane, other, mod_len, small_len
    )
    mlp_blocks, mixed = after((mlp_blocks, mixed))
    dmid, out_rows, dq, dmix, own, oth, gwh, gwp, sums, bsum = middle(
        gx, gy, pos, xrow, up, mixed, q, wh, wp, vec, bm1, mlp_blocks, mlp_len
    )
    parts = sum_core_parts(own, oth, gx, gy, "mlp")
    parts, dmix = after((parts, dmix))
    mlp_plane = travel(parts, 2, ndev)
    dmer, own, oth = backward(
        gx, gy, pos, bucket, nb, dq, dmix, gates, z, g, spec, mean, kcat, wf, vec, sums, bsum, gwh, gwp, mod_len, small_len
    )
    mlp_plane, own, oth = after((mlp_plane, own, oth))
    parts = sum_plane(mlp_plane, gx, "mlp")
    mod_parts = sum_core(own, oth, gx, gy, "mod")
    mlp_line = travel(parts, gy, ndev)
    mod_plane = travel(mod_parts, 2, ndev)
    gtok = tail(shape, dmer, wf, xrow, stat, dmid, vec)
    mod_plane, mlp_line, gtok, out_rows = after((mod_plane, mlp_line, gtok, out_rows))
    mod_line = travel(sum_plane(mod_plane, gx, "mod"), gy, ndev)
    grad_mlp = take(sum_line(mlp_line, [(0, mlp_line[0].shape[0])], "mlp")[0], mlp_len, device)
    out = out_tokens(shape, counts, out_rows)
    mod_line, out, grad_mlp = after((mod_line, out, grad_mlp))
    total_mod, total_small = sum_line(mod_line, [(0, mr), (mr, sr)], "mod")
    grad_mod = take(total_mod, mod_len, device)
    grad_small = take(total_small, small_len, device)
    return jnp.transpose(out, back), jnp.transpose(gtok, back), grad_mod, grad_mlp, grad_small


def solution(mesh):
    images = P(AXES, None, None, None)
    flat = P(AXES)
    return jax.shard_map(
        functools.partial(local, mesh.shape["gx"], mesh.shape["gy"]),
        mesh=mesh,
        in_specs=(images, flat, flat, flat, flat, flat, images),
        out_specs=(images, images, flat, flat, flat),
        check_vma=False,
    )
```
